32 devices in a mesh: dp: 8 (over z, x), mp: 4 (over y, core).
Axes of the slice: x: 2, y: 2, z: 4, core: 2. Of those that a mesh axis runs over, the one named last changes fastest.
Arguments:
- tokens: bfloat16 [49152, 1280], P(('dp', 'mp')), may hold values from -40 to 40, as said below
- lengths: int32 [768, 32], P('dp'), may hold values from 0 to 64, as said below
- cotangent: bfloat16 [49152, 1280], P(('dp', 'mp')), may hold values from -6 to 6
- query_weight: bfloat16 [1280, 1280], P(None, 'mp'), may hold values from -0.15625 to 0.15625
- key_weight: bfloat16 [1280, 1280], P(None, 'mp'), may hold values from -0.15625 to 0.15625
- value_weight: bfloat16 [1280, 1280], P(None, 'mp'), may hold values from -0.15625 to 0.15625
- out_weight: bfloat16 [1280, 1280], P('mp'), may hold values from -0.3125 to 0.3125
- up_weight: bfloat16 [1280, 5120], P(None, 'mp'), may hold values from -0.15625 to 0.15625
- hidden_bias: bfloat16 [5120], P('mp'), may hold values from -3 to 3
- down_weight: bfloat16 [5120, 1280], P('mp'), may hold values from -0.078125 to 0.078125
- output_bias: bfloat16 [1280], replicated, may hold values from -2 to 2
- first_gain: bfloat16 [1280], replicated, may hold values from 0.099609375 to 1.8984375
- second_gain: bfloat16 [1280], replicated, may hold values from 0.099609375 to 1.8984375
Outputs:
- layer_output: bfloat16 [49152, 1280], P(('dp', 'mp'))
- input_gradient: float32 [49152, 1280], P(('dp', 'mp'))
- query_gradient: float32 [1280, 1280], P(None, 'mp')
- key_gradient: float32 [1280, 1280], P(None, 'mp')
- value_gradient: float32 [1280, 1280], P(None, 'mp')
- out_gradient: float32 [1280, 1280], P('mp')
- up_gradient: float32 [1280, 5120], P(None, 'mp')
- hidden_bias_gradient: float32 [5120], P('mp')
- down_gradient: float32 [5120, 1280], P('mp')
- output_bias_gradient: float32 [1280], replicated
- first_gain_gradient: float32 [1280], replicated
- second_gain_gradient: float32 [1280], replicated
- rms_stats: float32 [3], replicated
The draws below stay inside these ranges and needn't reach their ends.
Inputs may be any that keep to these rules, and one draw needn't show every extreme that they name: Each row lists the lengths of the series packed into it in order, zeros only after the last; every row holds one series or more and at most 64 patches; some row holds a single series of 64. `tokens`: activations of order one.
All inputs are finite; a program needn't handle non-finite values.
Results may differ from the reference program's by a relative error of at most 0.018.
Values may be sent and summed in bfloat16 or wider, within the bound.
A program may use at most 384 MiB of HBM per device.

```python
import math
import jax
import jax.numpy as jnp
from jax import lax

D = 1280
H = 16
HD = 80
FF = 5120
L = 64
SLOTS = 32
ROWS = 768
TOKENS = 49152
N_MP = 4


def draw_tokens(key, part):
    key = jax.random.fold_in(key, 11)
    base_key, row_key, col_key = jax.random.split(key, 3)
    place = jnp.arange(TOKENS).astype(jnp.float32) / max(TOKENS - 1, 1)
    row_scale = jnp.exp(jnp.log(3.0) * place + jax.random.uniform(row_key, (TOKENS,), minval=-0.4, maxval=0.4))
    col_scale = jnp.exp(jax.random.uniform(col_key, (D,), minval=-0.7, maxval=0.7))
    base = jnp.clip(jax.random.normal(base_key, (TOKENS, D)), -4.0, 4.0)
    return (base * row_scale[:, None] * col_scale[None, :]).astype(jnp.bfloat16)


def draw_lengths(key, part):
    key = jax.random.fold_in(key, 23)
    piece_key, used_key, whole_key, forced_key = jax.random.split(key, 4)
    pieces = jax.random.randint(piece_key, (ROWS, SLOTS), 1, 4)
    used = jax.random.randint(used_key, (ROWS, 1), SLOTS // 2, SLOTS + 1)
    slot = jnp.arange(SLOTS)[None, :]
    pieces = jnp.where(slot < used, pieces, 0)
    ends = jnp.cumsum(pieces, axis=1)
    pieces = jnp.where(ends <= L, pieces, 0)
    forced = jax.random.randint(forced_key, (), 0, ROWS)
    whole = (jax.random.randint(whole_key, (ROWS, 1), 0, 16) == 0) | (jnp.arange(ROWS)[:, None] == forced)
    single = jnp.where(slot == 0, L, 0)
    return jnp.where(whole, single, pieces).astype(jnp.int32)


def block_levels(own_key, dims, cuts, low, high):
    loudness, own = 1.0, jax.random.fold_in(own_key, 6)
    for dim, blocks in cuts:
        heights = jnp.exp(jax.random.uniform(jax.random.fold_in(own, dim), (blocks,), jnp.float32, low / len(cuts), high / len(cuts)))
        loudness = loudness * jnp.repeat(heights, dims[dim] // blocks).reshape([-1 if axis == dim else 1 for axis in range(len(dims))])
    return loudness


def centred(key, extent, deviation, limit, cuts=(), kind=jnp.bfloat16):
    array = jax.random.normal(key, extent, jnp.float32) * deviation
    if len(cuts) > 0:
        array = block_levels(key, extent, cuts, -0.22, 0.18) * array
    return jnp.clip(array, min=-limit, max=limit).astype(kind)


def setup_inputs(seed: int = 0) -> dict:
    streams_of = jax.random.split(jax.random.key(seed), 14)
    tokens = draw_tokens(jax.random.fold_in(streams_of[13], 71), 0)
    lengths = draw_lengths(jax.random.fold_in(streams_of[13], 71), 0)
    cotangent = centred(streams_of[2], (TOKENS, D), 1.0, 6.0, ((0, 32),))
    query_weight = centred(streams_of[3], (D, H * HD), D ** -0.5, 0.15625, ((1, 4),))
    key_weight = centred(streams_of[4], (D, H * HD), D ** -0.5, 0.15625, ((1, 4),))
    value_weight = centred(streams_of[5], (D, H * HD), D ** -0.5, 0.15625, ((1, 4),))
    out_weight = centred(streams_of[6], (H * HD, D), (D // 4) ** -0.5, 0.3125, ((0, 4),))
    up_weight = centred(streams_of[7], (D, FF), D ** -0.5, 0.15625, ((1, 4),))
    hidden_bias = centred(streams_of[8], (FF,), 0.5, 3.0, ((0, 4),))
    down_weight = centred(streams_of[9], (FF, D), FF ** -0.5, 0.078125, ((0, 4),))
    output_bias = centred(streams_of[10], (D,), 0.3, 2.0)
    first_gain = jnp.clip(1.0 + 0.18 * jax.random.normal(streams_of[11], (D,), jnp.float32), 0.099609375, 1.8984375).astype(jnp.bfloat16)
    second_gain = jnp.clip(1.0 + 0.18 * jax.random.normal(streams_of[12], (D,), jnp.float32), 0.099609375, 1.8984375).astype(jnp.bfloat16)
    return dict(tokens=tokens, lengths=lengths, cotangent=cotangent, query_weight=query_weight, key_weight=key_weight, value_weight=value_weight, out_weight=out_weight, up_weight=up_weight, hidden_bias=hidden_bias, down_weight=down_weight, output_bias=output_bias, first_gain=first_gain, second_gain=second_gain)


EPSILON = 1e-06
MASKED_SCORE = -1e+30
HIGHEST = lax.Precision.HIGHEST

@jax.custom_vjp
def low(v):
    return lax.optimization_barrier(v.astype(jnp.bfloat16)).astype(jnp.float32)

@jax.custom_vjp
def low_back(v):
    return v

def low_keep(v):
    return (low(v), None)

def low_pass(kept, grad):
    return (grad,)

def back_keep(v):
    return (v, None)

def back_low(kept, grad):
    return (low(grad),)
low.defvjp(low_keep, low_pass)
low_back.defvjp(back_keep, back_low)

def matmul(left, right):
    return jnp.dot(left, right, precision=HIGHEST)

def segments(lengths):
    ends = jnp.cumsum(lengths, axis=1)
    places = lax.broadcasted_iota(jnp.int32, (lengths.shape[0], L, lengths.shape[1]), 1)
    return lax.optimization_barrier(jnp.sum((ends[:, None, :] <= places).astype(jnp.int32), axis=2))

def run_layer(inputs, query_weight, key_weight, value_weight, out_weight, up_weight, hidden_bias, down_weight, output_bias, first_gain, second_gain, lengths):
    rows_all = lengths.shape[0]
    group = math.gcd(rows_all, 64)
    blocks = rows_all // group
    block_tokens = group * L
    scale = 1.0 / math.sqrt(HD)
    input_blocks = inputs.reshape(blocks, block_tokens, D)
    length_blocks = lengths.reshape(blocks, group, lengths.shape[1])
    causal = lax.broadcasted_iota(jnp.int32, (L, L), 1) <= lax.broadcasted_iota(jnp.int32, (L, L), 0)
    out_groups = out_weight.reshape(N_MP, H * HD // N_MP, D)
    down_groups = down_weight.reshape(N_MP, FF // N_MP, D)

    def step(totals, pieces):
        block, block_lengths = pieces
        segment_ids = segments(block_lengths)
        valid = (segment_ids < SLOTS).reshape(-1).astype(jnp.float32)
        allowed = (segment_ids[:, :, None] == segment_ids[:, None, :]) & causal[None]
        first_scale = lax.rsqrt(lax.optimization_barrier(jnp.mean(block * block, axis=1, keepdims=True)) + EPSILON)
        first_normed = low(block * first_scale * first_gain)
        queries = low_back(low(matmul(first_normed, query_weight))).reshape(group, L, H, HD)
        keys = low_back(low(matmul(first_normed, key_weight))).reshape(group, L, H, HD)
        values = low_back(low(matmul(first_normed, value_weight))).reshape(group, L, H, HD)
        scores = low_back(jnp.einsum('rqhe,rkhe->rhqk', queries, keys, precision=HIGHEST) * scale)
        scores = jnp.where(allowed[:, None], scores, MASKED_SCORE)
        peak = lax.optimization_barrier(jnp.max(scores, axis=-1, keepdims=True))
        expo = jnp.exp(scores - peak)
        probs = expo / lax.optimization_barrier(jnp.sum(expo, axis=-1, keepdims=True))
        probs_low = low(probs)
        mixed = jnp.einsum('rhqk,rkhe->rqhe', probs_low, values, precision=HIGHEST)
        mixed = low_back(low(mixed.reshape(block_tokens, H * HD)))
        partial_attention = jnp.einsum('tgk,gkd->tgd', mixed.reshape(block_tokens, N_MP, H * HD // N_MP), out_groups, precision=HIGHEST)
        attention_out = low_back(lax.optimization_barrier(jnp.sum(low(partial_attention), axis=1)))
        hidden = block + attention_out
        second_scale = lax.rsqrt(lax.optimization_barrier(jnp.mean(hidden * hidden, axis=1, keepdims=True)) + EPSILON)
        second_normed = low(hidden * second_scale * second_gain)
        preact = low_back(matmul(second_normed, up_weight) + hidden_bias)
        active = low_back(low(preact * jax.nn.sigmoid(preact)))
        partial_feed = jnp.einsum('tgk,gkd->tgd', active.reshape(block_tokens, N_MP, FF // N_MP), down_groups, precision=HIGHEST)
        feed_out = low_back(lax.optimization_barrier(jnp.sum(low(partial_feed), axis=1)) + output_bias)
        result = hidden + feed_out
        mask_col = valid[:, None]
        sums = jnp.stack([jnp.sum(mask_col * attention_out * attention_out), jnp.sum(mask_col * feed_out * feed_out), jnp.sum(mask_col * result * result), jnp.sum(valid)])
        return (totals + sums, result)
    totals, results = lax.scan(jax.checkpoint(step), jnp.zeros((4,), jnp.float32), (input_blocks, length_blocks))
    return (results.reshape(rows_all * L, D), totals)

def reference(tokens, lengths, cotangent, query_weight, key_weight, value_weight, out_weight, up_weight, hidden_bias, down_weight, output_bias, first_gain, second_gain):
    primals = tuple((a.astype(jnp.float32) for a in (tokens, query_weight, key_weight, value_weight, out_weight, up_weight, hidden_bias, down_weight, output_bias, first_gain, second_gain)))

    def forward(*values):
        return run_layer(*values, lengths)
    (results, totals), pullback = jax.vjp(forward, *primals)
    grads = pullback((cotangent.astype(jnp.float32), jnp.zeros_like(totals)))
    rms_stats = jnp.sqrt(totals[:3] / (totals[3] * D))
    return (results.astype(jnp.bfloat16), grads[0], grads[1], grads[2], grads[3], grads[4], grads[5], grads[6], grads[7], grads[8], grads[9], grads[10], rms_stats)
```

```python
import functools
import math

import jax
import jax.numpy as jnp
from jax import lax
from jax.experimental import pallas as pl
from jax.experimental.pallas import tpu as pltpu
from jax.sharding import PartitionSpec as P

HD = 80
L = 64
SLOTS = 32
LANES = 128
EPSILON = 1e-06
MASKED = -1e30
F32 = jnp.float32
BF = jnp.bfloat16
NN = (((1,), (0,)), ((), ()))
NT = (((1,), (1,)), ((), ()))
TN = (((0,), (0,)), ((), ()))
VMEM_BYTES = 60 << 20


def dot(a, b, dims=NN):
    return lax.dot_general(a, b, dims, preferred_element_type=F32)


def pick(n, *sizes):
    return next((s for s in sizes if n % s == 0), n)


def feed_body(chunk, rows, n2, n2t, g, gt, wua, wub, wda, wdb, hba, hbb, feed, n2g, dua, dub, dda, ddb, ba, bb, acc_f, acc_n, act, pg, wu, wd):
    step = pl.program_id(0)
    T, D = n2.shape
    ft = wua.shape[1]

    @pl.when(step == 0)
    def _():
        acc_f[...] = jnp.zeros_like(acc_f)
        acc_n[...] = jnp.zeros_like(acc_n)

    wu[:, :ft], wu[:, ft:] = wua[...], wub[...]
    wd[:ft, :], wd[ft:, :] = wda[...], wdb[...]
    hb = jnp.concatenate([hba[...], hbb[...]], axis=1).astype(F32)
    ba[...] = jnp.zeros_like(ba)
    bb[...] = jnp.zeros_like(bb)

    def one(i, _):
        s = pl.ds(pl.multiple_of(i * chunk, chunk), chunk)
        p = dot(n2[s, :], wu[...]) + hb
        ag = dot(g[s, :], wd[...], NT)
        sg = 0.5 * jnp.tanh(0.5 * p) + 0.5
        ps = p * sg
        a = ps.astype(BF)
        q = (ag * (sg + ps * (1.0 - sg))).astype(BF)
        act[s, :] = a
        pg[s, :] = q
        b = jnp.sum(q.astype(F32), axis=0, keepdims=True)
        ba[...] += b[:, :ft]
        bb[...] += b[:, ft:]
        acc_f[s, :] += dot(a, wd[...])
        acc_n[s, :] += dot(q, wu[...], NT)
        return 0

    lax.fori_loop(0, T // chunk, one, 0)

    def two(i, _):
        s = pl.ds(pl.multiple_of(i * rows, rows), rows)
        u = dot(n2t[s, :], pg[...]).astype(BF)
        dua[s, :], dub[s, :] = u[:, :ft], u[:, ft:]
        d = dot(gt[s, :], act[...]).astype(BF)
        dda[s, :], ddb[s, :] = d[:, :ft], d[:, ft:]
        return 0

    lax.fori_loop(0, D // rows, two, 0)

    @pl.when(step == pl.num_programs(0) - 1)
    def _():
        feed[...] = acc_f[...].astype(BF)
        n2g[...] = acc_n[...].astype(BF)


def feed_forward(n2, n2t, g, gt, ups, downs, biases):
    T, D = n2.shape
    F = ups[0].shape[1]
    ft = pick(F, 256)
    chunk, rows = pick(T, 768, 384, 128), pick(D, 640, 256)
    one = lambda s: pl.BlockSpec(s, lambda f: (0, 0), pipeline_mode=pl.Buffered(1))
    up = pl.BlockSpec((D, ft), lambda f: (0, f))
    down = pl.BlockSpec((ft, D), lambda f: (f, 0))
    bias = pl.BlockSpec((1, ft), lambda f: (0, f))
    return pl.pallas_call(
        functools.partial(feed_body, chunk, rows),
        grid=(F // ft,),
        in_specs=[one((T, D)), one((D, T)), one((T, D)), one((D, T)), up, up, down, down, bias, bias],
        out_specs=[one((T, D)), one((T, D)), up, up, up, up, bias, bias],
        out_shape=[jax.ShapeDtypeStruct((T, D), BF)] * 2
        + [jax.ShapeDtypeStruct((D, F), BF)] * 4
        + [jax.ShapeDtypeStruct((1, F), F32)] * 2,
        scratch_shapes=[
            pltpu.VMEM((T, D), F32),
            pltpu.VMEM((T, D), F32),
            pltpu.VMEM((T, 2 * ft), BF),
            pltpu.VMEM((T, 2 * ft), BF),
            pltpu.VMEM((D, 2 * ft), BF),
            pltpu.VMEM((2 * ft, D), BF),
        ],
        compiler_params=pltpu.CompilerParams(vmem_limit_bytes=VMEM_BYTES),
        cost_estimate=pl.CostEstimate(
            flops=24 * T * D * F, bytes_accessed=24 * T * D + 16 * D * F, transcendentals=2 * T * F
        ),
        name="feed_forward",
    )(n2, n2t, g, gt, *ups, *downs, *biases)


def windows(C):
    out=[]
    for h in range(C//HD):
        w=min(LANES*(HD*h//LANES),C-2*LANES)
        out.append((w,HD*h-w))
    return out
def head_masks(C):
    lane=lax.broadcasted_iota(jnp.int32,(1,2*LANES),1)
    return [jnp.where((lane>=lo)&(lane<lo+HD),1.0,0.0).astype(BF) for _,lo in windows(C)]
def softmaxes(qs,ks,allowed):
    s=[jnp.where(allowed,dot(q,k,NT)*(1.0/math.sqrt(HD)),MASKED) for q,k in zip(qs,ks)]
    e=[jnp.exp(x-jnp.max(x,axis=1,keepdims=True)) for x in s]
    return [x*(1.0/jnp.sum(x,axis=1,keepdims=True)) for x in e]
def allow(idc,idr,s,B):
    causal=lax.broadcasted_iota(jnp.int32,(B,B),1)<=lax.broadcasted_iota(jnp.int32,(B,B),0)
    return (idc[s,:]==idr[:,s])&causal
def put(tiles,w,val):
    for n in range(2):
        t=w//LANES+n; part=val[:,n*LANES:(n+1)*LANES]
        tiles[t]=part if tiles[t] is None else tiles[t]+part
def fwd_body(B,C,per,n1,w,idc,idr,qkv,mixed,mixedt):
    T=n1.shape[0]
    qkv[...]=dot(n1[...],w[...]).astype(BF)
    masks=head_masks(C); wins=[w for w,_ in windows(C)]
    def block(i,_):
        s=pl.ds(pl.multiple_of(i*B,B),B)
        ok=allow(idc,idr,s,B)
        tiles=[None]*(C//LANES)
        cut=lambda n,w: qkv[s,n*C+w:n*C+w+2*LANES]
        for g in range(0,len(wins),per):
            hs=range(g,min(g+per,len(wins)))
            p=softmaxes([cut(0,wins[h])*masks[h] for h in hs],[cut(1,wins[h]) for h in hs],ok)
            o=[dot(x.astype(BF),cut(2,wins[h])*masks[h]) for x,h in zip(p,hs)]
            for h,x in zip(hs,o): put(tiles,wins[h],x)
        mx=jnp.concatenate(tiles,axis=1)
        mixed[s,:]=mx.astype(BF); mixedt[:,s]=mx.T.astype(BF)
        return 0
    lax.fori_loop(0,T//B,block,0)
def att_fwd(n1,w,idc,idr,tt=512,B=128,per=8):
    T,D=n1.shape; C=w.shape[1]//3
    tt=pick(T,tt,384,256,128)
    return pl.pallas_call(functools.partial(fwd_body,B,C,per),grid=(T//tt,),
        in_specs=[pl.BlockSpec((tt,D),lambda i:(i,0)),pl.BlockSpec((D,3*C),lambda i:(0,0),pipeline_mode=pl.Buffered(1)),pl.BlockSpec((tt,1),lambda i:(i,0)),pl.BlockSpec((1,tt),lambda i:(0,i))],
        out_specs=[pl.BlockSpec((tt,3*C),lambda i:(i,0)),pl.BlockSpec((tt,C),lambda i:(i,0)),pl.BlockSpec((C,tt),lambda i:(0,i))],
        out_shape=[jax.ShapeDtypeStruct((T,3*C),BF),jax.ShapeDtypeStruct((T,C),BF),jax.ShapeDtypeStruct((C,T),BF)],
        compiler_params=pltpu.CompilerParams(vmem_limit_bytes=VMEM_BYTES),
        cost_estimate=pl.CostEstimate(flops=int(1.5*2*T*D*3*C),bytes_accessed=2*(T*D+4*C*D+5*T*C),transcendentals=T*B*C//HD),
        name="attend")(n1,w,idc,idr)
def bwd_body(B,C,per,rows,n1t,w,wo,hg,qkv,mixedt,idc,idr,n1g,dw,dwo,dqkv,dmix):
    step=pl.program_id(0); last=pl.num_programs(0)-1
    tt=qkv.shape[0]; D=hg.shape[1]; scale=1.0/math.sqrt(HD)
    base=pl.multiple_of(step*tt,tt)
    dmix[...]=dot(hg[pl.ds(base,tt),:],wo[...],NT).astype(BF)
    masks=head_masks(C); wins=[w for w,_ in windows(C)]
    def block(i,_):
        s=pl.ds(pl.multiple_of(i*B,B),B)
        ok=allow(idc,idr,s,B)
        dq=[None]*(C//LANES); dk=list(dq); dv=list(dq)
        cut=lambda n,w: qkv[s,n*C+w:n*C+w+2*LANES]
        for g in range(0,len(wins),per):
            hs=range(g,min(g+per,len(wins)))
            q=[cut(0,wins[h])*masks[h] for h in hs]
            gm=[dmix[s,wins[h]:wins[h]+2*LANES]*masks[h] for h in hs]
            p=softmaxes(q,[cut(1,wins[h]) for h in hs],ok)
            dp=[dot(x,cut(2,wins[h]),NT) for x,h in zip(gm,hs)]
            ds=[(a*(b-jnp.sum(a*b,axis=1,keepdims=True))).astype(BF) for a,b in zip(p,dp)]
            for h,a,b,c,d in zip(hs,p,gm,ds,q):
                put(dv,wins[h],dot(a.astype(BF),b,TN))
                put(dk,wins[h],dot(c,d,TN))
                put(dq,wins[h],dot(c,cut(1,wins[h])*masks[h]))
        o=pl.ds(pl.multiple_of(base+i*B,B),B)
        for n,(tiles,c) in enumerate(((dq,scale),(dk,scale),(dv,None))):
            a=jnp.concatenate(tiles,axis=1)
            dqkv[o,n*C:(n+1)*C]=(a if c is None else a*c).astype(BF)
        return 0
    lax.fori_loop(0,tt//B,block,0)
    n1g[...]=dot(dqkv[pl.ds(base,tt),:],w[...],NT).astype(n1g.dtype)
    @pl.when(step==last)
    def _():
        def two(i,_):
            s=pl.ds(pl.multiple_of(i*rows,rows),rows)
            dw[s,:]=dot(n1t[s,:],dqkv[...]).astype(dw.dtype)
            return 0
        lax.fori_loop(0,D//rows,two,0)
        dwo[...]=dot(mixedt[...],hg[...]).astype(dwo.dtype)
def att_bwd(n1t,w,wo,hg,qkv,mixedt,idc,idr,tt=512,B=128,rows=256,per=8):
    D,T=n1t.shape; C=w.shape[1]//3
    tt=pick(T,tt,384,256,128)
    one=lambda s: pl.BlockSpec(s,lambda i:(0,0),pipeline_mode=pl.Buffered(1))
    return pl.pallas_call(functools.partial(bwd_body,B,C,per,rows),grid=(T//tt,),
        in_specs=[one((D,T)),one((D,3*C)),one((C,D)),one((T,D)),pl.BlockSpec((tt,3*C),lambda i:(i,0)),one((C,T)),pl.BlockSpec((tt,1),lambda i:(i,0)),pl.BlockSpec((1,tt),lambda i:(0,i))],
        out_specs=[pl.BlockSpec((tt,D),lambda i:(i,0)),one((D,3*C)),one((C,D))],
        out_shape=[jax.ShapeDtypeStruct((T,D),BF),jax.ShapeDtypeStruct((D,3*C),BF),jax.ShapeDtypeStruct((C,D),BF)],
        scratch_shapes=[pltpu.VMEM((T,3*C),BF),pltpu.VMEM((tt,C),BF)],
        compiler_params=pltpu.CompilerParams(vmem_limit_bytes=VMEM_BYTES),
        cost_estimate=pl.CostEstimate(flops=int(1.5*2*T*D*8*C),bytes_accessed=2*(3*T*D+8*C*D+5*T*C),transcendentals=T*B*C//HD),
        name="attend_back")(n1t,w,wo,hg,qkv,mixedt,idc,idr)


def pairs(n, bit):
    return [(i, i ^ bit) for i in range(n)]


def swap(a, axis, bit):
    return lax.ppermute(a, axis, pairs(lax.axis_size(axis), bit))


def add(*arrays):
    return sum(a.astype(F32) for a in arrays).astype(BF)


def halve(a, axis, bit):
    n = a.shape[0] // 2
    here = (lax.axis_index(axis) // bit) % 2
    sent = lax.dynamic_slice_in_dim(a, (1 - here) * n, n)
    kept = lax.dynamic_slice_in_dim(a, here * n, n)
    return add(kept, swap(sent, axis, bit))


def double(a, axis, bit):
    here = (lax.axis_index(axis) // bit) % 2
    other = swap(a, axis, bit)
    return jnp.where(here == 0, jnp.concatenate([a, other]), jnp.concatenate([other, a]))


def dp_bits(first):
    bits = [1 << n for n in range(lax.axis_size("dp").bit_length() - 1)]
    return bits[first:] [:1] + [b for b in bits if b != bits[first]] if len(bits) > first else bits


def dp_sum(a, first=0):
    bits = dp_bits(first)
    for bit in bits:
        a = halve(a, "dp", bit)
    for bit in reversed(bits):
        a = double(a, "dp", bit)
    return a


def all_sum(a):
    for axis in ("mp", "dp"):
        bit = 1
        while bit < lax.axis_size(axis):
            a = a + swap(a, axis, bit)
            bit *= 2
    return a


def normalize(values, gain):
    scale_rows = lax.rsqrt(jnp.mean(values * values, axis=1, keepdims=True) + EPSILON)
    return scale_rows, (values * scale_rows * gain.astype(F32)).astype(BF)


def norm_back(values, scale_rows, gain, grad):
    weighted = gain.astype(F32) * grad
    inner = jnp.sum(weighted * values, axis=1, keepdims=True)
    gain_part = jnp.sum(grad * values * scale_rows, axis=0)
    back = weighted * scale_rows - values * (
        scale_rows * scale_rows * scale_rows * inner / values.shape[1]
    )
    return gain_part, back


def segments(lengths):
    slots = lengths.shape[1]
    upto = lax.broadcasted_iota(jnp.int32, (1, slots, slots), 2) <= lax.broadcasted_iota(
        jnp.int32, (1, slots, slots), 1
    )
    ends = jnp.sum(jnp.where(upto, lengths[:, None, :], 0), axis=2)
    places = lax.broadcasted_iota(jnp.int32, (lengths.shape[0], L, slots), 1)
    return jnp.sum((ends[:, None, :] <= places).astype(jnp.int32), axis=2)


def gather_groups(weights):
    if lax.axis_size("mp") == 4:
        other = [swap(w, "mp", 2) for w in weights]
        return [
            (weights, [swap(w, "mp", 1) for w in weights]),
            (other, [swap(w, "mp", 1) for w in other]),
        ]
    dims = (1, 1, 1, 0, 1, 0, 1)
    whole = [lax.all_gather(w, "mp", axis=d, tiled=True) for w, d in zip(weights, dims)]
    return [tuple(zip(*(jnp.split(w, 2, axis=d) for w, d in zip(whole, dims))))]


def scatter_groups(groups, dims):
    if len(groups) == 2:
        own, other = ([add(a, swap(b, "mp", 1)) for a, b in zip(*g)] for g in groups)
        return [add(a, swap(b, "mp", 2)) for a, b in zip(own, other)]
    return [
        lax.psum_scatter(jnp.concatenate(pair, axis=d), "mp", scatter_dimension=d, tiled=True)
        for pair, d in zip(zip(*groups[0]), dims)
    ]


def per_device(
    tokens,
    lengths,
    cotangent,
    query_weight,
    key_weight,
    value_weight,
    out_weight,
    up_weight,
    hidden_bias,
    down_weight,
    output_bias,
    first_gain,
    second_gain,
):
    T, D = tokens.shape
    width = query_weight.shape[1]
    rows = T // L
    n_mp = lax.axis_size("mp")
    mp = lax.axis_index("mp")
    segment_ids = segments(lax.dynamic_slice_in_dim(lengths, mp * rows, rows))
    valid = (segment_ids < SLOTS).reshape(-1, 1).astype(F32)
    ids = (segment_ids + L * lax.broadcasted_iota(jnp.int32, (rows, L), 0)).reshape(-1)
    id_col, id_row = ids[:, None], ids[None, :]

    bias_row = hidden_bias.reshape(1, -1)
    groups = gather_groups(
        [query_weight, key_weight, value_weight, out_weight, up_weight, down_weight, bias_row]
    )
    inputs = tokens.astype(F32)
    r1, n1 = normalize(inputs, first_gain)
    n1t = n1.T
    attention = 0.0
    kept = []
    for a, b in groups:
        w = jnp.concatenate([a[0], b[0], a[1], b[1], a[2], b[2]], axis=1)
        wo = jnp.concatenate([a[3], b[3]], axis=0)
        qkv, mixed, mixedt = att_fwd(n1, w, id_col, id_row)
        attention = attention + dot(mixed, wo)
        kept.append((w, wo, qkv, mixedt))
    hidden = inputs + attention
    r2, n2 = normalize(hidden, second_gain)
    n2t, gt = n2.T, cotangent.T
    feed = output_bias.astype(F32)
    n2_grad = 0.0
    feed_grads = []
    bias_parts = []
    for a, b in groups:
        f, n, dua, dub, dda, ddb, ba, bb = feed_forward(
            n2, n2t, cotangent, gt, (a[4], b[4]), (a[5], b[5]), (a[6], b[6])
        )
        feed = feed + f.astype(F32)
        n2_grad = n2_grad + n.astype(F32)
        feed_grads.append(((dua, dda), (dub, ddb)))
        bias_parts.append((ba, bb))
    up_part, down_part = scatter_groups(feed_grads, (1, 1))
    up_total = dp_sum(up_part, 0).astype(F32)
    down_total = dp_sum(down_part, 1).T.astype(F32)
    result = hidden + feed
    grad_out = cotangent.astype(F32)
    second_part, second_back = norm_back(hidden, r2, second_gain, n2_grad)
    hidden_grad = grad_out + second_back
    low_grad = hidden_grad.astype(BF)
    sums = jnp.stack(
        [
            jnp.sum(valid * attention * attention),
            jnp.sum(valid * feed * feed),
            jnp.sum(valid * result * result),
            jnp.sum(valid),
        ]
    )
    if len(groups) == 2:
        hidden_units = bias_row.shape[1]
        bias = jnp.zeros((1, n_mp * hidden_units), F32)
        for flip, part in ((0, bias_parts[0][0]), (1, bias_parts[0][1]), (2, bias_parts[1][0]), (3, bias_parts[1][1])):
            bias = lax.dynamic_update_slice(bias, part, (0, (mp ^ flip) * hidden_units))
    else:
        bias = jnp.concatenate(bias_parts[0], axis=1)
    small = all_sum(
        jnp.concatenate([bias[0], second_part, jnp.sum(grad_out, axis=0), sums])
    )
    n_bias = bias.shape[1]
    bias_total = lax.dynamic_slice_in_dim(small, mp * bias_row.shape[1], bias_row.shape[1])
    second_total = small[n_bias : n_bias + D]
    output_bias_total = small[n_bias + D : n_bias + 2 * D]
    sums = small[n_bias + 2 * D :]
    rms_stats = jnp.sqrt(sums[:3] / (sums[3] * D))

    n1_grad = 0.0
    att_grads = []
    for w, wo, qkv, mixedt in kept:
        n, dw, dwo = att_bwd(n1t, w, wo, low_grad, qkv, mixedt, id_col, id_row)
        n1_grad = n1_grad + n.astype(F32)
        C = wo.shape[0]
        h = C // 2
        att_grads.append(
            tuple(
                (
                    jnp.concatenate([dw[:, i * C + k * h : i * C + (k + 1) * h] for i in range(3)], axis=1),
                    dwo[k * h : (k + 1) * h],
                )
                for k in range(2)
            )
        )
    if len(groups) == 2:
        joined_part, out_part = scatter_groups(att_grads, None)
        parts = [joined_part]
    else:
        (ja, oa), (jb, ob) = att_grads[0]
        h = ja.shape[1] // 3
        both = [
            jnp.concatenate([ja[:, i * h : (i + 1) * h], jb[:, i * h : (i + 1) * h]], axis=1)
            for i in range(3)
        ]
        parts = [lax.psum_scatter(x, "mp", scatter_dimension=1, tiled=True) for x in both]
        out_part = lax.psum_scatter(
            jnp.concatenate([oa, ob]), "mp", scatter_dimension=0, tiled=True
        )
    joined = dp_sum(jnp.concatenate(parts, axis=1), 0).astype(F32)
    out_total = dp_sum(out_part, 1).astype(F32)
    first_part, first_back = norm_back(inputs, r1, first_gain, n1_grad)
    input_gradient = hidden_grad + first_back
    first_total = all_sum(first_part)
    return (
        result.astype(BF),
        input_gradient,
        joined[:, :width],
        joined[:, width : 2 * width],
        joined[:, 2 * width :],
        out_total,
        up_total,
        bias_total.reshape(-1),
        down_total,
        output_bias_total,
        first_total,
        second_total,
        rms_stats,
    )


def solution(mesh):
    return jax.shard_map(
        per_device,
        mesh=mesh,
        in_specs=(
            P(("dp", "mp"), None),
            P("dp", None),
            P(("dp", "mp"), None),
            P(None, "mp"),
            P(None, "mp"),
            P(None, "mp"),
            P("mp", None),
            P(None, "mp"),
            P("mp"),
            P("mp", None),
            P(),
            P(),
            P(),
        ),
        out_specs=(
            P(("dp", "mp"), None),
            P(("dp", "mp"), None),
            P(None, "mp"),
            P(None, "mp"),
            P(None, "mp"),
            P("mp", None),
            P(None, "mp"),
            P("mp"),
            P("mp", None),
            P(),
            P(),
            P(),
            P(),
        ),
        check_vma=False,
    )
```

```python
import functools
import math

import jax
import jax.numpy as jnp
from jax import lax
from jax.experimental import pallas as pl
from jax.experimental.pallas import tpu as pltpu
from jax.sharding import PartitionSpec as P

HD = 80
L = 64
SLOTS = 32
LANES = 128
EPSILON = 1e-06
MASKED = -1e30
F32 = jnp.float32
BF = jnp.bfloat16
NN = (((1,), (0,)), ((), ()))
NT = (((1,), (1,)), ((), ()))
TN = (((0,), (0,)), ((), ()))
VMEM_BYTES = 60 << 20


def dot(a, b, dims=NN):
    return lax.dot_general(a, b, dims, preferred_element_type=F32)


def pick(n, *sizes):
    return next((s for s in sizes if n % s == 0), n)


def whole(shape):
    return pl.BlockSpec(shape, lambda *i: (0,) * len(shape), pipeline_mode=pl.Buffered(1))


def cost(flops, nbytes, exps=0):
    return pl.CostEstimate(flops=int(flops), bytes_accessed=int(nbytes), transcendentals=int(exps))


def row_sum(x):
    return jnp.sum(x, axis=0, keepdims=True)


def rms(x):
    return lax.rsqrt(jnp.mean(x * x, axis=1, keepdims=True) + EPSILON)


MESH = pl.DeviceIdType.MESH
CORE, Y = ("mp", 1), ("mp", 2)


def bit_of(axis, bit):
    return lax.rem(lax.axis_index(axis) // bit, 2)


def flip(axis, bit):
    return {axis: lax.axis_index(axis) + bit - 2 * bit * bit_of(axis, bit)}


class Traffic:
    def __init__(self, number, partners, arrays, buffers):
        self.number, self.partners = number, partners
        self.arrays, self.buffers = arrays, buffers
        self.events, self.slots, self.refs = [], {}, {}

    def on(self, step, place, *actions):
        self.events += [(step, place, f) for f in actions]
        return self

    def run(self, step, place):
        for at, where, action in self.events:
            if where == place:
                pl.when(step == at)(functools.partial(action, self))

    def greet(self):
        sem = pltpu.get_barrier_semaphore()
        for p in self.partners:
            pl.semaphore_signal(sem, inc=1, device_id=flip(*p), device_id_type=MESH)
        pl.semaphore_wait(sem, len(self.partners))

    def copy(self, name, src, dst, to):
        i = self.slots.setdefault(name, len(self.slots))
        return pltpu.make_async_remote_copy(
            src_ref=src,
            dst_ref=dst,
            send_sem=self.sems.at[0, i],
            recv_sem=self.sems.at[1, i],
            device_id=flip(*to),
            device_id_type=MESH,
        )

    def local(self, name, src, dst):
        i = self.slots.setdefault(name, len(self.slots))
        return pltpu.make_async_copy(src, dst, self.sems.at[0, i])


COPIES = 40


def launch(body, name, grid, args, in_specs, outs, out_specs, scratch, cost_estimate, traffic=None):
    n_args, n_outs = len(args), len(outs)
    names, arrays, buffers = [], [], []
    if traffic is not None:
        names = [*traffic.arrays, *traffic.buffers]
        arrays = list(traffic.arrays.values())
        buffers = [jax.ShapeDtypeStruct(s, BF) for s in traffic.buffers.values()]
        scratch = [*scratch, pltpu.SemaphoreType.DMA((2, COPIES))]

    def kernel(*refs):
        hook = lambda place: None
        inputs, refs = refs[:n_args], refs[n_args:]
        moved, refs = refs[: len(arrays)], refs[len(arrays) :]
        results, refs = refs[:n_outs], refs[n_outs:]
        landing, refs = refs[: len(buffers)], refs[len(buffers) :]
        if traffic is not None:
            step = pl.program_id(0)
            for d in range(1, len(grid)):
                step = step * grid[d] + pl.program_id(d)
            traffic.refs = dict(zip(names, [*moved, *landing]))
            traffic.sems, refs = refs[-1], refs[:-1]
            if traffic.partners:
                pl.when(step == 0)(traffic.greet)
            hook = lambda place: traffic.run(step, place)
        body(hook, *inputs, *results, *refs)

    anywhere = pl.BlockSpec(memory_space=pl.ANY)
    out = pl.pallas_call(
        kernel,
        grid=grid,
        in_specs=[*in_specs, *[anywhere] * len(arrays)],
        out_specs=[*out_specs, *[anywhere] * len(buffers)],
        out_shape=[*outs, *buffers],
        scratch_shapes=scratch,
        compiler_params=pltpu.CompilerParams(
            vmem_limit_bytes=VMEM_BYTES,
            **({} if traffic is None or not traffic.partners else dict(collective_id=traffic.number, has_side_effects=True)),
        ),
        cost_estimate=cost_estimate,
        name=name,
    )(*args, *arrays)
    return out[:n_outs], dict(zip(names[len(arrays) :], out[n_outs:]))


def add_rows(sources, target, rows):
    columns = target.shape[1]
    tile = pl.BlockSpec((pick(rows, 80, 64, 16), columns), lambda i: (i, 0))

    def body(*refs):
        refs[-1][...] = sum(r[...].astype(F32) for r in refs[:-1]).astype(BF)

    pltpu.emit_pipeline(
        body, grid=(rows // tile.block_shape[0],), in_specs=[tile] * len(sources), out_specs=[tile]
    )(*[r.at[pl.ds(pl.multiple_of(o, 16), rows), :] for r, o in sources], target)


class Stream:
    def __init__(self, tag, mine, theirs, rows, columns, order, base=0):
        self.tag, self.mine, self.theirs, self.base = tag, mine, theirs, base
        self.rows, self.columns, self.order = rows, columns, order

    def name(self, what):
        return self.tag + what

    def buffers(self, *what):
        size = lambda w: self.rows if w[0] in "cf" else self.rows >> len(self.order) if w[0] in "ey" else self.rows >> (int(w[1]) + 1)
        return {self.name(w): (size(w), self.columns) for w in what}

    def place(self, stages):
        first, n = 0, self.rows
        for bit in self.order[:stages]:
            n //= 2
            first = first + bit_of("dp", bit) * n
        return first, n

    def sources(self, t, first, arrived):
        out = [(t.refs[self.mine], first + self.base), (t.refs[self.name("c")], first)]
        for j in range(arrived):
            out.append((t.refs[self.name(f"r{j}")], first - self.place(j + 1)[0]))
        return out

    def core(self, t):
        src = t.refs[self.theirs].at[pl.ds(self.base, self.rows), :]
        return t.copy(self.name("c"), src, t.refs[self.name("c")], CORE)

    def start_core(self, t):
        self.core(t).start()

    def wait_core(self, t):
        self.core(t).wait()

    def exchange(self, t, j):
        return t.copy(self.name(f"r{j}"), t.refs[self.name(f"s{j}")], t.refs[self.name(f"r{j}")], ("dp", self.order[j]))

    def start(self, j):
        def action(t):
            first, n = self.place(j)
            n //= 2
            sent = first + (1 - bit_of("dp", self.order[j])) * n
            add_rows(self.sources(t, sent, j), t.refs[self.name(f"s{j}")], n)
            self.exchange(t, j).start()

        return action

    def wait(self, j):
        return lambda t: self.exchange(t, j).wait()

    def keep(self, t):
        first, n = self.place(len(self.order))
        add_rows(self.sources(t, first, len(self.order)), t.refs[self.name("e")], n)

    def cross(self, t):
        return t.copy(self.name("y"), t.refs[self.name("e")], t.refs[self.name("y")], Y)

    def start_cross(self, t):
        self.cross(t).start()

    def wait_cross(self, t):
        self.cross(t).wait()

    def total(self, other):
        def action(t):
            first, n = self.place(len(self.order))
            target = t.refs[self.name("f")].at[pl.ds(pl.multiple_of(first, 16), n), :]
            add_rows([(t.refs[self.name("e")], 0), (t.refs[other.name("y")], 0)], target, n)

        return action

    def spread(self, t, j):
        first, n = self.place(j + 1)
        part = t.refs[self.name("f")].at[pl.ds(pl.multiple_of(first, 16), n), :]
        return t.copy(self.name(f"f{j}"), part, part, ("dp", self.order[j]))

    def start_spread(self, j):
        return lambda t: self.spread(t, j).start()

    def wait_spread(self, j):
        return lambda t: self.spread(t, j).wait()


class Gather:
    def __init__(self, tag, rows, columns):
        self.tag, self.rows, self.columns = tag, rows, columns
        self.n = rows // 4

    def buffers(self, *what):
        return {self.tag + w: (self.n if w == "q" else self.rows, self.columns) for w in what}

    def quarter(self, ref, flip_x=0, flip_z=0, first=0, rows=None):
        x, z = bit_of("dp", 1), bit_of("dp", 2)
        x, z = (1 - x if flip_x else x), (1 - z if flip_z else z)
        start = pl.multiple_of((2 * z + x) * self.n + first, 16)
        return ref.at[pl.ds(start, self.n if rows is None else rows), :]

    def copies(self, t, step):
        own, o = t.refs[self.tag], t.refs.get(self.tag + "o")
        name = self.tag + step
        if step == "s":
            return [t.copy(name, own, t.refs[name], CORE)]
        if step == "y":
            return [t.copy(name, self.quarter(own), t.refs[self.tag + "q"], Y)]
        if step == "a":
            q = t.refs[self.tag + "q"]
            return [t.copy(name + str(b), q, self.quarter(o), ("dp", b)) for b in (1, 2)] + [
                t.local(name + "l", q, self.quarter(o))
            ]
        if step == "b":
            top = (self.n // 2 + 15) // 16 * 16
            to_x = self.quarter(o, flip_z=1, rows=top)
            to_z = self.quarter(o, flip_x=1, first=top, rows=self.n - top)
            return [t.copy(name + "1", to_x, to_x, ("dp", 1)), t.copy(name + "2", to_z, to_z, ("dp", 2))]
        return [t.copy(name, o, t.refs[self.tag + "p"], CORE)]

    def start(self, step):
        def action(t):
            for c in self.copies(t, step):
                c.start()

        return action

    def wait(self, step):
        def action(t):
            for c in self.copies(t, step):
                c.wait()

        return action


def windows(C):
    out = []
    for h in range(C // HD):
        w = min(LANES * (HD * h // LANES), C - 2 * LANES)
        out.append((w, HD * h - w))
    return out


def head_masks(C):
    lane = lax.broadcasted_iota(jnp.int32, (1, 2 * LANES), 1)
    return [jnp.where((lane >= lo) & (lane < lo + HD), 1.0, 0.0).astype(BF) for _, lo in windows(C)]


def softmaxes(qs, ks, allowed):
    s = [jnp.where(allowed, dot(q, k, NT) * (1.0 / math.sqrt(HD)), MASKED) for q, k in zip(qs, ks)]
    e = [jnp.exp(x - jnp.max(x, axis=1, keepdims=True)) for x in s]
    return [x * (1.0 / jnp.sum(x, axis=1, keepdims=True)) for x in e]


def allow(idc, idr, s, B):
    causal = lax.broadcasted_iota(jnp.int32, (B, B), 1) <= lax.broadcasted_iota(
        jnp.int32, (B, B), 0
    )
    return (idc[s, :] == idr[:, s]) & causal


def put(tiles, w, val):
    for n in range(2):
        t = w // LANES + n
        part = val[:, n * LANES : (n + 1) * LANES]
        tiles[t] = part if tiles[t] is None else tiles[t] + part


def fwd_body(B, C, pairs, traffic, hook, x, gain, idc, idr, qkv, mixed, w, n1, ab, sem):
    group = pl.program_id(0)
    tt = x.shape[0]
    first = pl.program_id(1) == 0
    hook("start")
    h = C // 2
    for g, pair in enumerate(pairs):

        @pl.when(first & (group == g))
        def _():
            for side in range(2):
                c = pltpu.make_async_copy(traffic.refs[pair[side]], ab, sem)
                c.start()
                c.wait()
                a = ab[...]
                for i in range(3):
                    w[0, :, i * C + side * h : i * C + (side + 1) * h] = a[:, i * h : (i + 1) * h]

    t = x[...].astype(F32)
    normed = (t * rms(t) * gain[...].astype(F32)).astype(BF)

    @pl.when(group == 0)
    def _():
        n1[...] = normed

    qkv[0] = dot(normed, w[0]).astype(BF)
    hook("middle")
    masks = head_masks(C)
    wins = [w0 for w0, _ in windows(C)]

    def block(i, _):
        s = pl.ds(pl.multiple_of(i * B, B), B)
        ok = allow(idc, idr, s, B)
        tiles = [None] * (C // LANES)
        cut = lambda n, w0: qkv[0, s, n * C + w0 : n * C + w0 + 2 * LANES]
        for g in range(0, len(wins), 8):
            hs = range(g, min(g + 8, len(wins)))
            p = softmaxes([cut(0, wins[h]) * masks[h] for h in hs], [cut(1, wins[h]) for h in hs], ok)
            o = [dot(a.astype(BF), cut(2, wins[h]) * masks[h]) for a, h in zip(p, hs)]
            for h, a in zip(hs, o):
                put(tiles, wins[h], a)
        mixed[0, s, :] = jnp.concatenate(tiles, axis=1).astype(BF)
        return 0

    lax.fori_loop(0, tt // B, block, 0)
    hook("end")


def attend(x, gain, idc, idr, h, pairs, traffic):
    T, D = x.shape
    C, G = 2 * h, len(pairs)
    tt, B = pick(T, 512, 384, 256, 128), 128
    by_group = lambda c: pl.BlockSpec((1, tt, c), lambda g, i: (g, i, 0))
    return launch(
        functools.partial(fwd_body, B, C, pairs, traffic),
        "attend",
        (G, T // tt),
        (x, gain, idc, idr),
        [
            pl.BlockSpec((tt, D), lambda g, i: (i, 0)),
            whole((1, D)),
            pl.BlockSpec((tt, 1), lambda g, i: (i, 0)),
            pl.BlockSpec((1, tt), lambda g, i: (0, i)),
        ],
        [
            jax.ShapeDtypeStruct((G, T, 3 * C), BF),
            jax.ShapeDtypeStruct((G, T, C), BF),
            jax.ShapeDtypeStruct((G, D, 3 * C), BF),
            jax.ShapeDtypeStruct((T, D), BF),
        ],
        [
            by_group(3 * C),
            by_group(C),
            pl.BlockSpec((1, D, 3 * C), lambda g, i: (g, 0, 0)),
            pl.BlockSpec((tt, D), lambda g, i: (jnp.where(g == 0, i, T // tt - 1), 0)),
        ],
        [pltpu.VMEM((D, 3 * h), BF), pltpu.SemaphoreType.DMA],
        cost(9 * T * D * C * G, 2 * G * (T * D + 4 * C * D + 5 * T * C), G * T * B * C // HD),
        traffic,
    )


def back_body(B, C, hook, hg, wo, qkv, idc, idr, dqkv, dmix):
    tt = hg.shape[0]
    scale = 1.0 / math.sqrt(HD)
    hook("start")
    dmix[...] = dot(hg[...], wo[0], NT).astype(BF)
    masks = head_masks(C)
    wins = [w0 for w0, _ in windows(C)]

    def block(i, _):
        s = pl.ds(pl.multiple_of(i * B, B), B)
        ok = allow(idc, idr, s, B)
        dq = [None] * (C // LANES)
        dk, dv = list(dq), list(dq)
        cut = lambda n, w0: qkv[0, s, n * C + w0 : n * C + w0 + 2 * LANES]
        for g in range(0, len(wins), 8):
            hs = range(g, min(g + 8, len(wins)))
            q = [cut(0, wins[h]) * masks[h] for h in hs]
            gm = [dmix[s, wins[h] : wins[h] + 2 * LANES] * masks[h] for h in hs]
            p = softmaxes(q, [cut(1, wins[h]) for h in hs], ok)
            dp = [dot(a, cut(2, wins[h]), NT) for a, h in zip(gm, hs)]
            ds = [(a * (b - jnp.sum(a * b, axis=1, keepdims=True))).astype(BF) for a, b in zip(p, dp)]
            for h, a, b, c, d in zip(hs, p, gm, ds, q):
                put(dv, wins[h], dot(a.astype(BF), b, TN))
                put(dk, wins[h], dot(c, d, TN))
                put(dq, wins[h], dot(c, cut(1, wins[h]) * masks[h]))
        for n, tiles in enumerate((dq, dk, dv)):
            a = jnp.concatenate(tiles, axis=1)
            dqkv[0, s, n * C : (n + 1) * C] = (a if n == 2 else a * scale).astype(BF)
        return 0

    lax.fori_loop(0, tt // B, block, 0)
    hook("end")


def attend_back(hg, wo, qkv, idc, idr, traffic):
    T, D = hg.shape
    G, C, _ = wo.shape
    tt, B = pick(T, 512, 384, 256, 128), 128
    by_group = pl.BlockSpec((1, tt, 3 * C), lambda g, i: (g, i, 0))
    return launch(
        functools.partial(back_body, B, C),
        "attend_back",
        (G, T // tt),
        (hg, wo, qkv, idc, idr),
        [
            pl.BlockSpec((tt, D), lambda g, i: (i, 0)),
            pl.BlockSpec((1, C, D), lambda g, i: (g, 0, 0)),
            by_group,
            pl.BlockSpec((tt, 1), lambda g, i: (i, 0)),
            pl.BlockSpec((1, tt), lambda g, i: (0, i)),
        ],
        [jax.ShapeDtypeStruct((G, T, 3 * C), BF)],
        [by_group],
        [pltpu.VMEM((tt, C), BF)],
        cost(12 * T * D * C * G, 2 * G * (T * D + C * D + 6 * T * C), G * T * B * C // HD),
        traffic,
    )


def weight_body(C, G, hook, n1, low, dqkv, mixed, *dw):
    hook("start")
    h = C // 2
    u = dot(n1[...], dqkv[0], TN).astype(BF)
    o = dot(low[...], mixed[0], TN).astype(BF)
    for g in range(G):

        @pl.when(pl.program_id(0) == g)
        def _():
            for side in range(2):
                to = dw[2 * g + side]
                for i in range(3):
                    to[:, i * h : (i + 1) * h] = u[:, i * C + side * h : i * C + (side + 1) * h]
                to[:, 3 * h : 4 * h] = o[:, side * h : (side + 1) * h]

    hook("end")


def weight_grads(n1, low, dqkv, mixed, traffic):
    T, D = n1.shape
    G, _, C = mixed.shape
    rows = pick(D, 256)
    steps = D // rows

    def out(g):
        place = lambda n, i: (jnp.where(n == g, i, jnp.where(n < g, 0, steps - 1)), 0)
        return pl.BlockSpec((rows, 2 * C), place)

    columns = pl.BlockSpec((T, rows), lambda g, i: (0, i))
    return launch(
        functools.partial(weight_body, C, G),
        "weight_grads",
        (G, steps),
        (n1, low, dqkv, mixed),
        [
            columns,
            columns,
            pl.BlockSpec((1, T, 3 * C), lambda g, i: (g, 0, 0)),
            pl.BlockSpec((1, T, C), lambda g, i: (g, 0, 0)),
        ],
        [jax.ShapeDtypeStruct((D, 2 * C), BF)] * (2 * G),
        [out(g) for g in range(G) for _ in range(2)],
        [],
        cost(8 * T * D * C * G, 2 * G * (2 * T * D + 4 * T * C + 4 * D * C)),
        traffic,
    )


def project_body(x, gain, valid, mixed, wo, hidden, n2, square):
    @pl.when(pl.program_id(0) == 0)
    def _():
        square[...] = jnp.zeros_like(square)

    a = sum(dot(mixed[g], wo[g]) for g in range(wo.shape[0]))
    h = x[...].astype(F32) + a
    hidden[...] = h
    n2[...] = (h * rms(h) * gain[...].astype(F32)).astype(BF)
    square[...] += row_sum(valid[...] * a * a)


def project(x, gain, valid, mixed, wo):
    T, D = x.shape
    G, C, _ = wo.shape
    tt = pick(T, 256, 128)
    tile = lambda c: pl.BlockSpec((tt, c), lambda i: (i, 0))
    out, _ = launch(
        lambda hook, *refs: project_body(*refs),
        "project",
        (T // tt,),
        (x, gain, valid, mixed, wo),
        [tile(D), whole((1, D)), tile(1), pl.BlockSpec((G, tt, C), lambda i: (0, i, 0)), whole(wo.shape)],
        [jax.ShapeDtypeStruct((T, D), F32), jax.ShapeDtypeStruct((T, D), BF), jax.ShapeDtypeStruct((1, D), F32)],
        [tile(D), tile(D), pl.BlockSpec((1, D), lambda i: (0, 0))],
        [],
        cost(2 * T * D * D, 12 * T * D),
    )
    return out


def feed_body(
    hook, n2, g, hba, hbb, upa, upb, downa, downb, feed, n2g, dua, dub, dda, ddb, ba, bb, acc_f, acc_n, act, pg, wu, wd
):
    step = pl.program_id(0)
    T, D = n2.shape
    ft = hba.shape[1]
    chunk = pick(T, 768, 384, 128)
    hook("start")

    @pl.when(step == 0)
    def _():
        acc_f[...] = jnp.zeros_like(acc_f)
        acc_n[...] = jnp.zeros_like(acc_n)

    wu[:, :ft], wu[:, ft:] = upa[...], upb[...]
    wd[:ft, :], wd[ft:, :] = downa[...], downb[...]
    hb = jnp.concatenate([hba[...], hbb[...]], axis=1).astype(F32)
    ba[...] = jnp.zeros_like(ba)
    bb[...] = jnp.zeros_like(bb)

    def one(i, _):
        s = pl.ds(pl.multiple_of(i * chunk, chunk), chunk)
        p = dot(n2[s, :], wu[...]) + hb
        ag = dot(g[s, :], wd[...], NT)
        sg = 0.5 * jnp.tanh(0.5 * p) + 0.5
        ps = p * sg
        a = ps.astype(BF)
        q = (ag * (sg + ps * (1.0 - sg))).astype(BF)
        act[s, :] = a
        pg[s, :] = q
        b = row_sum(q.astype(F32))
        ba[...] += b[:, :ft]
        bb[...] += b[:, ft:]
        acc_f[s, :] += dot(a, wd[...])
        acc_n[s, :] += dot(q, wu[...], NT)
        return 0

    lax.fori_loop(0, T // chunk, one, 0)
    hook("middle")
    u = dot(n2[...], pg[...], TN).astype(BF)
    dua[...], dub[...] = u[:, :ft], u[:, ft:]
    d = dot(act[...], g[...], TN).astype(BF)
    dda[...], ddb[...] = d[:ft], d[ft:]

    @pl.when(step == pl.num_programs(0) - 1)
    def _():
        feed[...] = acc_f[...].astype(BF)
        n2g[...] = acc_n[...].astype(BF)

    hook("end")


def feed_forward(n2, g, biases, ups, downs, traffic=None):
    T, D = n2.shape
    F = biases[0].shape[1]
    ft = pick(F, 256)
    up = pl.BlockSpec((D, ft), lambda f: (0, f))
    down = pl.BlockSpec((ft, D), lambda f: (f, 0))
    bias = pl.BlockSpec((1, ft), lambda f: (0, f))
    return launch(
        feed_body,
        "feed_forward",
        (F // ft,),
        (n2, g, *biases, *ups, *downs),
        [whole((T, D)), whole((T, D)), bias, bias, up, up, down, down],
        [jax.ShapeDtypeStruct((T, D), BF)] * 2
        + [jax.ShapeDtypeStruct((D, F), BF)] * 2
        + [jax.ShapeDtypeStruct((F, D), BF)] * 2
        + [jax.ShapeDtypeStruct((1, F), F32)] * 2,
        [whole((T, D)), whole((T, D)), up, up, down, down, bias, bias],
        [
            pltpu.VMEM((T, D), F32),
            pltpu.VMEM((T, D), F32),
            pltpu.VMEM((T, 2 * ft), BF),
            pltpu.VMEM((T, 2 * ft), BF),
            pltpu.VMEM((D, 2 * ft), BF),
            pltpu.VMEM((2 * ft, D), BF),
        ],
        cost(24 * T * D * F, 16 * T * D + 16 * D * F, 2 * T * F),
        traffic,
    )


def middle_body(n, *refs):
    hidden, g, gain, out_bias, valid = refs[:5]
    feeds, grads = refs[5 : 5 + n], refs[5 + n : 5 + 2 * n]
    out, low, sums = refs[5 + 2 * n :]

    @pl.when(pl.program_id(0) == 0)
    def _():
        sums[...] = jnp.zeros_like(sums)

    h, go = hidden[...], g[...].astype(F32)
    f = sum(a[...].astype(F32) for a in feeds) + out_bias[...].astype(F32)
    ng = sum(a[...].astype(F32) for a in grads)
    result = h + f
    out[...] = result.astype(BF)
    r2 = rms(h)
    wg = ng * gain[...].astype(F32)
    inner = jnp.sum(wg * h, axis=1, keepdims=True)
    low[...] = (go + wg * r2 - h * (r2 * r2 * r2 * inner / h.shape[1])).astype(BF)
    v = valid[...]
    for i, a in enumerate((ng * h * r2, go, v * f * f, v * result * result)):
        sums[i : i + 1, :] += row_sum(a)


def middle(hidden, g, gain, out_bias, valid, feeds, grads):
    T, D = hidden.shape
    tt = pick(T, 256, 128)
    tile = lambda c: pl.BlockSpec((tt, c), lambda i: (i, 0))
    n = len(feeds)
    out, _ = launch(
        lambda hook, *refs: middle_body(n, *refs),
        "middle",
        (T // tt,),
        (hidden, g, gain, out_bias, valid, *feeds, *grads),
        [tile(D), tile(D), whole((1, D)), whole((1, D)), tile(1)] + [tile(D)] * (2 * n),
        [jax.ShapeDtypeStruct((T, D), BF), jax.ShapeDtypeStruct((T, D), BF), jax.ShapeDtypeStruct((8, D), F32)],
        [tile(D), tile(D), pl.BlockSpec((8, D), lambda i: (0, 0))],
        [],
        cost(40 * T * D, (10 + 4 * n) * T * D),
    )
    return out


def last_body(hook, x, gain, low, dqkv, w, out, part):
    hook("start")

    @pl.when(pl.program_id(0) == 0)
    def _():
        part[...] = jnp.zeros_like(part)

    ng = sum(dot(dqkv[g], w[g], NT) for g in range(w.shape[0]))
    t = x[...].astype(F32)
    r1 = rms(t)
    wg = ng * gain[...].astype(F32)
    inner = jnp.sum(wg * t, axis=1, keepdims=True)
    out[...] = low[...].astype(F32) + wg * r1 - t * (r1 * r1 * r1 * inner / t.shape[1])
    part[...] += row_sum(ng * t * r1)
    hook("end")


def last(x, gain, low, dqkv, w, traffic):
    T, D = x.shape
    G, _, K = w.shape
    tt = pick(T, 256, 128)
    tile = lambda c: pl.BlockSpec((tt, c), lambda i: (i, 0))
    return launch(
        last_body,
        "last",
        (T // tt,),
        (x, gain, low, dqkv, w),
        [tile(D), whole((1, D)), tile(D), pl.BlockSpec((G, tt, K), lambda i: (0, i, 0)), whole(w.shape)],
        [jax.ShapeDtypeStruct((T, D), F32), jax.ShapeDtypeStruct((1, D), F32)],
        [tile(D), pl.BlockSpec((1, D), lambda i: (0, 0))],
        [],
        cost(6 * T * D * D, 8 * T * D + 6 * D * D),
        traffic,
    )


def swap(a, axis, bit):
    return lax.ppermute(a, axis, [(i, i ^ bit) for i in range(lax.axis_size(axis))])


def all_sum(a):
    for axis in ("mp", "dp"):
        bit = 1
        while bit < lax.axis_size(axis):
            a = a + swap(a, axis, bit)
            bit *= 2
    return a


def segments(lengths):
    slots = lengths.shape[1]
    upto = lax.broadcasted_iota(jnp.int32, (1, slots, slots), 2) <= lax.broadcasted_iota(
        jnp.int32, (1, slots, slots), 1
    )
    ends = jnp.sum(jnp.where(upto, lengths[:, None, :], 0), axis=2)
    places = lax.broadcasted_iota(jnp.int32, (lengths.shape[0], L, slots), 1)
    return jnp.sum((ends[:, None, :] <= places).astype(jnp.int32), axis=2)


def merge(*dicts):
    return {k: v for d in dicts for k, v in d.items()}


def fused(x, cotangent, weights, gains, out_bias, valid, ids, mp):
    T, D = x.shape
    joined, wo, up, down, bias = weights
    h = wo.shape[0]
    hidden_units = up.shape[1]
    near, far, deep = ("dp", 1), ("dp", 2), ("dp", 4)

    J, W = Gather("j", D, 3 * h), Gather("w", h, D)
    U, V = Gather("u", D, hidden_units), Gather("v", hidden_units, D)
    both, four = (J, W), (J, W, U, V)
    steps = T // pick(T, 512, 384, 256, 128)
    t = Traffic(
        1,
        [CORE, Y, near, far],
        dict(j=joined, w=wo, u=up, v=down),
        merge(*[g.buffers("s", "q", "o", "p") for g in both], *[g.buffers("s", "q") for g in (U, V)]),
    )
    t.on(0, "start", *[g.start(s) for s in "sy" for g in both], J.wait("s"))
    t.on(1, "start", *[g.wait("y") for g in both], *[g.start("a") for g in both])
    t.on(1, "start", *[g.start(s) for s in "ys" for g in (U, V)])
    t.on(steps, "start", *[g.wait("a") for g in both], *[g.start("b") for g in both])
    t.on(steps, "start", *[g.wait("b") for g in both], *[g.start("p") for g in both], J.wait("p"))
    t.on(2 * steps - 1, "end", W.wait("s"), W.wait("p"), *[g.wait(s) for s in "ys" for g in (U, V)])
    (qkv, mixed, w, n1), got = attend(x, gains[0], *ids, h, [("j", "js"), ("jo", "jp")], t)
    wo_all = jnp.stack([jnp.concatenate([wo, got["ws"]]), jnp.concatenate([got["wo"], got["wp"]])])
    hidden, n2, att_square = project(x, gains[1], valid, mixed, wo_all)

    bias_o = swap(bias, "mp", 2)
    t = Traffic(
        2,
        [CORE, near, far],
        dict(uq=got["uq"], vq=got["vq"], u=up, v=down),
        merge(*[g.buffers("o", "p") for g in (U, V)]),
    )
    fs = hidden_units // pick(hidden_units, 256)
    t.on(0, "start", *[g.start("a") for g in (U, V)])
    t.on(3, "start", *[g.wait("a") for g in (U, V)], *[g.start("b") for g in (U, V)])
    t.on(fs - 1, "middle", *[g.wait("b") for g in (U, V)], *[g.start("p") for g in (U, V)])
    t.on(fs - 1, "end", *[g.wait("p") for g in (U, V)])
    own, far_weights = feed_forward(
        n2, cotangent, (bias, swap(bias, "mp", 1)), (up, got["us"]), (down, got["vs"]), t
    )

    a, b = (1, 2, 4), (2, 1, 4)
    U0, D0 = Stream("u0", "u0a", "u0b", D, hidden_units, a), Stream("d0", "d0a", "d0b", hidden_units, D, b)
    U1, D1 = Stream("u1", "u1a", "u1b", D, hidden_units, a), Stream("d1", "d1a", "d1b", hidden_units, D, b)
    half = D // 2
    att = [
        [Stream(f"j{n}{m}", f"j{n}a", f"j{n}b", half, 4 * h, (a, b)[m], m * half) for m in range(2)]
        for n in range(2)
    ]
    first = (U0, D0)
    second = (U1, D1)
    t = Traffic(
        3,
        [CORE, near, far],
        dict(u0a=own[2], u0b=own[3], d0a=own[4], d0b=own[5]),
        merge(*[s.buffers("c", "s0", "r0", "s1", "r1") for s in first]),
    )
    t.on(0, "start", *[s.start_core for s in first])
    t.on(1, "start", *[s.wait_core for s in first], *[s.start(0) for s in first])
    t.on(fs - 1, "start", *[s.wait(0) for s in first], *[s.start(1) for s in first])
    t.on(fs - 1, "end", *[s.wait(1) for s in first])
    other, left = feed_forward(
        n2,
        cotangent,
        (bias_o, swap(bias_o, "mp", 1)),
        (far_weights["uo"], far_weights["up"]),
        (far_weights["vo"], far_weights["vp"]),
        t,
    )
    feeds = [own, other]
    out, low, sums = middle(
        hidden, cotangent, gains[1], out_bias, valid, [f[0] for f in feeds], [f[1] for f in feeds]
    )

    held = dict(u0a=own[2], d0a=own[4], u1a=other[2], u1b=other[3], d1a=other[4], d1b=other[5])
    held |= {k: left[k] for k in left if k[2] in "cr"}
    t = Traffic(
        4,
        [CORE, near, far, deep],
        held,
        merge(*[s.buffers("s2", "r2", "e") for s in first], *[s.buffers("c", "s0", "r0") for s in second]),
    )
    t.on(0, "start", *[s.start_core for s in second], *[s.start(2) for s in first])
    t.on(1, "start", *[s.wait_core for s in second], *[s.start(0) for s in second])
    t.on(3, "start", *[s.wait(2) for s in first], *[s.keep for s in first])
    t.on(2 * steps - 1, "end", *[s.wait(0) for s in second])
    (dqkv,), left = attend_back(low, wo_all, qkv, *ids, t)
    e0 = {k: left[k] for k in ("u0e", "d0e")}

    held = dict(u1a=other[2], d1a=other[4]) | {k: left[k] for k in left if k[:2] in ("u1", "d1") and k[2] in "cr"}
    t = Traffic(
        5, [near, far, deep], held, merge(*[s.buffers("s1", "r1", "s2", "r2", "e") for s in second])
    )
    ws = D // pick(D, 256)
    t.on(0, "start", *[s.start(1) for s in second])
    t.on(ws + 1, "start", *[s.wait(1) for s in second], *[s.start(2) for s in second])
    t.on(2 * ws - 1, "end", *[s.wait(2) for s in second], *[s.keep for s in second])
    dw, left = weight_grads(n1, low, dqkv, mixed, t)

    held = dict(j0a=dw[0], j0b=dw[1], j1a=dw[2], j1b=dw[3], u1e=left["u1e"], d1e=left["d1e"]) | e0
    flat = [s for pair in att for s in pair]
    t = Traffic(
        6,
        [CORE, Y, near, far, deep],
        held,
        merge(
            *[s.buffers("f") for s in first],
            *[s.buffers("y") for s in second],
            *[s.buffers("c", "s0", "r0", "s1", "r1", "s2", "r2", "e") for s in flat],
            *[s.buffers("f") for s in att[0]],
            *[s.buffers("y") for s in att[1]],
        ),
    )
    ls = T // pick(T, 256, 128)
    t.on(0, "start", *[s.start_core for s in flat], *[s.start_cross for s in second])
    t.on(1, "start", *[s.wait_core for s in flat], *[s.start(0) for s in flat])
    t.on(3, "start", *[s.wait_cross for s in second])
    t.on(3, "start", *[f(s) for s, o in zip(first, second) for f in (lambda s: s.total(o), lambda s: s.start_spread(2))])
    end = [s.wait(0) for s in flat] + [s.start(1) for s in flat]
    end += [f for s in first for f in (s.wait_spread(2), s.start_spread(1))]
    end += [s.wait(1) for s in flat] + [s.start(2) for s in flat]
    end += [f for s in first for f in (s.wait_spread(1), s.start_spread(0))]
    end += [s.wait(2) for s in flat] + [s.keep for s in flat]
    end += [s.start_cross for s in att[1]] + [s.wait_cross for s in att[1]]
    end += [f for s, o in zip(*att) for f in (s.total(o), s.start_spread(2))]
    for j in (2, 1):
        end += [f for s in att[0] for f in (s.wait_spread(j), s.start_spread(j - 1))]
    end += [s.wait_spread(0) for s in (*att[0], *first)]
    t.on(ls - 1, "end", *end)
    (input_gradient, first_part), done = last(x, gains[0], low, dqkv, w, t)
    joined_total = jnp.concatenate([done["j00f"], done["j01f"]])
    units = jnp.zeros((1, lax.axis_size("mp") * hidden_units), F32)
    for change, part in ((0, own[6]), (1, own[7]), (2, other[6]), (3, other[7])):
        units = lax.dynamic_update_slice(units, part, (0, (mp ^ change) * hidden_units))
    return (out, input_gradient, joined_total, done["u0f"], done["d0f"]), (units, sums, att_square, first_part)


def gathered(x, cotangent, weights, gains, out_bias, valid, ids):
    D = x.shape[1]
    joined, wo, up, down, bias = weights
    every = lambda a, d: lax.all_gather(a, "mp", axis=d, tiled=True)
    two = lambda a, d: tuple(jnp.split(every(a, d), 2, axis=d))
    sides = [jnp.concatenate(p, axis=1) for p in zip(*(two(a, 1) for a in jnp.split(joined, 3, axis=1)))]
    plain = Traffic(0, [], dict(a=sides[0], b=sides[1]), {})
    (qkv, mixed, w, n1), _ = attend(x, gains[0], *ids, sides[0].shape[1] // 3, [("a", "b")], plain)
    wo_all = every(wo, 0)[None]
    hidden, n2, att_square = project(x, gains[1], valid, mixed, wo_all)
    f, _ = feed_forward(n2, cotangent, two(bias, 1), two(up, 1), two(down, 0))
    out, low, sums = middle(hidden, cotangent, gains[1], out_bias, valid, [f[0]], [f[1]])
    (dqkv,), _ = attend_back(low, wo_all, qkv, *ids, None)
    dw, _ = weight_grads(n1, low, dqkv, mixed, None)
    (input_gradient, first_part), _ = last(x, gains[0], low, dqkv, w, None)

    def total(pair, d):
        part = lax.psum_scatter(jnp.concatenate(pair, axis=d), "mp", scatter_dimension=d, tiled=True)
        return lax.psum(part, "dp")

    cut = [jnp.split(a, 4, axis=1) for a in dw]
    joined_total = jnp.concatenate([total(pair, 1) for pair in zip(*cut)], axis=1)
    grads = (out, input_gradient, joined_total, total(f[2:4], 1), total(f[4:6], 0))
    return grads, (jnp.concatenate(f[6:], axis=1), sums, att_square, first_part)


def per_device(
    tokens,
    lengths,
    cotangent,
    query_weight,
    key_weight,
    value_weight,
    out_weight,
    up_weight,
    hidden_bias,
    down_weight,
    output_bias,
    first_gain,
    second_gain,
):
    T, D = tokens.shape
    h = query_weight.shape[1]
    rows = T // L
    mp = lax.axis_index("mp")
    segment_ids = segments(lax.dynamic_slice_in_dim(lengths, mp * rows, rows))
    valid = (segment_ids < SLOTS).reshape(-1, 1).astype(F32)
    ids = (segment_ids + L * lax.broadcasted_iota(jnp.int32, (rows, L), 0)).reshape(-1)
    ids = (ids[:, None], ids[None, :])
    joined = jnp.concatenate([query_weight, key_weight, value_weight], axis=1)
    bias = hidden_bias.reshape(1, -1)
    gains = (first_gain.reshape(1, -1), second_gain.reshape(1, -1))
    weights = (joined, out_weight, up_weight, down_weight, bias)
    rest = (gains, output_bias.reshape(1, -1), valid, ids)
    if lax.axis_size("mp") == 4 and lax.axis_size("dp") == 8:
        grads, parts = fused(tokens, cotangent, weights, *rest, mp)
    else:
        grads, parts = gathered(tokens, cotangent, weights, *rest)
    out, input_gradient, joined_total, up_total, down_total = grads
    units, sums, att_square, first_part = parts
    n = units.shape[1]
    squares = jnp.stack([jnp.sum(att_square), jnp.sum(sums[2]), jnp.sum(sums[3]), jnp.sum(valid)])
    small = all_sum(jnp.concatenate([units[0], sums[0], sums[1], squares]))
    squares = small[n + 2 * D :]
    joined_total = joined_total.astype(F32)
    return (
        out,
        input_gradient,
        joined_total[:, :h],
        joined_total[:, h : 2 * h],
        joined_total[:, 2 * h : 3 * h],
        joined_total[:, 3 * h :].T,
        up_total.astype(F32),
        lax.dynamic_slice_in_dim(small, mp * bias.shape[1], bias.shape[1]),
        down_total.astype(F32),
        small[n + D : n + 2 * D],
        all_sum(first_part[0]),
        small[n : n + D],
        jnp.sqrt(squares[:3] / (squares[3] * D)),
    )


def solution(mesh):
    return jax.shard_map(
        per_device,
        mesh=mesh,
        in_specs=(
            P(("dp", "mp"), None),
            P("dp", None),
            P(("dp", "mp"), None),
            P(None, "mp"),
            P(None, "mp"),
            P(None, "mp"),
            P("mp", None),
            P(None, "mp"),
            P("mp"),
            P("mp", None),
            P(),
            P(),
            P(),
        ),
        out_specs=(
            P(("dp", "mp"), None),
            P(("dp", "mp"), None),
            P(None, "mp"),
            P(None, "mp"),
            P(None, "mp"),
            P("mp", None),
            P(None, "mp"),
            P("mp"),
            P("mp", None),
            P(),
            P(),
            P(),
            P(),
        ),
        check_vma=False,
    )
```

```python
import functools
import math

import jax
import jax.numpy as jnp
from jax import lax
from jax.experimental import pallas as pl
from jax.experimental.pallas import tpu as pltpu
from jax.sharding import PartitionSpec as P

HD = 80
L = 64
SLOTS = 32
LANES = 128
EPSILON = 1e-06
MASKED = -1e30
F32 = jnp.float32
BF = jnp.bfloat16
NN = (((1,), (0,)), ((), ()))
NT = (((1,), (1,)), ((), ()))
TN = (((0,), (0,)), ((), ()))
VMEM_BYTES = 60 << 20


def dot(a, b, dims=NN):
    return lax.dot_general(a, b, dims, preferred_element_type=F32)


def pick(n, *sizes):
    return next((s for s in sizes if n % s == 0), n)


def whole(shape):
    return pl.BlockSpec(shape, lambda *i: (0,) * len(shape), pipeline_mode=pl.Buffered(1))


def cost(flops, nbytes, exps=0):
    return pl.CostEstimate(flops=int(flops), bytes_accessed=int(nbytes), transcendentals=int(exps))


def row_sum(x):
    return jnp.sum(x, axis=0, keepdims=True)


def rms(x):
    return lax.rsqrt(jnp.mean(x * x, axis=1, keepdims=True) + EPSILON)


MESH = pl.DeviceIdType.MESH
CORE, Y = ("mp", 1), ("mp", 2)


def bit_of(axis, bit):
    return lax.rem(lax.axis_index(axis) // bit, 2)


def flip(axis, bit):
    return {axis: lax.axis_index(axis) + bit - 2 * bit * bit_of(axis, bit)}


class Traffic:
    def __init__(self, number, partners, arrays, buffers, scratch=None):
        self.number, self.partners = number, partners
        self.arrays, self.buffers, self.scratch = arrays, buffers, scratch or {}
        self.events, self.slots, self.refs = [], {}, {}

    def on(self, step, place, *actions):
        self.events += [(step, place, f) for f in actions]
        return self

    def run(self, step, place):
        for at, where, action in self.events:
            if where == place:
                pl.when(step == at)(functools.partial(action, self))

    def greet(self):
        sem = pltpu.get_barrier_semaphore()
        for p in self.partners:
            pl.semaphore_signal(sem, inc=1, device_id=flip(*p), device_id_type=MESH)
        pl.semaphore_wait(sem, len(self.partners))

    def copy(self, name, src, dst, to):
        i = self.slots.setdefault(name, len(self.slots))
        return pltpu.make_async_remote_copy(
            src_ref=src,
            dst_ref=dst,
            send_sem=self.sems.at[0, i],
            recv_sem=self.sems.at[1, i],
            device_id=flip(*to),
            device_id_type=MESH,
        )

    def local(self, name, src, dst):
        i = self.slots.setdefault(name, len(self.slots))
        return pltpu.make_async_copy(src, dst, self.sems.at[0, i])


COPIES = 48


def launch(body, name, grid, args, in_specs, outs, out_specs, scratch, cost_estimate, traffic=None):
    n_args, n_outs = len(args), len(outs)
    names, arrays, buffers = [], [], []
    if traffic is not None:
        names = [*traffic.arrays, *traffic.buffers]
        arrays = list(traffic.arrays.values())
        buffers = [jax.ShapeDtypeStruct(s, BF) for s in traffic.buffers.values()]
        names += [*traffic.scratch]
        scratch = [*scratch, *traffic.scratch.values(), pltpu.SemaphoreType.DMA((2, COPIES))]

    def kernel(*refs):
        hook = lambda place: None
        inputs, refs = refs[:n_args], refs[n_args:]
        moved, refs = refs[: len(arrays)], refs[len(arrays) :]
        results, refs = refs[:n_outs], refs[n_outs:]
        landing, refs = refs[: len(buffers)], refs[len(buffers) :]
        if traffic is not None:
            step = pl.program_id(0)
            for d in range(1, len(grid)):
                step = step * grid[d] + pl.program_id(d)
            traffic.sems, refs = refs[-1], refs[:-1]
            n = len(refs) - len(traffic.scratch)
            traffic.refs = dict(zip(names, [*moved, *landing, *refs[n:]]))
            refs = refs[:n]
            if traffic.partners:
                pl.when(step == 0)(traffic.greet)
            hook = lambda place: traffic.run(step, place)
        body(hook, *inputs, *results, *refs)

    anywhere = pl.BlockSpec(memory_space=pl.ANY)
    out = pl.pallas_call(
        kernel,
        grid=grid,
        in_specs=[*in_specs, *[anywhere] * len(arrays)],
        out_specs=[*out_specs, *[anywhere] * len(buffers)],
        out_shape=[*outs, *buffers],
        scratch_shapes=scratch,
        compiler_params=pltpu.CompilerParams(
            vmem_limit_bytes=VMEM_BYTES,
            **({} if traffic is None or not traffic.partners else dict(collective_id=traffic.number, has_side_effects=True)),
        ),
        cost_estimate=cost_estimate,
        name=name,
    )(*args, *arrays)
    return out[:n_outs], dict(zip(names[len(arrays) : len(arrays) + len(buffers)], out[n_outs:]))


def add_rows(sources, target, rows):
    columns = target.shape[1]
    tile = pl.BlockSpec((rows // 2 if rows // 2 % 16 == 0 else rows, columns), lambda i: (i, 0))

    def body(*refs):
        refs[-1][...] = sum(r[...].astype(F32) for r in refs[:-1]).astype(BF)

    pltpu.emit_pipeline(
        body, grid=(rows // tile.block_shape[0],), in_specs=[tile] * len(sources), out_specs=[tile]
    )(*[r.at[pl.ds(pl.multiple_of(o, 16), rows), :] for r, o in sources], target)


class Stream:
    def __init__(self, tag, mine, theirs, rows, columns, order, cut, base=0, joins=None):
        self.tag, self.mine, self.theirs, self.base = tag, mine, theirs, base
        self.rows, self.columns, self.order = rows, columns, order
        self.cut, self.joins = cut, joins

    def name(self, what):
        return self.tag + what

    def buffers(self, *what):
        size = lambda w: self.rows if w[0] in "cf" else self.rows >> self.cut if w[0] in "ey" else self.rows >> (int(w[1]) + 1)
        return {self.name(w): (size(w), self.columns) for w in what}

    def place(self, stages):
        first, n = 0, self.rows
        for bit in self.order[:stages]:
            n //= 2
            first = first + bit_of("dp", bit) * n
        return first, n

    def sources(self, t, first, arrived):
        out = [(t.refs[self.mine], first + self.base), (t.refs[self.name("c")], first)]
        for j in range(arrived):
            out.append((t.refs[self.name(f"r{j}")], first - self.place(j + 1)[0]))
        if self.joins is not None and arrived >= self.cut:
            out.append((t.refs[self.joins + "y"], first - self.place(self.cut)[0]))
        return out

    def core(self, t):
        src = t.refs[self.theirs].at[pl.ds(self.base, self.rows), :]
        return t.copy(self.name("c"), src, t.refs[self.name("c")], CORE)

    def start_core(self, t):
        self.core(t).start()

    def wait_core(self, t):
        self.core(t).wait()

    def exchange(self, t, j):
        return t.copy(self.name(f"r{j}"), t.refs[self.name(f"s{j}")], t.refs[self.name(f"r{j}")], ("dp", self.order[j]))

    def start(self, j):
        def action(t):
            first, n = self.place(j)
            n //= 2
            sent = first + (1 - bit_of("dp", self.order[j])) * n
            add_rows(self.sources(t, sent, j), t.refs[self.name(f"s{j}")], n)
            self.exchange(t, j).start()

        return action

    def wait(self, j):
        return lambda t: self.exchange(t, j).wait()

    def keep(self, t):
        first, n = self.place(self.cut)
        add_rows(self.sources(t, first, self.cut), t.refs[self.name("e")], n)

    def cross(self, t):
        return t.copy(self.name("y"), t.refs[self.name("e")], t.refs[self.name("y")], Y)

    def start_cross(self, t):
        self.cross(t).start()

    def wait_cross(self, t):
        self.cross(t).wait()

    def total(self, t):
        first, n = self.place(len(self.order))
        target = t.refs[self.name("f")].at[pl.ds(pl.multiple_of(first, 16), n), :]
        add_rows(self.sources(t, first, len(self.order)), target, n)

    def spread(self, t, j):
        first, n = self.place(j + 1)
        part = t.refs[self.name("f")].at[pl.ds(pl.multiple_of(first, 16), n), :]
        return t.copy(self.name(f"f{j}"), part, part, ("dp", self.order[j]))

    def start_spread(self, j):
        return lambda t: self.spread(t, j).start()

    def wait_spread(self, j):
        return lambda t: self.spread(t, j).wait()


def sum_rows(sources, target, rows):
    step = pick(rows, 80, 64, 32, 16)

    def one(i, _):
        part = lambda o: pl.ds(pl.multiple_of(o + i * step, 16), step)
        target[part(0), :] = sum(r[part(o), :].astype(F32) for r, o in sources).astype(BF)
        return 0

    lax.fori_loop(0, rows // step, one, 0)


class Near(Stream):
    def scratch(self, *what):
        size = lambda w: self.rows if w == "m" else self.buffers(w)[self.name(w)][0]
        return {self.name(w): pltpu.VMEM((size(w), self.columns), BF) for w in what}

    def sources(self, t, first, arrived):
        out = super().sources(t, first, arrived)
        return [(t.refs[self.name("m")], first), *out[1:]]

    def load(self, t):
        src = t.refs[self.mine].at[pl.ds(self.base, self.rows), :]
        return t.local(self.name("m"), src, t.refs[self.name("m")])

    def start_load(self, t):
        self.load(t).start()

    def wait_load(self, t):
        self.load(t).wait()

    def start(self, j):
        def action(t):
            first, n = self.place(j)
            n //= 2
            sent = first + (1 - bit_of("dp", self.order[j])) * n
            sum_rows(self.sources(t, sent, j), t.refs[self.name(f"s{j}")], n)
            self.exchange(t, j).start()

        return action

    def keep(self, t):
        first, n = self.place(self.cut)
        sum_rows(self.sources(t, first, self.cut), t.refs[self.name("e")], n)

    def total(self, t):
        first, n = self.place(len(self.order))
        target = t.refs[self.name("f")].at[pl.ds(pl.multiple_of(first, 16), n), :]
        sum_rows(self.sources(t, first, len(self.order)), target, n)

    def store(self, t):
        out = t.refs["joined"].at[pl.ds(self.base, self.rows), :]
        return t.local(self.name("o"), t.refs[self.name("f")], out)

    def start_store(self, t):
        self.store(t).start()

    def wait_store(self, t):
        self.store(t).wait()


class Gather:
    def __init__(self, tag, rows, columns):
        self.tag, self.rows, self.columns = tag, rows, columns
        self.n = rows // 4

    def buffers(self, *what):
        return {self.tag + w: (self.n if w == "q" else self.rows, self.columns) for w in what}

    def quarter(self, ref, flip_x=0, flip_z=0, first=0, rows=None):
        x, z = bit_of("dp", 1), bit_of("dp", 2)
        x, z = (1 - x if flip_x else x), (1 - z if flip_z else z)
        start = pl.multiple_of((2 * z + x) * self.n + first, 16)
        return ref.at[pl.ds(start, self.n if rows is None else rows), :]

    def copies(self, t, step):
        own, o = t.refs[self.tag], t.refs.get(self.tag + "o")
        name = self.tag + step
        if step == "s":
            return [t.copy(name, own, t.refs[name], CORE)]
        if step == "y":
            return [t.copy(name, self.quarter(own), t.refs[self.tag + "q"], Y)]
        if step == "a":
            q = t.refs[self.tag + "q"]
            return [t.copy(name + str(b), q, self.quarter(o), ("dp", b)) for b in (1, 2)] + [
                t.local(name + "l", q, self.quarter(o))
            ]
        if step == "b":
            top = (self.n // 2 + 15) // 16 * 16
            to_x = self.quarter(o, flip_z=1, rows=top)
            to_z = self.quarter(o, flip_x=1, first=top, rows=self.n - top)
            return [t.copy(name + "1", to_x, to_x, ("dp", 1)), t.copy(name + "2", to_z, to_z, ("dp", 2))]
        return [t.copy(name, o, t.refs[self.tag + "p"], CORE)]

    def start(self, step):
        def action(t):
            for c in self.copies(t, step):
                c.start()

        return action

    def wait(self, step):
        def action(t):
            for c in self.copies(t, step):
                c.wait()

        return action


def windows(C):
    out = []
    for h in range(C // HD):
        w = min(LANES * (HD * h // LANES), C - 2 * LANES)
        out.append((w, HD * h - w))
    return out


def head_masks(C):
    lane = lax.broadcasted_iota(jnp.int32, (1, 2 * LANES), 1)
    return [jnp.where((lane >= lo) & (lane < lo + HD), 1.0, 0.0).astype(BF) for _, lo in windows(C)]


def softmaxes(qs, ks, allowed):
    s = [jnp.where(allowed, dot(q, k, NT) * (1.0 / math.sqrt(HD)), MASKED) for q, k in zip(qs, ks)]
    e = [jnp.exp(x - jnp.max(x, axis=1, keepdims=True)) for x in s]
    return [x * (1.0 / jnp.sum(x, axis=1, keepdims=True)) for x in e]


def allow(idc, idr, s, B):
    causal = lax.broadcasted_iota(jnp.int32, (B, B), 1) <= lax.broadcasted_iota(
        jnp.int32, (B, B), 0
    )
    return (idc[s, :] == idr[:, s]) & causal


def put(tiles, w, val):
    for n in range(2):
        t = w // LANES + n
        part = val[:, n * LANES : (n + 1) * LANES]
        tiles[t] = part if tiles[t] is None else tiles[t] + part


def fwd_body(B, C, pairs, traffic, hook, x, gain, idc, idr, qkv, mixed, w, n1, ab, sem):
    group = pl.program_id(0)
    tt = x.shape[0]
    first = pl.program_id(1) == 0
    hook("start")
    h = C // 2
    for g, pair in enumerate(pairs):

        @pl.when(first & (group == g))
        def _():
            for side in range(2):
                c = pltpu.make_async_copy(traffic.refs[pair[side]], ab, sem)
                c.start()
                c.wait()
                a = ab[...]
                for i in range(3):
                    w[0, :, i * C + side * h : i * C + (side + 1) * h] = a[:, i * h : (i + 1) * h]

    t = x[...].astype(F32)
    normed = (t * rms(t) * gain[...].astype(F32)).astype(BF)

    @pl.when(group == 0)
    def _():
        n1[...] = normed

    qkv[0] = dot(normed, w[0]).astype(BF)
    hook("middle")
    masks = head_masks(C)
    wins = [w0 for w0, _ in windows(C)]

    def block(i, _):
        s = pl.ds(pl.multiple_of(i * B, B), B)
        ok = allow(idc, idr, s, B)
        tiles = [None] * (C // LANES)
        cut = lambda n, w0: qkv[0, s, n * C + w0 : n * C + w0 + 2 * LANES]
        for g in range(0, len(wins), 8):
            hs = range(g, min(g + 8, len(wins)))
            p = softmaxes([cut(0, wins[h]) * masks[h] for h in hs], [cut(1, wins[h]) for h in hs], ok)
            o = [dot(a.astype(BF), cut(2, wins[h]) * masks[h]) for a, h in zip(p, hs)]
            for h, a in zip(hs, o):
                put(tiles, wins[h], a)
        mixed[0, s, :] = jnp.concatenate(tiles, axis=1).astype(BF)
        return 0

    lax.fori_loop(0, tt // B, block, 0)
    hook("end")


def attend(x, gain, idc, idr, h, pairs, traffic):
    T, D = x.shape
    C, G = 2 * h, len(pairs)
    tt, B = pick(T, 512, 384, 256, 128), 128
    by_group = lambda c: pl.BlockSpec((1, tt, c), lambda g, i: (g, i, 0))
    return launch(
        functools.partial(fwd_body, B, C, pairs, traffic),
        "attend",
        (G, T // tt),
        (x, gain, idc, idr),
        [
            pl.BlockSpec((tt, D), lambda g, i: (i, 0)),
            whole((1, D)),
            pl.BlockSpec((tt, 1), lambda g, i: (i, 0)),
            pl.BlockSpec((1, tt), lambda g, i: (0, i)),
        ],
        [
            jax.ShapeDtypeStruct((G, T, 3 * C), BF),
            jax.ShapeDtypeStruct((G, T, C), BF),
            jax.ShapeDtypeStruct((G, D, 3 * C), BF),
            jax.ShapeDtypeStruct((T, D), BF),
        ],
        [
            by_group(3 * C),
            by_group(C),
            pl.BlockSpec((1, D, 3 * C), lambda g, i: (g, 0, 0)),
            pl.BlockSpec((tt, D), lambda g, i: (jnp.where(g == 0, i, T // tt - 1), 0)),
        ],
        [pltpu.VMEM((D, 3 * h), BF), pltpu.SemaphoreType.DMA],
        cost(9 * T * D * C * G, 2 * G * (T * D + 4 * C * D + 5 * T * C), G * T * B * C // HD),
        traffic,
    )


def back_body(B, C, hook, hg, wo, qkv, idc, idr, dqkv, dmix):
    tt = hg.shape[0]
    scale = 1.0 / math.sqrt(HD)
    hook("start")
    dmix[...] = dot(hg[...], wo[0], NT).astype(BF)
    masks = head_masks(C)
    wins = [w0 for w0, _ in windows(C)]

    def block(i, _):
        s = pl.ds(pl.multiple_of(i * B, B), B)
        ok = allow(idc, idr, s, B)
        dq = [None] * (C // LANES)
        dk, dv = list(dq), list(dq)
        cut = lambda n, w0: qkv[0, s, n * C + w0 : n * C + w0 + 2 * LANES]
        for g in range(0, len(wins), 8):
            hs = range(g, min(g + 8, len(wins)))
            q = [cut(0, wins[h]) * masks[h] for h in hs]
            gm = [dmix[s, wins[h] : wins[h] + 2 * LANES] * masks[h] for h in hs]
            p = softmaxes(q, [cut(1, wins[h]) for h in hs], ok)
            dp = [dot(a, cut(2, wins[h]), NT) for a, h in zip(gm, hs)]
            ds = [(a * (b - jnp.sum(a * b, axis=1, keepdims=True))).astype(BF) for a, b in zip(p, dp)]
            for h, a, b, c, d in zip(hs, p, gm, ds, q):
                put(dv, wins[h], dot(a.astype(BF), b, TN))
                put(dk, wins[h], dot(c, d, TN))
                put(dq, wins[h], dot(c, cut(1, wins[h]) * masks[h]))
        for n, tiles in enumerate((dq, dk, dv)):
            a = jnp.concatenate(tiles, axis=1)
            dqkv[0, s, n * C : (n + 1) * C] = (a if n == 2 else a * scale).astype(BF)
        return 0

    lax.fori_loop(0, tt // B, block, 0)
    hook("end")


def attend_back(hg, wo, qkv, idc, idr, traffic):
    T, D = hg.shape
    G, C, _ = wo.shape
    tt, B = pick(T, 512, 384, 256, 128), 128
    by_group = pl.BlockSpec((1, tt, 3 * C), lambda g, i: (g, i, 0))
    return launch(
        functools.partial(back_body, B, C),
        "attend_back",
        (G, T // tt),
        (hg, wo, qkv, idc, idr),
        [
            pl.BlockSpec((tt, D), lambda g, i: (i, 0)),
            pl.BlockSpec((1, C, D), lambda g, i: (g, 0, 0)),
            by_group,
            pl.BlockSpec((tt, 1), lambda g, i: (i, 0)),
            pl.BlockSpec((1, tt), lambda g, i: (0, i)),
        ],
        [jax.ShapeDtypeStruct((G, T, 3 * C), BF)],
        [by_group],
        [pltpu.VMEM((tt, C), BF)],
        cost(12 * T * D * C * G, 2 * G * (T * D + C * D + 6 * T * C), G * T * B * C // HD),
        traffic,
    )


def weight_body(C, G, hook, n1, low, dqkv, mixed, *dw):
    hook("start")
    h = C // 2
    u = dot(n1[...], dqkv[0], TN).astype(BF)
    o = dot(low[...], mixed[0], TN).astype(BF)
    for g in range(G):

        @pl.when(pl.program_id(0) == g)
        def _():
            for side in range(2):
                to = dw[2 * g + side]
                for i in range(3):
                    to[:, i * h : (i + 1) * h] = u[:, i * C + side * h : i * C + (side + 1) * h]
                to[:, 3 * h : 4 * h] = o[:, side * h : (side + 1) * h]

    hook("end")


def weight_grads(n1, low, dqkv, mixed, traffic):
    T, D = n1.shape
    G, _, C = mixed.shape
    rows = pick(D, 256)
    steps = D // rows

    def out(g):
        place = lambda n, i: (jnp.where(n == g, i, jnp.where(n < g, 0, steps - 1)), 0)
        return pl.BlockSpec((rows, 2 * C), place)

    columns = pl.BlockSpec((T, rows), lambda g, i: (0, i))
    return launch(
        functools.partial(weight_body, C, G),
        "weight_grads",
        (G, steps),
        (n1, low, dqkv, mixed),
        [
            columns,
            columns,
            pl.BlockSpec((1, T, 3 * C), lambda g, i: (g, 0, 0)),
            pl.BlockSpec((1, T, C), lambda g, i: (g, 0, 0)),
        ],
        [jax.ShapeDtypeStruct((D, 2 * C), BF)] * (2 * G),
        [out(g) for g in range(G) for _ in range(2)],
        [],
        cost(8 * T * D * C * G, 2 * G * (2 * T * D + 4 * T * C + 4 * D * C)),
        traffic,
    )


def project_body(x, gain, valid, mixed, wo, hidden, n2, square):
    @pl.when(pl.program_id(0) == 0)
    def _():
        square[...] = jnp.zeros_like(square)

    a = sum(dot(mixed[g], wo[g]) for g in range(wo.shape[0]))
    h = x[...].astype(F32) + a
    hidden[...] = h
    n2[...] = (h * rms(h) * gain[...].astype(F32)).astype(BF)
    square[...] += row_sum(valid[...] * a * a)


def project(x, gain, valid, mixed, wo):
    T, D = x.shape
    G, C, _ = wo.shape
    tt = pick(T, 256, 128)
    tile = lambda c: pl.BlockSpec((tt, c), lambda i: (i, 0))
    out, _ = launch(
        lambda hook, *refs: project_body(*refs),
        "project",
        (T // tt,),
        (x, gain, valid, mixed, wo),
        [tile(D), whole((1, D)), tile(1), pl.BlockSpec((G, tt, C), lambda i: (0, i, 0)), whole(wo.shape)],
        [jax.ShapeDtypeStruct((T, D), F32), jax.ShapeDtypeStruct((T, D), BF), jax.ShapeDtypeStruct((1, D), F32)],
        [tile(D), tile(D), pl.BlockSpec((1, D), lambda i: (0, 0))],
        [],
        cost(2 * T * D * D, 12 * T * D),
    )
    return out


def feed_body(
    hook, n2, g, hba, hbb, upa, upb, downa, downb, feed, n2g, dua, dub, dda, ddb, ba, bb, acc_f, acc_n, act, pg, wu, wd
):
    step = pl.program_id(0)
    T, D = n2.shape
    ft = hba.shape[1]
    chunk = pick(T, 768, 384, 128)
    hook("start")

    @pl.when(step == 0)
    def _():
        acc_f[...] = jnp.zeros_like(acc_f)
        acc_n[...] = jnp.zeros_like(acc_n)

    wu[:, :ft], wu[:, ft:] = upa[...], upb[...]
    wd[:ft, :], wd[ft:, :] = downa[...], downb[...]
    hb = jnp.concatenate([hba[...], hbb[...]], axis=1).astype(F32)
    ba[...] = jnp.zeros_like(ba)
    bb[...] = jnp.zeros_like(bb)

    def one(i, _):
        s = pl.ds(pl.multiple_of(i * chunk, chunk), chunk)
        p = dot(n2[s, :], wu[...]) + hb
        ag = dot(g[s, :], wd[...], NT)
        sg = 0.5 * jnp.tanh(0.5 * p) + 0.5
        ps = p * sg
        a = ps.astype(BF)
        q = (ag * (sg + ps * (1.0 - sg))).astype(BF)
        act[s, :] = a
        pg[s, :] = q
        b = row_sum(q.astype(F32))
        ba[...] += b[:, :ft]
        bb[...] += b[:, ft:]
        acc_f[s, :] += dot(a, wd[...])
        acc_n[s, :] += dot(q, wu[...], NT)
        return 0

    lax.fori_loop(0, T // chunk, one, 0)
    hook("middle")
    u = dot(n2[...], pg[...], TN).astype(BF)
    dua[...], dub[...] = u[:, :ft], u[:, ft:]
    d = dot(act[...], g[...], TN).astype(BF)
    dda[...], ddb[...] = d[:ft], d[ft:]

    @pl.when(step == pl.num_programs(0) - 1)
    def _():
        feed[...] = acc_f[...].astype(BF)
        n2g[...] = acc_n[...].astype(BF)

    hook("end")


def feed_forward(n2, g, biases, ups, downs, traffic=None):
    T, D = n2.shape
    F = biases[0].shape[1]
    ft = pick(F, 256)
    up = pl.BlockSpec((D, ft), lambda f: (0, f))
    down = pl.BlockSpec((ft, D), lambda f: (f, 0))
    bias = pl.BlockSpec((1, ft), lambda f: (0, f))
    return launch(
        feed_body,
        "feed_forward",
        (F // ft,),
        (n2, g, *biases, *ups, *downs),
        [whole((T, D)), whole((T, D)), bias, bias, up, up, down, down],
        [jax.ShapeDtypeStruct((T, D), BF)] * 2
        + [jax.ShapeDtypeStruct((D, F), BF)] * 2
        + [jax.ShapeDtypeStruct((F, D), BF)] * 2
        + [jax.ShapeDtypeStruct((1, F), F32)] * 2,
        [whole((T, D)), whole((T, D)), up, up, down, down, bias, bias],
        [
            pltpu.VMEM((T, D), F32),
            pltpu.VMEM((T, D), F32),
            pltpu.VMEM((T, 2 * ft), BF),
            pltpu.VMEM((T, 2 * ft), BF),
            pltpu.VMEM((D, 2 * ft), BF),
            pltpu.VMEM((2 * ft, D), BF),
        ],
        cost(24 * T * D * F, 16 * T * D + 16 * D * F, 2 * T * F),
        traffic,
    )


def middle_body(n, hook, *refs):
    hook("start")
    hidden, g, gain, out_bias, valid = refs[:5]
    feeds, grads = refs[5 : 5 + n], refs[5 + n : 5 + 2 * n]
    out, low, sums = refs[5 + 2 * n :]

    @pl.when(pl.program_id(0) == 0)
    def _():
        sums[...] = jnp.zeros_like(sums)

    h, go = hidden[...], g[...].astype(F32)
    f = sum(a[...].astype(F32) for a in feeds) + out_bias[...].astype(F32)
    ng = sum(a[...].astype(F32) for a in grads)
    result = h + f
    out[...] = result.astype(BF)
    r2 = rms(h)
    wg = ng * gain[...].astype(F32)
    inner = jnp.sum(wg * h, axis=1, keepdims=True)
    low[...] = (go + wg * r2 - h * (r2 * r2 * r2 * inner / h.shape[1])).astype(BF)
    v = valid[...]
    for i, a in enumerate((ng * h * r2, go, v * f * f, v * result * result)):
        sums[i : i + 1, :] += row_sum(a)
    hook("end")


def middle(hidden, g, gain, out_bias, valid, feeds, grads, traffic=None):
    T, D = hidden.shape
    tt = pick(T, 256, 128)
    tile = lambda c: pl.BlockSpec((tt, c), lambda i: (i, 0))
    n = len(feeds)
    return launch(
        functools.partial(middle_body, n),
        "middle",
        (T // tt,),
        (hidden, g, gain, out_bias, valid, *feeds, *grads),
        [tile(D), tile(D), whole((1, D)), whole((1, D)), tile(1)] + [tile(D)] * (2 * n),
        [jax.ShapeDtypeStruct((T, D), BF), jax.ShapeDtypeStruct((T, D), BF), jax.ShapeDtypeStruct((8, D), F32)],
        [tile(D), tile(D), pl.BlockSpec((8, D), lambda i: (0, 0))],
        [],
        cost(40 * T * D, (10 + 4 * n) * T * D),
        traffic,
    )


def last_body(traffic, hook, x, gain, low, dqkv, w, out, part, summed=None):
    hook("start")

    @pl.when(pl.program_id(0) == 0)
    def _():
        part[...] = jnp.zeros_like(part)

    ng = sum(dot(dqkv[g], w[g], NT) for g in range(w.shape[0]))
    t = x[...].astype(F32)
    r1 = rms(t)
    wg = ng * gain[...].astype(F32)
    inner = jnp.sum(wg * t, axis=1, keepdims=True)
    out[...] = low[...].astype(F32) + wg * r1 - t * (r1 * r1 * r1 * inner / t.shape[1])
    part[...] += row_sum(ng * t * r1)
    if traffic is not None:
        traffic.refs["part"], traffic.refs["summed"] = part, summed
    hook("end")


def last(x, gain, low, dqkv, w, traffic=None, small=None):
    T, D = x.shape
    G, _, K = w.shape
    rows = [] if small is None else [small]
    tt = pick(T, 256, 128)
    tile = lambda c: pl.BlockSpec((tt, c), lambda i: (i, 0))
    return launch(
        functools.partial(last_body, traffic),
        "last",
        (T // tt,),
        (x, gain, low, dqkv, w),
        [tile(D), whole((1, D)), tile(D), pl.BlockSpec((G, tt, K), lambda i: (0, i, 0)), whole(w.shape)],
        [jax.ShapeDtypeStruct((n, D), F32) for n in (T, 1, *rows)],
        [tile(D), *[pl.BlockSpec((n, D), lambda i: (0, 0)) for n in (1, *rows)]],
        [],
        cost(6 * T * D * D, 8 * T * D + 6 * D * D),
        traffic,
    )


def finish_body(h, joined, up, down, q, k, v, o, up_out, down_out):
    j = joined[...].astype(F32).T
    for i, ref in enumerate((q, k, v, o)):
        ref[...] = j[i * h : (i + 1) * h]
    up_out[...] = up[...].astype(F32)
    down_out[...] = down[...].astype(F32)


def finish(joined, up, down):
    D, F = up.shape
    h = joined.shape[1] // 4
    rows = pick(D, 256)
    steps = D // rows
    tile = lambda n, c: pl.BlockSpec((n // steps, c), lambda i: (i, 0))
    ups = [tile(D, F), tile(F, D)]
    out, _ = launch(
        lambda hook, *refs: finish_body(h, *refs),
        "finish",
        (steps,),
        (joined, up, down),
        [tile(D, 4 * h), *ups],
        [jax.ShapeDtypeStruct((h, D), F32)] * 4 + [jax.ShapeDtypeStruct(a.shape, F32) for a in (up, down)],
        [pl.BlockSpec((h, rows), lambda i: (0, i))] * 4 + ups,
        [],
        cost(D * D, 6 * (4 * h * D + 2 * D * F)),
    )
    return out


def swap(a, axis, bit):
    return lax.ppermute(a, axis, [(i, i ^ bit) for i in range(lax.axis_size(axis))])


def segments(lengths):
    slots = lengths.shape[1]
    upto = lax.broadcasted_iota(jnp.int32, (1, slots, slots), 2) <= lax.broadcasted_iota(
        jnp.int32, (1, slots, slots), 1
    )
    ends = jnp.sum(jnp.where(upto, lengths[:, None, :], 0), axis=2)
    places = lax.broadcasted_iota(jnp.int32, (lengths.shape[0], L, slots), 1)
    return jnp.sum((ends[:, None, :] <= places).astype(jnp.int32), axis=2)


def merge(*dicts):
    return {k: v for d in dicts for k, v in d.items()}


def fused(x, cotangent, weights, gains, out_bias, valid, ids, mp):
    T, D = x.shape
    joined, wo, up, down, bias = weights
    h = wo.shape[0]
    hidden_units = up.shape[1]
    near, far, deep = ("dp", 1), ("dp", 2), ("dp", 4)

    J, W = Gather("j", D, 3 * h), Gather("w", h, D)
    U, V = Gather("u", D, hidden_units), Gather("v", hidden_units, D)
    both, four = (J, W), (J, W, U, V)
    steps = T // pick(T, 512, 384, 256, 128)
    t = Traffic(
        1,
        [CORE, Y, near, far],
        dict(j=joined, w=wo, u=up, v=down),
        merge(*[g.buffers("s", "q", "o", "p") for g in both], *[g.buffers("s", "q") for g in (U, V)]),
    )
    t.on(0, "start", *[g.start(s) for s in "sy" for g in both], J.wait("s"))
    t.on(1, "start", *[g.wait("y") for g in both], *[g.start("a") for g in both])
    t.on(1, "start", *[g.start(s) for s in "ys" for g in (U, V)])
    t.on(steps, "start", *[g.wait("a") for g in both], *[g.start("b") for g in both])
    t.on(steps, "start", *[g.wait("b") for g in both], *[g.start("p") for g in both], J.wait("p"))
    t.on(2 * steps - 1, "end", W.wait("s"), W.wait("p"), *[g.wait(s) for s in "ys" for g in (U, V)])
    (qkv, mixed, w, n1), got = attend(x, gains[0], *ids, h, [("j", "js"), ("jo", "jp")], t)
    wo_all = jnp.stack([jnp.concatenate([wo, got["ws"]]), jnp.concatenate([got["wo"], got["wp"]])])
    hidden, n2, att_square = project(x, gains[1], valid, mixed, wo_all)

    bias_o = swap(bias, "mp", 2)
    t = Traffic(
        2,
        [CORE, near, far],
        dict(uq=got["uq"], vq=got["vq"], u=up, v=down),
        merge(*[g.buffers("o", "p") for g in (U, V)]),
    )
    fs = hidden_units // pick(hidden_units, 256)
    t.on(0, "start", *[g.start("a") for g in (U, V)])
    t.on(2, "middle", *[g.wait("a") for g in (U, V)], *[g.start("b") for g in (U, V)])
    t.on(3, "middle", *[g.wait("b") for g in (U, V)], *[g.start("p") for g in (U, V)])
    t.on(fs - 1, "end", *[g.wait("p") for g in (U, V)])
    own, far_weights = feed_forward(
        n2, cotangent, (bias, swap(bias, "mp", 1)), (up, got["us"]), (down, got["vs"]), t
    )

    a, b = (1, 2, 4), (2, 1, 4)
    U0, D0 = (
        Stream("u0", "u0a", "u0b", D, hidden_units, a, 2, joins="u1"),
        Stream("d0", "d0a", "d0b", hidden_units, D, b, 2, joins="d1"),
    )
    U1, D1 = Stream("u1", "u1a", "u1b", D, hidden_units, a, 2), Stream("d1", "d1a", "d1b", hidden_units, D, b, 2)
    half = D // 2
    att = [
        [
            Near(f"j{n}{m}", f"j{n}a", f"j{n}b", half, 4 * h, (a, b)[m], 1, m * half, None if n else f"j1{m}")
            for m in range(2)
        ]
        for n in range(2)
    ]
    first = (U0, D0)
    second = (U1, D1)
    t = Traffic(
        3,
        [CORE, near, far],
        dict(u0a=own[2], u0b=own[3], d0a=own[4], d0b=own[5]),
        merge(*[s.buffers("c", "s0", "r0", "s1", "r1") for s in first]),
    )
    t.on(0, "start", *[s.start_core for s in first])
    t.on(0, "middle", *[s.wait_core for s in first], *[s.start(0) for s in first])
    t.on(3, "start", *[s.wait(0) for s in first], *[s.start(1) for s in first])
    t.on(fs - 1, "end", *[s.wait(1) for s in first])
    other, left = feed_forward(
        n2,
        cotangent,
        (bias_o, swap(bias_o, "mp", 1)),
        (far_weights["uo"], far_weights["up"]),
        (far_weights["vo"], far_weights["vp"]),
        t,
    )
    feeds = [own, other]
    t = Traffic(
        7,
        [CORE],
        dict(u1b=other[3], d1b=other[5]),
        merge(*[s.buffers("c") for s in second]),
    )
    ls = T // pick(T, 256, 128)
    t.on(0, "start", *[s.start_core for s in second]).on(ls - 1, "end", *[s.wait_core for s in second])
    (out, low, sums), cores = middle(
        hidden, cotangent, gains[1], out_bias, valid, [f[0] for f in feeds], [f[1] for f in feeds], t
    )

    held = dict(u1a=other[2], d1a=other[4]) | cores
    t = Traffic(4, [near, far], held, merge(*[s.buffers("s0", "r0", "s1", "r1") for s in second]))
    t.on(0, "start", *[s.start(0) for s in second])
    t.on(2 * steps - 2, "start", *[s.wait(0) for s in second], *[s.start(1) for s in second])
    t.on(2 * steps - 1, "end", *[s.wait(1) for s in second])
    (dqkv,), arrived = attend_back(low, wo_all, qkv, *ids, t)

    t = Traffic(
        5, [Y], held | {k: v for k, v in arrived.items() if k[2] == "r"}, merge(*[s.buffers("e", "y") for s in second])
    )
    ws = D // pick(D, 256)
    t.on(0, "start", *[f for s in second for f in (s.keep, s.start_cross)])
    t.on(2 * ws - 1, "end", *[s.wait_cross for s in second])
    dw, crossed = weight_grads(n1, low, dqkv, mixed, t)

    units = jnp.zeros((1, lax.axis_size("mp") * hidden_units), F32)
    for change, part in ((0, own[6]), (1, own[7]), (2, other[6]), (3, other[7])):
        units = lax.dynamic_update_slice(units, part, (0, (mp ^ change) * hidden_units))
    count = jnp.where(jnp.arange(D) == 0, jnp.sum(valid), 0.0)[None]
    rows = jnp.concatenate([units.reshape(-1, D), sums[:4], att_square, count])
    n_rows = rows.shape[0] + 1
    tall = (n_rows + 7) // 8 * 8
    small = jnp.pad(rows, ((1, tall - n_rows), (0, 0)))

    held = dict(j0a=dw[0], j0b=dw[1], j1a=dw[2], j1b=dw[3], u1y=crossed["u1y"], d1y=crossed["d1y"], small=small)
    held |= dict(u0a=own[2], d0a=own[4]) | {k: v for k, v in left.items() if k[2] in "cr"}
    flat = [s for pair in att for s in pair]
    bits = [CORE, Y, near, far, deep]
    t = Traffic(
        6,
        bits,
        held,
        merge(*[s.buffers("s2", "r2", "f") for s in first], dict(joined=(D, 4 * h))),
        merge(
            *[s.scratch("m", "c", "s0", "r0") for s in flat],
            *[s.scratch("s1", "r1", "s2", "r2", "f") for s in att[0]],
            *[s.scratch("e", "y") for s in att[1]],
            {f"t{n}": pltpu.VMEM((tall, D), F32) for n in range(2 * len(bits) + 1)},
        ),
    )

    def load_small(t):
        return t.local("small", t.refs["small"], t.refs["t0"])

    def first_small(t):
        load_small(t).wait()
        t.refs["t0"][0:1, :] = t.refs["part"][...]

    def exchange_small(t, n):
        return t.copy(f"t{n}", t.refs[f"t{2 * n}"], t.refs[f"t{2 * n + 1}"], bits[n])

    def store_small(t):
        t.refs["summed"][...] = t.refs[f"t{2 * len(bits)}"][...]

    def start_small(n):
        return lambda t: exchange_small(t, n).start()

    def end_small(n):
        def action(t):
            exchange_small(t, n).wait()
            t.refs[f"t{2 * n + 2}"][...] = t.refs[f"t{2 * n}"][...] + t.refs[f"t{2 * n + 1}"][...]

        return action

    t.on(0, "start", *[s.start_core for s in flat], *[s.start_load for s in flat])
    t.on(0, "start", lambda t: load_small(t).start(), *[s.start(2) for s in first])
    t.on(1, "start", *[s.wait_load for s in flat], *[s.wait_core for s in flat], *[s.start(0) for s in flat])
    end = [first_small, start_small(0)]
    end += [f for s in first for f in (s.wait(2), s.total, s.start_spread(2))]
    end += [end_small(0), start_small(1)]
    end += [f for s in att[1] for f in (s.wait(0), s.keep, s.start_cross)] + [s.wait(0) for s in att[0]]
    end += [end_small(1), start_small(2)]
    end += [f for s in first for f in (s.wait_spread(2), s.start_spread(1))]
    end += [s.wait_cross for s in att[1]] + [s.start(1) for s in att[0]]
    end += [end_small(2), start_small(3)]
    end += [f for s in att[0] for f in (s.wait(1), s.start(2))]
    end += [f for s in first for f in (s.wait_spread(1), s.start_spread(0))]
    end += [f for s in att[0] for f in (s.wait(2), s.total, s.start_spread(2))]
    end += [end_small(3), start_small(4)]
    for j in (2, 1):
        end += [f for s in att[0] for f in (s.wait_spread(j), s.start_spread(j - 1))]
    end += [end_small(4), store_small]
    end += [f for s in att[0] for f in (s.wait_spread(0), s.start_store)]
    end += [s.wait_spread(0) for s in first] + [s.wait_store for s in att[0]]
    t.on(ls - 1, "end", *end)
    (input_gradient, _, summed), done = last(x, gains[0], low, dqkv, w, t, tall)
    return (out, input_gradient, done["joined"], done["u0f"], done["d0f"]), summed


def gathered(x, cotangent, weights, gains, out_bias, valid, ids):
    D = x.shape[1]
    joined, wo, up, down, bias = weights
    every = lambda a, d: lax.all_gather(a, "mp", axis=d, tiled=True)
    two = lambda a, d: tuple(jnp.split(every(a, d), 2, axis=d))
    sides = [jnp.concatenate(p, axis=1) for p in zip(*(two(a, 1) for a in jnp.split(joined, 3, axis=1)))]
    plain = Traffic(0, [], dict(a=sides[0], b=sides[1]), {})
    (qkv, mixed, w, n1), _ = attend(x, gains[0], *ids, sides[0].shape[1] // 3, [("a", "b")], plain)
    wo_all = every(wo, 0)[None]
    hidden, n2, att_square = project(x, gains[1], valid, mixed, wo_all)
    f, _ = feed_forward(n2, cotangent, two(bias, 1), two(up, 1), two(down, 0))
    (out, low, sums), _ = middle(hidden, cotangent, gains[1], out_bias, valid, [f[0]], [f[1]])
    (dqkv,), _ = attend_back(low, wo_all, qkv, *ids, None)
    dw, _ = weight_grads(n1, low, dqkv, mixed, None)
    (input_gradient, first_part), _ = last(x, gains[0], low, dqkv, w)

    def total(pair, d):
        part = lax.psum_scatter(jnp.concatenate(pair, axis=d), "mp", scatter_dimension=d, tiled=True)
        return lax.psum(part, "dp")

    cut = [jnp.split(a, 4, axis=1) for a in dw]
    joined_total = jnp.concatenate([total(pair, 1) for pair in zip(*cut)], axis=1)
    grads = (out, input_gradient, joined_total, total(f[2:4], 1), total(f[4:6], 0))
    units = jnp.concatenate(f[6:], axis=1).reshape(-1, D)
    count = jnp.where(jnp.arange(D) == 0, jnp.sum(valid), 0.0)[None]
    return grads, lax.psum(jnp.concatenate([first_part, units, sums[:4], att_square, count]), ("dp", "mp"))


def per_device(
    tokens,
    lengths,
    cotangent,
    query_weight,
    key_weight,
    value_weight,
    out_weight,
    up_weight,
    hidden_bias,
    down_weight,
    output_bias,
    first_gain,
    second_gain,
):
    T, D = tokens.shape
    rows = T // L
    mp = lax.axis_index("mp")
    segment_ids = segments(lax.dynamic_slice_in_dim(lengths, mp * rows, rows))
    valid = (segment_ids < SLOTS).reshape(-1, 1).astype(F32)
    ids = (segment_ids + L * lax.broadcasted_iota(jnp.int32, (rows, L), 0)).reshape(-1)
    ids = (ids[:, None], ids[None, :])
    joined = jnp.concatenate([query_weight, key_weight, value_weight], axis=1)
    bias = hidden_bias.reshape(1, -1)
    gains = (first_gain.reshape(1, -1), second_gain.reshape(1, -1))
    weights = (joined, out_weight, up_weight, down_weight, bias)
    rest = (gains, output_bias.reshape(1, -1), valid, ids)
    if lax.axis_size("mp") == 4 and lax.axis_size("dp") == 8:
        grads, small = fused(tokens, cotangent, weights, *rest, mp)
    else:
        grads, small = gathered(tokens, cotangent, weights, *rest)
    out, input_gradient, joined_total, up_total, down_total = grads
    n = hidden_bias.shape[0] * lax.axis_size("mp") // D + 1
    squares = jnp.sum(small[n + 2 : n + 6], axis=1)
    mean = lambda i: jnp.sqrt(squares[i] / (squares[3] * D))
    q, k, v, o, up_total, down_total = finish(joined_total, up_total, down_total)
    return (
        out,
        input_gradient,
        q.T,
        k.T,
        v.T,
        o,
        up_total,
        lax.dynamic_slice_in_dim(small[1:n].reshape(-1), mp * bias.shape[1], bias.shape[1]),
        down_total,
        small[n + 1],
        small[0],
        small[n],
        jnp.stack([mean(2), mean(0), mean(1)]),
    )


def solution(mesh):
    return jax.shard_map(
        per_device,
        mesh=mesh,
        in_specs=(
            P(("dp", "mp"), None),
            P("dp", None),
            P(("dp", "mp"), None),
            P(None, "mp"),
            P(None, "mp"),
            P(None, "mp"),
            P("mp", None),
            P(None, "mp"),
            P("mp"),
            P("mp", None),
            P(),
            P(),
            P(),
        ),
        out_specs=(
            P(("dp", "mp"), None),
            P(("dp", "mp"), None),
            P(None, "mp"),
            P(None, "mp"),
            P(None, "mp"),
            P("mp", None),
            P(None, "mp"),
            P("mp"),
            P("mp", None),
            P(),
            P(),
            P(),
            P(),
        ),
        check_vma=False,
    )
```

```python
import functools
import math

import jax
import jax.numpy as jnp
from jax import lax
from jax.experimental import pallas as pl
from jax.experimental.pallas import tpu as pltpu
from jax.sharding import PartitionSpec as P

HD = 80
L = 64
SLOTS = 32
LANES = 128
EPSILON = 1e-06
MASKED = -1e30
F32 = jnp.float32
BF = jnp.bfloat16
NN = (((1,), (0,)), ((), ()))
NT = (((1,), (1,)), ((), ()))
TN = (((0,), (0,)), ((), ()))
VMEM_BYTES = 60 << 20


def dot(a, b, dims=NN):
    return lax.dot_general(a, b, dims, preferred_element_type=F32)


def pick(n, *sizes):
    return next((s for s in sizes if n % s == 0), n)


def whole(shape):
    return pl.BlockSpec(shape, lambda *i: (0,) * len(shape), pipeline_mode=pl.Buffered(1))


def cost(flops, nbytes, exps=0):
    return pl.CostEstimate(flops=int(flops), bytes_accessed=int(nbytes), transcendentals=int(exps))


def row_sum(x):
    return jnp.sum(x, axis=0, keepdims=True)


def rms(x):
    return lax.rsqrt(jnp.mean(x * x, axis=1, keepdims=True) + EPSILON)


MESH = pl.DeviceIdType.MESH
CORE, Y = ("mp", 1), ("mp", 2)


def bit_of(axis, bit):
    return lax.rem(lax.axis_index(axis) // bit, 2)


def flip(axis, bit):
    return {axis: lax.axis_index(axis) + bit - 2 * bit * bit_of(axis, bit)}


class Traffic:
    def __init__(self, number, partners, arrays, buffers, scratch=None):
        self.number, self.partners = number, partners
        self.arrays, self.buffers, self.scratch = arrays, buffers, scratch or {}
        self.events, self.slots, self.refs = [], {}, {}

    def on(self, step, place, *actions):
        self.events += [(step, place, f) for f in actions]
        return self

    def run(self, step, place):
        for at, where, action in self.events:
            if where == place:
                pl.when(step == at)(functools.partial(action, self))

    def greet(self):
        sem = pltpu.get_barrier_semaphore()
        for p in self.partners:
            pl.semaphore_signal(sem, inc=1, device_id=flip(*p), device_id_type=MESH)
        pl.semaphore_wait(sem, len(self.partners))

    def copy(self, name, src, dst, to):
        i = self.slots.setdefault(name, len(self.slots))
        return pltpu.make_async_remote_copy(
            src_ref=src,
            dst_ref=dst,
            send_sem=self.sems.at[0, i],
            recv_sem=self.sems.at[1, i],
            device_id=flip(*to),
            device_id_type=MESH,
        )

    def local(self, name, src, dst):
        i = self.slots.setdefault(name, len(self.slots))
        return pltpu.make_async_copy(src, dst, self.sems.at[0, i])


COPIES = 48


def launch(body, name, grid, args, in_specs, outs, out_specs, scratch, cost_estimate, traffic=None):
    n_args, n_outs = len(args), len(outs)
    names, arrays, buffers = [], [], []
    if traffic is not None:
        names = [*traffic.arrays, *traffic.buffers]
        arrays = list(traffic.arrays.values())
        buffers = [jax.ShapeDtypeStruct(s, BF) for s in traffic.buffers.values()]
        names += [*traffic.scratch]
        scratch = [*scratch, *traffic.scratch.values(), pltpu.SemaphoreType.DMA((2, COPIES))]

    def kernel(*refs):
        hook = lambda place: None
        inputs, refs = refs[:n_args], refs[n_args:]
        moved, refs = refs[: len(arrays)], refs[len(arrays) :]
        results, refs = refs[:n_outs], refs[n_outs:]
        landing, refs = refs[: len(buffers)], refs[len(buffers) :]
        if traffic is not None:
            step = pl.program_id(0)
            for d in range(1, len(grid)):
                step = step * grid[d] + pl.program_id(d)
            traffic.sems, refs = refs[-1], refs[:-1]
            n = len(refs) - len(traffic.scratch)
            traffic.refs = dict(zip(names, [*moved, *landing, *refs[n:]]))
            refs = refs[:n]
            if traffic.partners:
                pl.when(step == 0)(traffic.greet)
            hook = lambda place: traffic.run(step, place)
        body(hook, *inputs, *results, *refs)

    anywhere = pl.BlockSpec(memory_space=pl.ANY)
    out = pl.pallas_call(
        kernel,
        grid=grid,
        in_specs=[*in_specs, *[anywhere] * len(arrays)],
        out_specs=[*out_specs, *[anywhere] * len(buffers)],
        out_shape=[*outs, *buffers],
        scratch_shapes=scratch,
        compiler_params=pltpu.CompilerParams(
            vmem_limit_bytes=VMEM_BYTES,
            **({} if traffic is None or not traffic.partners else dict(collective_id=traffic.number, has_side_effects=True)),
        ),
        cost_estimate=cost_estimate,
        name=name,
    )(*args, *arrays)
    return out[:n_outs], dict(zip(names[len(arrays) : len(arrays) + len(buffers)], out[n_outs:]))


def add_rows(sources, target, rows):
    columns = target.shape[1]
    tile = pl.BlockSpec((rows // 2 if rows // 2 % 16 == 0 else rows, columns), lambda i: (i, 0))

    def body(*refs):
        refs[-1][...] = sum(r[...].astype(F32) for r in refs[:-1]).astype(BF)

    pltpu.emit_pipeline(
        body, grid=(rows // tile.block_shape[0],), in_specs=[tile] * len(sources), out_specs=[tile]
    )(*[r.at[pl.ds(pl.multiple_of(o, 16), rows), :] for r, o in sources], target)


class Stream:
    def __init__(self, tag, mine, theirs, rows, columns, order, cut, base=0, joins=None):
        self.tag, self.mine, self.theirs, self.base = tag, mine, theirs, base
        self.rows, self.columns, self.order = rows, columns, order
        self.cut, self.joins = cut, joins

    def name(self, what):
        return self.tag + what

    def buffers(self, *what):
        size = lambda w: self.rows if w[0] in "cf" else self.rows >> self.cut if w[0] in "ey" else self.rows >> (int(w[1]) + 1)
        return {self.name(w): (size(w), self.columns) for w in what}

    def place(self, stages):
        first, n = 0, self.rows
        for bit in self.order[:stages]:
            n //= 2
            first = first + bit_of("dp", bit) * n
        return first, n

    def sources(self, t, first, arrived):
        out = [(t.refs[self.mine], first + self.base), (t.refs[self.name("c")], first)]
        for j in range(arrived):
            out.append((t.refs[self.name(f"r{j}")], first - self.place(j + 1)[0]))
        if self.joins is not None and arrived >= self.cut:
            out.append((t.refs[self.joins + "y"], first - self.place(self.cut)[0]))
        return out

    def core(self, t):
        src = t.refs[self.theirs].at[pl.ds(self.base, self.rows), :]
        return t.copy(self.name("c"), src, t.refs[self.name("c")], CORE)

    def start_core(self, t):
        self.core(t).start()

    def wait_core(self, t):
        self.core(t).wait()

    def exchange(self, t, j):
        return t.copy(self.name(f"r{j}"), t.refs[self.name(f"s{j}")], t.refs[self.name(f"r{j}")], ("dp", self.order[j]))

    def start(self, j):
        def action(t):
            first, n = self.place(j)
            n //= 2
            sent = first + (1 - bit_of("dp", self.order[j])) * n
            add_rows(self.sources(t, sent, j), t.refs[self.name(f"s{j}")], n)
            self.exchange(t, j).start()

        return action

    def wait(self, j):
        return lambda t: self.exchange(t, j).wait()

    def keep(self, t):
        first, n = self.place(self.cut)
        add_rows(self.sources(t, first, self.cut), t.refs[self.name("e")], n)

    def cross(self, t):
        return t.copy(self.name("y"), t.refs[self.name("e")], t.refs[self.name("y")], Y)

    def start_cross(self, t):
        self.cross(t).start()

    def wait_cross(self, t):
        self.cross(t).wait()

    def total(self, t):
        first, n = self.place(len(self.order))
        target = t.refs[self.name("f")].at[pl.ds(pl.multiple_of(first, 16), n), :]
        add_rows(self.sources(t, first, len(self.order)), target, n)

    def spread(self, t, j):
        first, n = self.place(j + 1)
        part = t.refs[self.name("f")].at[pl.ds(pl.multiple_of(first, 16), n), :]
        return t.copy(self.name(f"f{j}"), part, part, ("dp", self.order[j]))

    def start_spread(self, j):
        return lambda t: self.spread(t, j).start()

    def wait_spread(self, j):
        return lambda t: self.spread(t, j).wait()


def sum_rows(sources, target, rows):
    step = pick(rows, 80, 64, 32, 16)

    def one(i, _):
        part = lambda o: pl.ds(pl.multiple_of(o + i * step, 16), step)
        target[part(0), :] = sum(r[part(o), :].astype(F32) for r, o in sources).astype(BF)
        return 0

    lax.fori_loop(0, rows // step, one, 0)


class Near(Stream):
    def scratch(self, *what):
        size = lambda w: self.rows if w == "m" else self.buffers(w)[self.name(w)][0]
        return {self.name(w): pltpu.VMEM((size(w), self.columns), BF) for w in what}

    def sources(self, t, first, arrived):
        out = super().sources(t, first, arrived)
        return [(t.refs[self.name("m")], first), *out[1:]]

    def load(self, t):
        src = t.refs[self.mine].at[pl.ds(self.base, self.rows), :]
        return t.local(self.name("m"), src, t.refs[self.name("m")])

    def start_load(self, t):
        self.load(t).start()

    def wait_load(self, t):
        self.load(t).wait()

    def start(self, j):
        def action(t):
            first, n = self.place(j)
            n //= 2
            sent = first + (1 - bit_of("dp", self.order[j])) * n
            sum_rows(self.sources(t, sent, j), t.refs[self.name(f"s{j}")], n)
            self.exchange(t, j).start()

        return action

    def keep(self, t):
        first, n = self.place(self.cut)
        sum_rows(self.sources(t, first, self.cut), t.refs[self.name("e")], n)

    def total(self, t):
        first, n = self.place(len(self.order))
        target = t.refs[self.name("f")].at[pl.ds(pl.multiple_of(first, 16), n), :]
        sum_rows(self.sources(t, first, len(self.order)), target, n)

    def store(self, t):
        out = t.refs["joined"].at[pl.ds(self.base, self.rows), :]
        return t.local(self.name("o"), t.refs[self.name("f")], out)

    def start_store(self, t):
        self.store(t).start()

    def wait_store(self, t):
        self.store(t).wait()


class Gather:
    def __init__(self, tag, rows, columns):
        self.tag, self.rows, self.columns = tag, rows, columns
        self.n = rows // 4

    def buffers(self, *what):
        return {self.tag + w: (self.n if w == "q" else self.rows, self.columns) for w in what}

    def quarter(self, ref, flip_x=0, flip_z=0, first=0, rows=None):
        x, z = bit_of("dp", 1), bit_of("dp", 2)
        x, z = (1 - x if flip_x else x), (1 - z if flip_z else z)
        start = pl.multiple_of((2 * z + x) * self.n + first, 16)
        return ref.at[pl.ds(start, self.n if rows is None else rows), :]

    def copies(self, t, step):
        own, o = t.refs[self.tag], t.refs.get(self.tag + "o")
        name = self.tag + step
        if step == "s":
            return [t.copy(name, own, t.refs[name], CORE)]
        if step == "y":
            return [t.copy(name, self.quarter(own), t.refs[self.tag + "q"], Y)]
        if step == "a":
            q = t.refs[self.tag + "q"]
            return [t.copy(name + str(b), q, self.quarter(o), ("dp", b)) for b in (1, 2)]
        if step == "b":
            top = (self.n // 2 + 15) // 16 * 16
            to_x = self.quarter(o, flip_z=1, rows=top)
            to_z = self.quarter(o, flip_x=1, first=top, rows=self.n - top)
            return [t.copy(name + "1", to_x, to_x, ("dp", 1)), t.copy(name + "2", to_z, to_z, ("dp", 2))]
        return [t.copy(name, o, t.refs[self.tag + "p"], CORE)]

    def start(self, step):
        def action(t):
            for c in self.copies(t, step):
                c.start()
            if step == "a":
                add_rows([(t.refs[self.tag + "q"], 0)], self.quarter(t.refs[self.tag + "o"]), self.n)

        return action

    def wait(self, step):
        def action(t):
            for c in self.copies(t, step):
                c.wait()

        return action


def windows(C):
    out = []
    for h in range(C // HD):
        w = min(LANES * (HD * h // LANES), C - 2 * LANES)
        out.append((w, HD * h - w))
    return out


def head_masks(C):
    lane = lax.broadcasted_iota(jnp.int32, (1, 2 * LANES), 1)
    return [jnp.where((lane >= lo) & (lane < lo + HD), 1.0, 0.0).astype(BF) for _, lo in windows(C)]


def softmaxes(qs, ks, allowed):
    s = [jnp.where(allowed, dot(q, k, NT) * (1.0 / math.sqrt(HD)), MASKED) for q, k in zip(qs, ks)]
    e = [jnp.exp(x - jnp.max(x, axis=1, keepdims=True)) for x in s]
    return [x * (1.0 / jnp.sum(x, axis=1, keepdims=True)) for x in e]


def allow(idc, idr, s, B):
    causal = lax.broadcasted_iota(jnp.int32, (B, B), 1) <= lax.broadcasted_iota(
        jnp.int32, (B, B), 0
    )
    return (idc[s, :] == idr[:, s]) & causal


def put(tiles, w, val):
    for n in range(2):
        t = w // LANES + n
        part = val[:, n * LANES : (n + 1) * LANES]
        tiles[t] = part if tiles[t] is None else tiles[t] + part


def fwd_body(B, C, pairs, traffic, hook, x, gain, idc, idr, qkv, mixed, w, n1, ab, sem):
    group = pl.program_id(0)
    tt = x.shape[0]
    first = pl.program_id(1) == 0
    hook("start")
    h = C // 2
    for g, pair in enumerate(pairs):

        @pl.when(first & (group == g))
        def _():
            for side in range(2):
                c = pltpu.make_async_copy(traffic.refs[pair[side]], ab, sem)
                c.start()
                c.wait()
                a = ab[...]
                for i in range(3):
                    w[0, :, i * C + side * h : i * C + (side + 1) * h] = a[:, i * h : (i + 1) * h]

    t = x[...].astype(F32)
    normed = (t * rms(t) * gain[...].astype(F32)).astype(BF)

    @pl.when(group == 0)
    def _():
        n1[...] = normed

    qkv[0] = dot(normed, w[0]).astype(BF)
    hook("middle")
    masks = head_masks(C)
    wins = [w0 for w0, _ in windows(C)]

    def block(i, _):
        s = pl.ds(pl.multiple_of(i * B, B), B)
        ok = allow(idc, idr, s, B)
        tiles = [None] * (C // LANES)
        cut = lambda n, w0: qkv[0, s, n * C + w0 : n * C + w0 + 2 * LANES]
        for g in range(0, len(wins), 8):
            hs = range(g, min(g + 8, len(wins)))
            p = softmaxes([cut(0, wins[h]) * masks[h] for h in hs], [cut(1, wins[h]) for h in hs], ok)
            o = [dot(a.astype(BF), cut(2, wins[h]) * masks[h]) for a, h in zip(p, hs)]
            for h, a in zip(hs, o):
                put(tiles, wins[h], a)
        mixed[0, s, :] = jnp.concatenate(tiles, axis=1).astype(BF)
        return 0

    lax.fori_loop(0, tt // B, block, 0)
    hook("end")


def attend(x, gain, idc, idr, h, pairs, traffic):
    T, D = x.shape
    C, G = 2 * h, len(pairs)
    tt, B = pick(T, 512, 384, 256, 128), 128
    by_group = lambda c: pl.BlockSpec((1, tt, c), lambda g, i: (g, i, 0))
    return launch(
        functools.partial(fwd_body, B, C, pairs, traffic),
        "attend",
        (G, T // tt),
        (x, gain, idc, idr),
        [
            pl.BlockSpec((tt, D), lambda g, i: (i, 0)),
            whole((1, D)),
            pl.BlockSpec((tt, 1), lambda g, i: (i, 0)),
            pl.BlockSpec((1, tt), lambda g, i: (0, i)),
        ],
        [
            jax.ShapeDtypeStruct((G, T, 3 * C), BF),
            jax.ShapeDtypeStruct((G, T, C), BF),
            jax.ShapeDtypeStruct((G, D, 3 * C), BF),
            jax.ShapeDtypeStruct((T, D), BF),
        ],
        [
            by_group(3 * C),
            by_group(C),
            pl.BlockSpec((1, D, 3 * C), lambda g, i: (g, 0, 0)),
            pl.BlockSpec((tt, D), lambda g, i: (jnp.where(g == 0, i, T // tt - 1), 0)),
        ],
        [pltpu.VMEM((D, 3 * h), BF), pltpu.SemaphoreType.DMA],
        cost(9 * T * D * C * G, 2 * G * (T * D + 4 * C * D + 5 * T * C), G * T * B * C // HD),
        traffic,
    )


def back_body(B, C, hook, hg, wo, qkv, idc, idr, dqkv, dmix):
    tt = hg.shape[0]
    scale = 1.0 / math.sqrt(HD)
    hook("start")
    dmix[...] = dot(hg[...], wo[0], NT).astype(BF)
    masks = head_masks(C)
    wins = [w0 for w0, _ in windows(C)]

    def block(i, _):
        s = pl.ds(pl.multiple_of(i * B, B), B)
        ok = allow(idc, idr, s, B)
        dq = [None] * (C // LANES)
        dk, dv = list(dq), list(dq)
        cut = lambda n, w0: qkv[0, s, n * C + w0 : n * C + w0 + 2 * LANES]
        for g in range(0, len(wins), 8):
            hs = range(g, min(g + 8, len(wins)))
            q = [cut(0, wins[h]) * masks[h] for h in hs]
            gm = [dmix[s, wins[h] : wins[h] + 2 * LANES] * masks[h] for h in hs]
            p = softmaxes(q, [cut(1, wins[h]) for h in hs], ok)
            dp = [dot(a, cut(2, wins[h]), NT) for a, h in zip(gm, hs)]
            ds = [(a * (b - jnp.sum(a * b, axis=1, keepdims=True))).astype(BF) for a, b in zip(p, dp)]
            for h, a, b, c, d in zip(hs, p, gm, ds, q):
                put(dv, wins[h], dot(a.astype(BF), b, TN))
                put(dk, wins[h], dot(c, d, TN))
                put(dq, wins[h], dot(c, cut(1, wins[h]) * masks[h]))
        for n, tiles in enumerate((dq, dk, dv)):
            a = jnp.concatenate(tiles, axis=1)
            dqkv[0, s, n * C : (n + 1) * C] = (a if n == 2 else a * scale).astype(BF)
        return 0

    lax.fori_loop(0, tt // B, block, 0)
    hook("end")


def attend_back(hg, wo, qkv, idc, idr, traffic):
    T, D = hg.shape
    G, C, _ = wo.shape
    tt, B = pick(T, 512, 384, 256, 128), 128
    by_group = pl.BlockSpec((1, tt, 3 * C), lambda g, i: (g, i, 0))
    return launch(
        functools.partial(back_body, B, C),
        "attend_back",
        (G, T // tt),
        (hg, wo, qkv, idc, idr),
        [
            pl.BlockSpec((tt, D), lambda g, i: (i, 0)),
            pl.BlockSpec((1, C, D), lambda g, i: (g, 0, 0)),
            by_group,
            pl.BlockSpec((tt, 1), lambda g, i: (i, 0)),
            pl.BlockSpec((1, tt), lambda g, i: (0, i)),
        ],
        [jax.ShapeDtypeStruct((G, T, 3 * C), BF)],
        [by_group],
        [pltpu.VMEM((tt, C), BF)],
        cost(12 * T * D * C * G, 2 * G * (T * D + C * D + 6 * T * C), G * T * B * C // HD),
        traffic,
    )


def weight_body(C, G, hook, n1, low, dqkv, mixed, *dw):
    hook("start")
    h = C // 2
    u = dot(n1[...], dqkv[0], TN).astype(BF)
    o = dot(low[...], mixed[0], TN).astype(BF)
    for g in range(G):

        @pl.when(pl.program_id(0) == g)
        def _():
            for side in range(2):
                to = dw[2 * g + side]
                for i in range(3):
                    to[:, i * h : (i + 1) * h] = u[:, i * C + side * h : i * C + (side + 1) * h]
                to[:, 3 * h : 4 * h] = o[:, side * h : (side + 1) * h]

    hook("end")


def weight_grads(n1, low, dqkv, mixed, traffic):
    T, D = n1.shape
    G, _, C = mixed.shape
    rows = pick(D, 256)
    steps = D // rows

    def out(g):
        place = lambda n, i: (jnp.where(n == g, i, jnp.where(n < g, 0, steps - 1)), 0)
        return pl.BlockSpec((rows, 2 * C), place)

    columns = pl.BlockSpec((T, rows), lambda g, i: (0, i))
    return launch(
        functools.partial(weight_body, C, G),
        "weight_grads",
        (G, steps),
        (n1, low, dqkv, mixed),
        [
            columns,
            columns,
            pl.BlockSpec((1, T, 3 * C), lambda g, i: (g, 0, 0)),
            pl.BlockSpec((1, T, C), lambda g, i: (g, 0, 0)),
        ],
        [jax.ShapeDtypeStruct((D, 2 * C), BF)] * (2 * G),
        [out(g) for g in range(G) for _ in range(2)],
        [],
        cost(8 * T * D * C * G, 2 * G * (2 * T * D + 4 * T * C + 4 * D * C)),
        traffic,
    )


def project_body(x, gain, valid, mixed, wo, hidden, n2, square):
    @pl.when(pl.program_id(0) == 0)
    def _():
        square[...] = jnp.zeros_like(square)

    a = sum(dot(mixed[g], wo[g]) for g in range(wo.shape[0]))
    h = x[...].astype(F32) + a
    hidden[...] = h
    n2[...] = (h * rms(h) * gain[...].astype(F32)).astype(BF)
    square[...] += row_sum(valid[...] * a * a)


def project(x, gain, valid, mixed, wo):
    T, D = x.shape
    G, C, _ = wo.shape
    tt = pick(T, 256, 128)
    tile = lambda c: pl.BlockSpec((tt, c), lambda i: (i, 0))
    out, _ = launch(
        lambda hook, *refs: project_body(*refs),
        "project",
        (T // tt,),
        (x, gain, valid, mixed, wo),
        [tile(D), whole((1, D)), tile(1), pl.BlockSpec((G, tt, C), lambda i: (0, i, 0)), whole(wo.shape)],
        [jax.ShapeDtypeStruct((T, D), F32), jax.ShapeDtypeStruct((T, D), BF), jax.ShapeDtypeStruct((1, D), F32)],
        [tile(D), tile(D), pl.BlockSpec((1, D), lambda i: (0, 0))],
        [],
        cost(2 * T * D * D, 12 * T * D),
    )
    return out


def feed_body(
    hook, n2, g, hba, hbb, upa, upb, downa, downb, feed, n2g, dua, dub, dda, ddb, ba, bb, acc_f, acc_n, act, pg, wu, wd
):
    step = pl.program_id(0)
    T, D = n2.shape
    ft = hba.shape[1]
    chunk = pick(T, 768, 384, 128)
    hook("start")

    @pl.when(step == 0)
    def _():
        acc_f[...] = jnp.zeros_like(acc_f)
        acc_n[...] = jnp.zeros_like(acc_n)

    wu[:, :ft], wu[:, ft:] = upa[...], upb[...]
    wd[:ft, :], wd[ft:, :] = downa[...], downb[...]
    hb = jnp.concatenate([hba[...], hbb[...]], axis=1).astype(F32)
    ba[...] = jnp.zeros_like(ba)
    bb[...] = jnp.zeros_like(bb)

    def one(i, _):
        s = pl.ds(pl.multiple_of(i * chunk, chunk), chunk)
        p = dot(n2[s, :], wu[...]) + hb
        ag = dot(g[s, :], wd[...], NT)
        sg = 0.5 * jnp.tanh(0.5 * p) + 0.5
        ps = p * sg
        a = ps.astype(BF)
        q = (ag * (sg + ps * (1.0 - sg))).astype(BF)
        act[s, :] = a
        pg[s, :] = q
        b = row_sum(q.astype(F32))
        ba[...] += b[:, :ft]
        bb[...] += b[:, ft:]
        acc_f[s, :] += dot(a, wd[...])
        acc_n[s, :] += dot(q, wu[...], NT)
        return 0

    lax.fori_loop(0, T // chunk, one, 0)
    hook("middle")
    u = dot(n2[...], pg[...], TN).astype(BF)
    dua[...], dub[...] = u[:, :ft], u[:, ft:]
    d = dot(act[...], g[...], TN).astype(BF)
    dda[...], ddb[...] = d[:ft], d[ft:]

    @pl.when(step == pl.num_programs(0) - 1)
    def _():
        feed[...] = acc_f[...].astype(BF)
        n2g[...] = acc_n[...].astype(BF)

    hook("end")


def feed_forward(n2, g, biases, ups, downs, traffic=None):
    T, D = n2.shape
    F = biases[0].shape[1]
    ft = pick(F, 256)
    up = pl.BlockSpec((D, ft), lambda f: (0, f))
    down = pl.BlockSpec((ft, D), lambda f: (f, 0))
    bias = pl.BlockSpec((1, ft), lambda f: (0, f))
    return launch(
        feed_body,
        "feed_forward",
        (F // ft,),
        (n2, g, *biases, *ups, *downs),
        [whole((T, D)), whole((T, D)), bias, bias, up, up, down, down],
        [jax.ShapeDtypeStruct((T, D), BF)] * 2
        + [jax.ShapeDtypeStruct((D, F), BF)] * 2
        + [jax.ShapeDtypeStruct((F, D), BF)] * 2
        + [jax.ShapeDtypeStruct((1, F), F32)] * 2,
        [whole((T, D)), whole((T, D)), up, up, down, down, bias, bias],
        [
            pltpu.VMEM((T, D), F32),
            pltpu.VMEM((T, D), F32),
            pltpu.VMEM((T, 2 * ft), BF),
            pltpu.VMEM((T, 2 * ft), BF),
            pltpu.VMEM((D, 2 * ft), BF),
            pltpu.VMEM((2 * ft, D), BF),
        ],
        cost(24 * T * D * F, 16 * T * D + 16 * D * F, 2 * T * F),
        traffic,
    )


def middle_body(n, hook, *refs):
    hook("start")
    hidden, g, gain, out_bias, valid = refs[:5]
    feeds, grads = refs[5 : 5 + n], refs[5 + n : 5 + 2 * n]
    out, low, sums = refs[5 + 2 * n :]

    @pl.when(pl.program_id(0) == 0)
    def _():
        sums[...] = jnp.zeros_like(sums)

    h, go = hidden[...], g[...].astype(F32)
    f = sum(a[...].astype(F32) for a in feeds) + out_bias[...].astype(F32)
    ng = sum(a[...].astype(F32) for a in grads)
    result = h + f
    out[...] = result.astype(BF)
    r2 = rms(h)
    wg = ng * gain[...].astype(F32)
    inner = jnp.sum(wg * h, axis=1, keepdims=True)
    low[...] = (go + wg * r2 - h * (r2 * r2 * r2 * inner / h.shape[1])).astype(BF)
    v = valid[...]
    for i, a in enumerate((ng * h * r2, go, v * f * f, v * result * result)):
        sums[i : i + 1, :] += row_sum(a)
    hook("end")


def middle(hidden, g, gain, out_bias, valid, feeds, grads, traffic=None):
    T, D = hidden.shape
    tt = pick(T, 256, 128)
    tile = lambda c: pl.BlockSpec((tt, c), lambda i: (i, 0))
    n = len(feeds)
    return launch(
        functools.partial(middle_body, n),
        "middle",
        (T // tt,),
        (hidden, g, gain, out_bias, valid, *feeds, *grads),
        [tile(D), tile(D), whole((1, D)), whole((1, D)), tile(1)] + [tile(D)] * (2 * n),
        [jax.ShapeDtypeStruct((T, D), BF), jax.ShapeDtypeStruct((T, D), BF), jax.ShapeDtypeStruct((8, D), F32)],
        [tile(D), tile(D), pl.BlockSpec((8, D), lambda i: (0, 0))],
        [],
        cost(40 * T * D, (10 + 4 * n) * T * D),
        traffic,
    )


def last_body(traffic, hook, x, gain, low, dqkv, w, out, part, summed=None):
    hook("start")

    @pl.when(pl.program_id(0) == 0)
    def _():
        part[...] = jnp.zeros_like(part)

    ng = sum(dot(dqkv[g], w[g], NT) for g in range(w.shape[0]))
    t = x[...].astype(F32)
    r1 = rms(t)
    wg = ng * gain[...].astype(F32)
    inner = jnp.sum(wg * t, axis=1, keepdims=True)
    out[...] = low[...].astype(F32) + wg * r1 - t * (r1 * r1 * r1 * inner / t.shape[1])
    part[...] += row_sum(ng * t * r1)
    if traffic is not None:
        traffic.refs["part"], traffic.refs["summed"] = part, summed
    hook("end")


def last(x, gain, low, dqkv, w, traffic=None, small=None):
    T, D = x.shape
    G, _, K = w.shape
    rows = [] if small is None else [small]
    tt = pick(T, 256, 128)
    tile = lambda c: pl.BlockSpec((tt, c), lambda i: (i, 0))
    return launch(
        functools.partial(last_body, traffic),
        "last",
        (T // tt,),
        (x, gain, low, dqkv, w),
        [tile(D), whole((1, D)), tile(D), pl.BlockSpec((G, tt, K), lambda i: (0, i, 0)), whole(w.shape)],
        [jax.ShapeDtypeStruct((n, D), F32) for n in (T, 1, *rows)],
        [tile(D), *[pl.BlockSpec((n, D), lambda i: (0, 0)) for n in (1, *rows)]],
        [],
        cost(6 * T * D * D, 8 * T * D + 6 * D * D),
        traffic,
    )


def finish_body(h, joined, up, down, q, k, v, o, up_out, down_out):
    j = joined[...].astype(F32).T
    for i, ref in enumerate((q, k, v, o)):
        ref[...] = j[i * h : (i + 1) * h]
    up_out[...] = up[...].astype(F32)
    down_out[...] = down[...].astype(F32)


def finish(joined, up, down):
    D, F = up.shape
    h = joined.shape[1] // 4
    rows = pick(D, 256)
    steps = D // rows
    tile = lambda n, c: pl.BlockSpec((n // steps, c), lambda i: (i, 0))
    ups = [tile(D, F), tile(F, D)]
    out, _ = launch(
        lambda hook, *refs: finish_body(h, *refs),
        "finish",
        (steps,),
        (joined, up, down),
        [tile(D, 4 * h), *ups],
        [jax.ShapeDtypeStruct((h, D), F32)] * 4 + [jax.ShapeDtypeStruct(a.shape, F32) for a in (up, down)],
        [pl.BlockSpec((h, rows), lambda i: (0, i))] * 4 + ups,
        [],
        cost(D * D, 6 * (4 * h * D + 2 * D * F)),
    )
    return out


def swap(a, axis, bit):
    return lax.ppermute(a, axis, [(i, i ^ bit) for i in range(lax.axis_size(axis))])


def segments(lengths):
    slots = lengths.shape[1]
    upto = lax.broadcasted_iota(jnp.int32, (1, slots, slots), 2) <= lax.broadcasted_iota(
        jnp.int32, (1, slots, slots), 1
    )
    ends = jnp.sum(jnp.where(upto, lengths[:, None, :], 0), axis=2)
    places = lax.broadcasted_iota(jnp.int32, (lengths.shape[0], L, slots), 1)
    return jnp.sum((ends[:, None, :] <= places).astype(jnp.int32), axis=2)


def merge(*dicts):
    return {k: v for d in dicts for k, v in d.items()}


def fused(x, cotangent, weights, gains, out_bias, valid, ids, mp):
    T, D = x.shape
    joined, wo, up, down, bias = weights
    h = wo.shape[0]
    hidden_units = up.shape[1]
    near, far, deep = ("dp", 1), ("dp", 2), ("dp", 4)

    J, W = Gather("j", D, 3 * h), Gather("w", h, D)
    U, V = Gather("u", D, hidden_units), Gather("v", hidden_units, D)
    both, four = (J, W), (J, W, U, V)
    steps = T // pick(T, 512, 384, 256, 128)
    t = Traffic(
        1,
        [CORE, Y, near, far],
        dict(j=joined, w=wo, u=up, v=down),
        merge(*[g.buffers("s", "q", "o", "p") for g in both], *[g.buffers("s", "q") for g in (U, V)]),
    )
    t.on(0, "start", *[g.start(s) for s in "sy" for g in both], J.wait("s"))
    t.on(0, "middle", *[g.wait("y") for g in both], *[g.start("a") for g in both])
    t.on(0, "middle", *[g.start(s) for s in "ys" for g in (U, V)])
    t.on(2, "start", *[g.wait("a") for g in both], *[g.start("b") for g in both])
    t.on(steps - 1, "end", *[g.wait("b") for g in both], *[g.start("p") for g in both])
    t.on(steps, "start", J.wait("p"))
    t.on(2 * steps - 1, "end", W.wait("s"), W.wait("p"), *[g.wait(s) for s in "ys" for g in (U, V)])
    (qkv, mixed, w, n1), got = attend(x, gains[0], *ids, h, [("j", "js"), ("jo", "jp")], t)
    wo_all = jnp.stack([jnp.concatenate([wo, got["ws"]]), jnp.concatenate([got["wo"], got["wp"]])])
    hidden, n2, att_square = project(x, gains[1], valid, mixed, wo_all)

    bias_o = swap(bias, "mp", 2)
    t = Traffic(
        2,
        [CORE, near, far],
        dict(uq=got["uq"], vq=got["vq"], u=up, v=down),
        merge(*[g.buffers("o", "p") for g in (U, V)]),
    )
    fs = hidden_units // pick(hidden_units, 256)
    t.on(0, "start", *[g.start("a") for g in (U, V)])
    t.on(3, "start", *[g.wait("a") for g in (U, V)], *[g.start("b") for g in (U, V)])
    t.on(4, "start", *[g.wait("b") for g in (U, V)], *[g.start("p") for g in (U, V)])
    t.on(fs - 1, "end", *[g.wait("p") for g in (U, V)])
    own, far_weights = feed_forward(
        n2, cotangent, (bias, swap(bias, "mp", 1)), (up, got["us"]), (down, got["vs"]), t
    )

    a, b = (1, 2, 4), (2, 1, 4)
    U0, D0 = (
        Stream("u0", "u0a", "u0b", D, hidden_units, a, 2, joins="u1"),
        Stream("d0", "d0a", "d0b", hidden_units, D, b, 2, joins="d1"),
    )
    U1, D1 = Stream("u1", "u1a", "u1b", D, hidden_units, a, 2), Stream("d1", "d1a", "d1b", hidden_units, D, b, 2)
    half = D // 2
    att = [
        [
            Near(f"j{n}{m}", f"j{n}a", f"j{n}b", half, 4 * h, (a, b)[m], 1, m * half, None if n else f"j1{m}")
            for m in range(2)
        ]
        for n in range(2)
    ]
    first = (U0, D0)
    second = (U1, D1)
    t = Traffic(
        3,
        [CORE, near, far],
        dict(u0a=own[2], u0b=own[3], d0a=own[4], d0b=own[5]),
        merge(*[s.buffers("c", "s0", "r0", "s1", "r1") for s in first]),
    )
    t.on(0, "start", *[s.start_core for s in first])
    t.on(0, "middle", *[s.wait_core for s in first], *[s.start(0) for s in first])
    t.on(3, "start", *[s.wait(0) for s in first], *[s.start(1) for s in first])
    t.on(fs - 1, "end", *[s.wait(1) for s in first])
    other, left = feed_forward(
        n2,
        cotangent,
        (bias_o, swap(bias_o, "mp", 1)),
        (far_weights["uo"], far_weights["up"]),
        (far_weights["vo"], far_weights["vp"]),
        t,
    )
    feeds = [own, other]
    t = Traffic(
        7,
        [CORE],
        dict(u1b=other[3], d1b=other[5]),
        merge(*[s.buffers("c") for s in second]),
    )
    ls = T // pick(T, 256, 128)
    t.on(0, "start", *[s.start_core for s in second]).on(ls - 1, "end", *[s.wait_core for s in second])
    (out, low, sums), cores = middle(
        hidden, cotangent, gains[1], out_bias, valid, [f[0] for f in feeds], [f[1] for f in feeds], t
    )

    held = dict(u1a=other[2], d1a=other[4]) | cores
    t = Traffic(4, [near, far], held, merge(*[s.buffers("s0", "r0", "s1", "r1") for s in second]))
    t.on(0, "start", *[s.start(0) for s in second])
    t.on(2 * steps - 2, "start", *[s.wait(0) for s in second], *[s.start(1) for s in second])
    t.on(2 * steps - 1, "end", *[s.wait(1) for s in second])
    (dqkv,), arrived = attend_back(low, wo_all, qkv, *ids, t)

    t = Traffic(
        5, [Y], held | {k: v for k, v in arrived.items() if k[2] == "r"}, merge(*[s.buffers("e", "y") for s in second])
    )
    ws = D // pick(D, 256)
    t.on(0, "start", *[f for s in second for f in (s.keep, s.start_cross)])
    t.on(2 * ws - 1, "end", *[s.wait_cross for s in second])
    dw, crossed = weight_grads(n1, low, dqkv, mixed, t)

    units = jnp.zeros((1, lax.axis_size("mp") * hidden_units), F32)
    for change, part in ((0, own[6]), (1, own[7]), (2, other[6]), (3, other[7])):
        units = lax.dynamic_update_slice(units, part, (0, (mp ^ change) * hidden_units))
    count = jnp.where(jnp.arange(D) == 0, jnp.sum(valid), 0.0)[None]
    rows = jnp.concatenate([units.reshape(-1, D), sums[:4], att_square, count])
    n_rows = rows.shape[0] + 1
    tall = (n_rows + 7) // 8 * 8
    small = jnp.pad(rows, ((1, tall - n_rows), (0, 0)))

    held = dict(j0a=dw[0], j0b=dw[1], j1a=dw[2], j1b=dw[3], u1y=crossed["u1y"], d1y=crossed["d1y"], small=small)
    held |= dict(u0a=own[2], d0a=own[4]) | {k: v for k, v in left.items() if k[2] in "cr"}
    flat = [s for pair in att for s in pair]
    bits = [CORE, Y, near, far, deep]
    t = Traffic(
        6,
        bits,
        held,
        merge(*[s.buffers("s2", "r2", "f") for s in first], dict(joined=(D, 4 * h))),
        merge(
            *[s.scratch("m", "c", "s0", "r0") for s in flat],
            *[s.scratch("s1", "r1", "s2", "r2", "f") for s in att[0]],
            *[s.scratch("e", "y") for s in att[1]],
            {f"t{n}": pltpu.VMEM((tall, D), F32) for n in range(2 * len(bits) + 1)},
        ),
    )

    def load_small(t):
        return t.local("small", t.refs["small"], t.refs["t0"])

    def first_small(t):
        load_small(t).wait()
        t.refs["t0"][0:1, :] = t.refs["part"][...]

    def exchange_small(t, n):
        return t.copy(f"t{n}", t.refs[f"t{2 * n}"], t.refs[f"t{2 * n + 1}"], bits[n])

    def store_small(t):
        t.refs["summed"][...] = t.refs[f"t{2 * len(bits)}"][...]

    def start_small(n):
        return lambda t: exchange_small(t, n).start()

    def end_small(n):
        def action(t):
            exchange_small(t, n).wait()
            t.refs[f"t{2 * n + 2}"][...] = t.refs[f"t{2 * n}"][...] + t.refs[f"t{2 * n + 1}"][...]

        return action

    t.on(0, "start", *[s.start_core for s in flat], *[s.start_load for s in flat])
    t.on(0, "start", lambda t: load_small(t).start(), *[s.start(2) for s in first])
    t.on(1, "start", *[s.wait_load for s in flat], *[s.wait_core for s in flat], *[s.start(0) for s in flat])
    end = [first_small, start_small(0)]
    end += [f for s in first for f in (s.wait(2), s.total, s.start_spread(2))]
    end += [end_small(0), start_small(1)]
    end += [f for s in att[1] for f in (s.wait(0), s.keep, s.start_cross)] + [s.wait(0) for s in att[0]]
    end += [end_small(1), start_small(2)]
    end += [f for s in first for f in (s.wait_spread(2), s.start_spread(1))]
    end += [s.wait_cross for s in att[1]] + [s.start(1) for s in att[0]]
    end += [end_small(2), start_small(3)]
    end += [f for s in att[0] for f in (s.wait(1), s.start(2))]
    end += [f for s in first for f in (s.wait_spread(1), s.start_spread(0))]
    end += [f for s in att[0] for f in (s.wait(2), s.total, s.start_spread(2))]
    end += [end_small(3), start_small(4)]
    for j in (2, 1):
        end += [f for s in att[0] for f in (s.wait_spread(j), s.start_spread(j - 1))]
    end += [end_small(4), store_small]
    end += [f for s in att[0] for f in (s.wait_spread(0), s.start_store)]
    end += [s.wait_spread(0) for s in first] + [s.wait_store for s in att[0]]
    t.on(ls - 1, "end", *end)
    (input_gradient, _, summed), done = last(x, gains[0], low, dqkv, w, t, tall)
    return (out, input_gradient, done["joined"], done["u0f"], done["d0f"]), summed


def gathered(x, cotangent, weights, gains, out_bias, valid, ids):
    D = x.shape[1]
    joined, wo, up, down, bias = weights
    every = lambda a, d: lax.all_gather(a, "mp", axis=d, tiled=True)
    two = lambda a, d: tuple(jnp.split(every(a, d), 2, axis=d))
    sides = [jnp.concatenate(p, axis=1) for p in zip(*(two(a, 1) for a in jnp.split(joined, 3, axis=1)))]
    plain = Traffic(0, [], dict(a=sides[0], b=sides[1]), {})
    (qkv, mixed, w, n1), _ = attend(x, gains[0], *ids, sides[0].shape[1] // 3, [("a", "b")], plain)
    wo_all = every(wo, 0)[None]
    hidden, n2, att_square = project(x, gains[1], valid, mixed, wo_all)
    f, _ = feed_forward(n2, cotangent, two(bias, 1), two(up, 1), two(down, 0))
    (out, low, sums), _ = middle(hidden, cotangent, gains[1], out_bias, valid, [f[0]], [f[1]])
    (dqkv,), _ = attend_back(low, wo_all, qkv, *ids, None)
    dw, _ = weight_grads(n1, low, dqkv, mixed, None)
    (input_gradient, first_part), _ = last(x, gains[0], low, dqkv, w)

    def total(pair, d):
        part = lax.psum_scatter(jnp.concatenate(pair, axis=d), "mp", scatter_dimension=d, tiled=True)
        return lax.psum(part, "dp")

    cut = [jnp.split(a, 4, axis=1) for a in dw]
    joined_total = jnp.concatenate([total(pair, 1) for pair in zip(*cut)], axis=1)
    grads = (out, input_gradient, joined_total, total(f[2:4], 1), total(f[4:6], 0))
    units = jnp.concatenate(f[6:], axis=1).reshape(-1, D)
    count = jnp.where(jnp.arange(D) == 0, jnp.sum(valid), 0.0)[None]
    return grads, lax.psum(jnp.concatenate([first_part, units, sums[:4], att_square, count]), ("dp", "mp"))


def per_device(
    tokens,
    lengths,
    cotangent,
    query_weight,
    key_weight,
    value_weight,
    out_weight,
    up_weight,
    hidden_bias,
    down_weight,
    output_bias,
    first_gain,
    second_gain,
):
    T, D = tokens.shape
    rows = T // L
    mp = lax.axis_index("mp")
    segment_ids = segments(lax.dynamic_slice_in_dim(lengths, mp * rows, rows))
    valid = (segment_ids < SLOTS).reshape(-1, 1).astype(F32)
    ids = (segment_ids + L * lax.broadcasted_iota(jnp.int32, (rows, L), 0)).reshape(-1)
    ids = (ids[:, None], ids[None, :])
    joined = jnp.concatenate([query_weight, key_weight, value_weight], axis=1)
    bias = hidden_bias.reshape(1, -1)
    gains = (first_gain.reshape(1, -1), second_gain.reshape(1, -1))
    weights = (joined, out_weight, up_weight, down_weight, bias)
    rest = (gains, output_bias.reshape(1, -1), valid, ids)
    if lax.axis_size("mp") == 4 and lax.axis_size("dp") == 8:
        grads, small = fused(tokens, cotangent, weights, *rest, mp)
    else:
        grads, small = gathered(tokens, cotangent, weights, *rest)
    out, input_gradient, joined_total, up_total, down_total = grads
    n = hidden_bias.shape[0] * lax.axis_size("mp") // D + 1
    squares = jnp.sum(small[n + 2 : n + 6], axis=1)
    mean = lambda i: jnp.sqrt(squares[i] / (squares[3] * D))
    q, k, v, o, up_total, down_total = finish(joined_total, up_total, down_total)
    return (
        out,
        input_gradient,
        q.T,
        k.T,
        v.T,
        o,
        up_total,
        lax.dynamic_slice_in_dim(small[1:n].reshape(-1), mp * bias.shape[1], bias.shape[1]),
        down_total,
        small[n + 1],
        small[0],
        small[n],
        jnp.stack([mean(2), mean(0), mean(1)]),
    )


def solution(mesh):
    return jax.shard_map(
        per_device,
        mesh=mesh,
        in_specs=(
            P(("dp", "mp"), None),
            P("dp", None),
            P(("dp", "mp"), None),
            P(None, "mp"),
            P(None, "mp"),
            P(None, "mp"),
            P("mp", None),
            P(None, "mp"),
            P("mp"),
            P("mp", None),
            P(),
            P(),
            P(),
        ),
        out_specs=(
            P(("dp", "mp"), None),
            P(("dp", "mp"), None),
            P(None, "mp"),
            P(None, "mp"),
            P(None, "mp"),
            P("mp", None),
            P(None, "mp"),
            P("mp"),
            P("mp", None),
            P(),
            P(),
            P(),
            P(),
        ),
        check_vma=False,
    )
```

```python
import functools
import math

import jax
import jax.numpy as jnp
from jax import lax
from jax.experimental import pallas as pl
from jax.experimental.pallas import tpu as pltpu
from jax.sharding import PartitionSpec as P

HD = 80
L = 64
SLOTS = 32
LANES = 128
EPSILON = 1e-06
MASKED = -1e30
F32 = jnp.float32
BF = jnp.bfloat16
NN = (((1,), (0,)), ((), ()))
NT = (((1,), (1,)), ((), ()))
TN = (((0,), (0,)), ((), ()))
VMEM_BYTES = 60 << 20


def dot(a, b, dims=NN):
    return lax.dot_general(a, b, dims, preferred_element_type=F32)


def pick(n, *sizes):
    return next((s for s in sizes if n % s == 0), n)


def whole(shape):
    return pl.BlockSpec(shape, lambda *i: (0,) * len(shape), pipeline_mode=pl.Buffered(1))


def cost(flops, nbytes, exps=0):
    return pl.CostEstimate(flops=int(flops), bytes_accessed=int(nbytes), transcendentals=int(exps))


def row_sum(x):
    return jnp.sum(x, axis=0, keepdims=True)


def rms(x):
    return lax.rsqrt(jnp.mean(x * x, axis=1, keepdims=True) + EPSILON)


MESH = pl.DeviceIdType.MESH
CORE, Y = ("mp", 1), ("mp", 2)


def bit_of(axis, bit):
    return lax.rem(lax.axis_index(axis) // bit, 2)


def flip(axis, bit):
    return {axis: lax.axis_index(axis) + bit - 2 * bit * bit_of(axis, bit)}


class Traffic:
    def __init__(self, number, partners, arrays, buffers, scratch=None):
        self.number, self.partners = number, partners
        self.arrays, self.buffers, self.scratch = arrays, buffers, scratch or {}
        self.events, self.slots, self.refs = [], {}, {}

    def on(self, step, place, *actions):
        self.events += [(step, place, f) for f in actions]
        return self

    def run(self, step, place):
        for at, where, action in self.events:
            if where == place:
                pl.when(step == at)(functools.partial(action, self))

    def greet(self):
        sem = pltpu.get_barrier_semaphore()
        for p in self.partners:
            pl.semaphore_signal(sem, inc=1, device_id=flip(*p), device_id_type=MESH)
        pl.semaphore_wait(sem, len(self.partners))

    def copy(self, name, src, dst, to):
        i = self.slots.setdefault(name, len(self.slots))
        return pltpu.make_async_remote_copy(
            src_ref=src,
            dst_ref=dst,
            send_sem=self.sems.at[0, i],
            recv_sem=self.sems.at[1, i],
            device_id=flip(*to),
            device_id_type=MESH,
        )

    def local(self, name, src, dst):
        i = self.slots.setdefault(name, len(self.slots))
        return pltpu.make_async_copy(src, dst, self.sems.at[0, i])


COPIES = 48


def launch(body, name, grid, args, in_specs, outs, out_specs, scratch, cost_estimate, traffic=None):
    n_args, n_outs = len(args), len(outs)
    names, arrays, buffers = [], [], []
    if traffic is not None:
        names = [*traffic.arrays, *traffic.buffers]
        arrays = list(traffic.arrays.values())
        buffers = [jax.ShapeDtypeStruct(s, BF) for s in traffic.buffers.values()]
        names += [*traffic.scratch]
        scratch = [*scratch, *traffic.scratch.values(), pltpu.SemaphoreType.DMA((2, COPIES))]

    def kernel(*refs):
        hook = lambda place: None
        inputs, refs = refs[:n_args], refs[n_args:]
        moved, refs = refs[: len(arrays)], refs[len(arrays) :]
        results, refs = refs[:n_outs], refs[n_outs:]
        landing, refs = refs[: len(buffers)], refs[len(buffers) :]
        if traffic is not None:
            step = pl.program_id(0)
            for d in range(1, len(grid)):
                step = step * grid[d] + pl.program_id(d)
            traffic.sems, refs = refs[-1], refs[:-1]
            n = len(refs) - len(traffic.scratch)
            traffic.refs = dict(zip(names, [*moved, *landing, *refs[n:]]))
            refs = refs[:n]
            if traffic.partners:
                pl.when(step == 0)(traffic.greet)
            hook = lambda place: traffic.run(step, place)
        body(hook, *inputs, *results, *refs)

    anywhere = pl.BlockSpec(memory_space=pl.ANY)
    out = pl.pallas_call(
        kernel,
        grid=grid,
        in_specs=[*in_specs, *[anywhere] * len(arrays)],
        out_specs=[*out_specs, *[anywhere] * len(buffers)],
        out_shape=[*outs, *buffers],
        scratch_shapes=scratch,
        compiler_params=pltpu.CompilerParams(
            vmem_limit_bytes=VMEM_BYTES,
            **({} if traffic is None or not traffic.partners else dict(collective_id=traffic.number, has_side_effects=True)),
        ),
        cost_estimate=cost_estimate,
        name=name,
    )(*args, *arrays)
    return out[:n_outs], dict(zip(names[len(arrays) : len(arrays) + len(buffers)], out[n_outs:]))


def add_rows(sources, target, rows):
    columns = target.shape[1]
    tile = pl.BlockSpec((rows // 2 if rows // 2 % 16 == 0 else rows, columns), lambda i: (i, 0))

    def body(*refs):
        refs[-1][...] = sum(r[...].astype(F32) for r in refs[:-1]).astype(BF)

    pltpu.emit_pipeline(
        body, grid=(rows // tile.block_shape[0],), in_specs=[tile] * len(sources), out_specs=[tile]
    )(*[r.at[pl.ds(pl.multiple_of(o, 16), rows), :] for r, o in sources], target)


class Stream:
    def __init__(self, tag, mine, theirs, rows, columns, order, cut, base=0, joins=None):
        self.tag, self.mine, self.theirs, self.base = tag, mine, theirs, base
        self.rows, self.columns, self.order = rows, columns, order
        self.cut, self.joins = cut, joins

    def name(self, what):
        return self.tag + what

    def buffers(self, *what):
        size = lambda w: self.rows if w[0] in "cf" else self.rows >> self.cut if w[0] in "ey" else self.rows >> (int(w[1]) + 1)
        return {self.name(w): (size(w), self.columns) for w in what}

    def place(self, stages):
        first, n = 0, self.rows
        for bit in self.order[:stages]:
            n //= 2
            first = first + bit_of("dp", bit) * n
        return first, n

    def raw(self, t, first, arrived):
        out = [(t.refs[self.mine], first + self.base), (t.refs[self.name("c")], first)]
        return out + [(t.refs[self.name(f"r{j}")], first - self.place(j + 1)[0]) for j in range(arrived)]

    def sources(self, t, first, arrived):
        if self.joins is None or arrived < self.cut:
            return self.raw(t, first, arrived)
        start = self.place(self.cut)[0]
        joined = (t.refs[self.joins + "y"], first - start)
        if self.name("e") not in t.refs:
            return [*self.raw(t, first, arrived), joined]
        late = [(t.refs[self.name(f"r{j}")], first - self.place(j + 1)[0]) for j in range(self.cut, arrived)]
        return [(t.refs[self.name("e")], first - start), *late, joined]

    def core(self, t):
        src = t.refs[self.theirs].at[pl.ds(self.base, self.rows), :]
        return t.copy(self.name("c"), src, t.refs[self.name("c")], CORE)

    def start_core(self, t):
        self.core(t).start()

    def wait_core(self, t):
        self.core(t).wait()

    def exchange(self, t, j):
        return t.copy(self.name(f"r{j}"), t.refs[self.name(f"s{j}")], t.refs[self.name(f"r{j}")], ("dp", self.order[j]))

    def start(self, j):
        def action(t):
            first, n = self.place(j)
            n //= 2
            sent = first + (1 - bit_of("dp", self.order[j])) * n
            add_rows(self.sources(t, sent, j), t.refs[self.name(f"s{j}")], n)
            self.exchange(t, j).start()

        return action

    def wait(self, j):
        return lambda t: self.exchange(t, j).wait()

    def keep(self, t):
        first, n = self.place(self.cut)
        add_rows(self.raw(t, first, self.cut), t.refs[self.name("e")], n)

    def cross(self, t):
        return t.copy(self.name("y"), t.refs[self.name("e")], t.refs[self.name("y")], Y)

    def start_cross(self, t):
        self.cross(t).start()

    def wait_cross(self, t):
        self.cross(t).wait()

    def total(self, t):
        first, n = self.place(len(self.order))
        target = t.refs[self.name("f")].at[pl.ds(pl.multiple_of(first, 16), n), :]
        add_rows(self.sources(t, first, len(self.order)), target, n)

    def spread(self, t, j):
        first, n = self.place(j + 1)
        part = t.refs[self.name("f")].at[pl.ds(pl.multiple_of(first, 16), n), :]
        return t.copy(self.name(f"f{j}"), part, part, ("dp", self.order[j]))

    def start_spread(self, j):
        return lambda t: self.spread(t, j).start()

    def wait_spread(self, j):
        return lambda t: self.spread(t, j).wait()


def sum_rows(sources, target, rows):
    step = pick(rows, 80, 64, 32, 16)

    def one(i, _):
        part = lambda o: pl.ds(pl.multiple_of(o + i * step, 16), step)
        target[part(0), :] = sum(r[part(o), :].astype(F32) for r, o in sources).astype(BF)
        return 0

    lax.fori_loop(0, rows // step, one, 0)


class Near(Stream):
    def scratch(self, *what):
        size = lambda w: self.rows if w == "m" else self.buffers(w)[self.name(w)][0]
        return {self.name(w): pltpu.VMEM((size(w), self.columns), BF) for w in what}

    def raw(self, t, first, arrived):
        out = super().raw(t, first, arrived)
        return [(t.refs[self.name("m")], first), *out[1:]]

    def load(self, t):
        src = t.refs[self.mine].at[pl.ds(self.base, self.rows), :]
        return t.local(self.name("m"), src, t.refs[self.name("m")])

    def start_load(self, t):
        self.load(t).start()

    def wait_load(self, t):
        self.load(t).wait()

    def start(self, j):
        def action(t):
            first, n = self.place(j)
            n //= 2
            sent = first + (1 - bit_of("dp", self.order[j])) * n
            sum_rows(self.sources(t, sent, j), t.refs[self.name(f"s{j}")], n)
            self.exchange(t, j).start()

        return action

    def keep(self, t):
        first, n = self.place(self.cut)
        sum_rows(self.raw(t, first, self.cut), t.refs[self.name("e")], n)

    def total(self, t):
        first, n = self.place(len(self.order))
        target = t.refs[self.name("f")].at[pl.ds(pl.multiple_of(first, 16), n), :]
        sum_rows(self.sources(t, first, len(self.order)), target, n)

    def store(self, t):
        out = t.refs["joined"].at[pl.ds(self.base, self.rows), :]
        return t.local(self.name("o"), t.refs[self.name("f")], out)

    def start_store(self, t):
        self.store(t).start()

    def wait_store(self, t):
        self.store(t).wait()


class Gather:
    def __init__(self, tag, rows, columns):
        self.tag, self.rows, self.columns = tag, rows, columns
        self.n = rows // 4

    def buffers(self, *what):
        return {self.tag + w: (self.n if w == "q" else self.rows, self.columns) for w in what}

    def quarter(self, ref, flip_x=0, flip_z=0, first=0, rows=None):
        x, z = bit_of("dp", 1), bit_of("dp", 2)
        x, z = (1 - x if flip_x else x), (1 - z if flip_z else z)
        start = pl.multiple_of((2 * z + x) * self.n + first, 16)
        return ref.at[pl.ds(start, self.n if rows is None else rows), :]

    def copies(self, t, step):
        own, o = t.refs[self.tag], t.refs.get(self.tag + "o")
        name = self.tag + step
        if step == "s":
            return [t.copy(name, own, t.refs[name], CORE)]
        if step == "y":
            return [t.copy(name, self.quarter(own), t.refs[self.tag + "q"], Y)]
        if step == "a":
            q = t.refs[self.tag + "q"]
            return [t.copy(name + str(b), q, self.quarter(o), ("dp", b)) for b in (1, 2)]
        if step == "b":
            top = (self.n // 2 + 15) // 16 * 16
            to_x = self.quarter(o, flip_z=1, rows=top)
            to_z = self.quarter(o, flip_x=1, first=top, rows=self.n - top)
            return [t.copy(name + "1", to_x, to_x, ("dp", 1)), t.copy(name + "2", to_z, to_z, ("dp", 2))]
        return [t.copy(name, o, t.refs[self.tag + "p"], CORE)]

    def start(self, step):
        def action(t):
            for c in self.copies(t, step):
                c.start()
            if step == "a":
                add_rows([(t.refs[self.tag + "q"], 0)], self.quarter(t.refs[self.tag + "o"]), self.n)

        return action

    def wait(self, step):
        def action(t):
            for c in self.copies(t, step):
                c.wait()

        return action


def windows(C):
    out = []
    for h in range(C // HD):
        w = min(LANES * (HD * h // LANES), C - 2 * LANES)
        out.append((w, HD * h - w))
    return out


def head_masks(C):
    lane = lax.broadcasted_iota(jnp.int32, (1, 2 * LANES), 1)
    return [jnp.where((lane >= lo) & (lane < lo + HD), 1.0, 0.0).astype(BF) for _, lo in windows(C)]


def softmaxes(qs, ks, allowed):
    s = [jnp.where(allowed, dot(q, k, NT) * (1.0 / math.sqrt(HD)), MASKED) for q, k in zip(qs, ks)]
    e = [jnp.exp(x - jnp.max(x, axis=1, keepdims=True)) for x in s]
    return [x * (1.0 / jnp.sum(x, axis=1, keepdims=True)) for x in e]


def allow(idc, idr, s, B):
    causal = lax.broadcasted_iota(jnp.int32, (B, B), 1) <= lax.broadcasted_iota(
        jnp.int32, (B, B), 0
    )
    return (idc[s, :] == idr[:, s]) & causal


def put(tiles, w, val):
    for n in range(2):
        t = w // LANES + n
        part = val[:, n * LANES : (n + 1) * LANES]
        tiles[t] = part if tiles[t] is None else tiles[t] + part


def fwd_body(B, C, pairs, traffic, hook, x, gain, idc, idr, qkv, mixed, w, n1, ab, sem):
    group = pl.program_id(0)
    tt = x.shape[0]
    first = pl.program_id(1) == 0
    hook("start")
    h = C // 2
    for g, pair in enumerate(pairs):

        @pl.when(first & (group == g))
        def _():
            for side in range(2):
                c = pltpu.make_async_copy(traffic.refs[pair[side]], ab, sem)
                c.start()
                c.wait()
                a = ab[...]
                for i in range(3):
                    w[0, :, i * C + side * h : i * C + (side + 1) * h] = a[:, i * h : (i + 1) * h]

    t = x[...].astype(F32)
    normed = (t * rms(t) * gain[...].astype(F32)).astype(BF)

    @pl.when(group == 0)
    def _():
        n1[...] = normed

    qkv[0] = dot(normed, w[0]).astype(BF)
    hook("middle")
    masks = head_masks(C)
    wins = [w0 for w0, _ in windows(C)]

    def block(i, _):
        s = pl.ds(pl.multiple_of(i * B, B), B)
        ok = allow(idc, idr, s, B)
        tiles = [None] * (C // LANES)
        cut = lambda n, w0: qkv[0, s, n * C + w0 : n * C + w0 + 2 * LANES]
        for g in range(0, len(wins), 8):
            hs = range(g, min(g + 8, len(wins)))
            p = softmaxes([cut(0, wins[h]) * masks[h] for h in hs], [cut(1, wins[h]) for h in hs], ok)
            o = [dot(a.astype(BF), cut(2, wins[h]) * masks[h]) for a, h in zip(p, hs)]
            for h, a in zip(hs, o):
                put(tiles, wins[h], a)
        mixed[0, s, :] = jnp.concatenate(tiles, axis=1).astype(BF)
        return 0

    lax.fori_loop(0, tt // B, block, 0)
    hook("end")


def attend(x, gain, idc, idr, h, pairs, traffic):
    T, D = x.shape
    C, G = 2 * h, len(pairs)
    tt, B = pick(T, 512, 384, 256, 128), 128
    by_group = lambda c: pl.BlockSpec((1, tt, c), lambda g, i: (g, i, 0))
    return launch(
        functools.partial(fwd_body, B, C, pairs, traffic),
        "attend",
        (G, T // tt),
        (x, gain, idc, idr),
        [
            pl.BlockSpec((tt, D), lambda g, i: (i, 0)),
            whole((1, D)),
            pl.BlockSpec((tt, 1), lambda g, i: (i, 0)),
            pl.BlockSpec((1, tt), lambda g, i: (0, i)),
        ],
        [
            jax.ShapeDtypeStruct((G, T, 3 * C), BF),
            jax.ShapeDtypeStruct((G, T, C), BF),
            jax.ShapeDtypeStruct((G, D, 3 * C), BF),
            jax.ShapeDtypeStruct((T, D), BF),
        ],
        [
            by_group(3 * C),
            by_group(C),
            pl.BlockSpec((1, D, 3 * C), lambda g, i: (g, 0, 0)),
            pl.BlockSpec((tt, D), lambda g, i: (jnp.where(g == 0, i, T // tt - 1), 0)),
        ],
        [pltpu.VMEM((D, 3 * h), BF), pltpu.SemaphoreType.DMA],
        cost(9 * T * D * C * G, 2 * G * (T * D + 4 * C * D + 5 * T * C), G * T * B * C // HD),
        traffic,
    )


def back_body(B, C, hook, hg, wo, qkv, idc, idr, dqkv, dmix):
    tt = hg.shape[0]
    scale = 1.0 / math.sqrt(HD)
    hook("start")
    dmix[...] = dot(hg[...], wo[0], NT).astype(BF)
    masks = head_masks(C)
    wins = [w0 for w0, _ in windows(C)]

    def block(i, _):
        s = pl.ds(pl.multiple_of(i * B, B), B)
        ok = allow(idc, idr, s, B)
        dq = [None] * (C // LANES)
        dk, dv = list(dq), list(dq)
        cut = lambda n, w0: qkv[0, s, n * C + w0 : n * C + w0 + 2 * LANES]
        for g in range(0, len(wins), 8):
            hs = range(g, min(g + 8, len(wins)))
            q = [cut(0, wins[h]) * masks[h] for h in hs]
            gm = [dmix[s, wins[h] : wins[h] + 2 * LANES] * masks[h] for h in hs]
            p = softmaxes(q, [cut(1, wins[h]) for h in hs], ok)
            dp = [dot(a, cut(2, wins[h]), NT) for a, h in zip(gm, hs)]
            ds = [(a * (b - jnp.sum(a * b, axis=1, keepdims=True))).astype(BF) for a, b in zip(p, dp)]
            for h, a, b, c, d in zip(hs, p, gm, ds, q):
                put(dv, wins[h], dot(a.astype(BF), b, TN))
                put(dk, wins[h], dot(c, d, TN))
                put(dq, wins[h], dot(c, cut(1, wins[h]) * masks[h]))
        for n, tiles in enumerate((dq, dk, dv)):
            a = jnp.concatenate(tiles, axis=1)
            dqkv[0, s, n * C : (n + 1) * C] = (a if n == 2 else a * scale).astype(BF)
        return 0

    lax.fori_loop(0, tt // B, block, 0)
    hook("end")


def attend_back(hg, wo, qkv, idc, idr, traffic):
    T, D = hg.shape
    G, C, _ = wo.shape
    tt, B = pick(T, 512, 384, 256, 128), 128
    by_group = pl.BlockSpec((1, tt, 3 * C), lambda g, i: (g, i, 0))
    return launch(
        functools.partial(back_body, B, C),
        "attend_back",
        (G, T // tt),
        (hg, wo, qkv, idc, idr),
        [
            pl.BlockSpec((tt, D), lambda g, i: (i, 0)),
            pl.BlockSpec((1, C, D), lambda g, i: (g, 0, 0)),
            by_group,
            pl.BlockSpec((tt, 1), lambda g, i: (i, 0)),
            pl.BlockSpec((1, tt), lambda g, i: (0, i)),
        ],
        [jax.ShapeDtypeStruct((G, T, 3 * C), BF)],
        [by_group],
        [pltpu.VMEM((tt, C), BF)],
        cost(12 * T * D * C * G, 2 * G * (T * D + C * D + 6 * T * C), G * T * B * C // HD),
        traffic,
    )


def weight_body(C, G, hook, n1, low, dqkv, mixed, *dw):
    hook("start")
    h = C // 2
    u = dot(n1[...], dqkv[0], TN).astype(BF)
    o = dot(low[...], mixed[0], TN).astype(BF)
    for g in range(G):

        @pl.when(pl.program_id(0) == g)
        def _():
            for side in range(2):
                to = dw[2 * g + side]
                for i in range(3):
                    to[:, i * h : (i + 1) * h] = u[:, i * C + side * h : i * C + (side + 1) * h]
                to[:, 3 * h : 4 * h] = o[:, side * h : (side + 1) * h]

    hook("end")


def weight_grads(n1, low, dqkv, mixed, traffic):
    T, D = n1.shape
    G, _, C = mixed.shape
    rows = pick(D, 256)
    steps = D // rows

    def out(g):
        place = lambda n, i: (jnp.where(n == g, i, jnp.where(n < g, 0, steps - 1)), 0)
        return pl.BlockSpec((rows, 2 * C), place)

    columns = pl.BlockSpec((T, rows), lambda g, i: (0, i))
    return launch(
        functools.partial(weight_body, C, G),
        "weight_grads",
        (G, steps),
        (n1, low, dqkv, mixed),
        [
            columns,
            columns,
            pl.BlockSpec((1, T, 3 * C), lambda g, i: (g, 0, 0)),
            pl.BlockSpec((1, T, C), lambda g, i: (g, 0, 0)),
        ],
        [jax.ShapeDtypeStruct((D, 2 * C), BF)] * (2 * G),
        [out(g) for g in range(G) for _ in range(2)],
        [],
        cost(8 * T * D * C * G, 2 * G * (2 * T * D + 4 * T * C + 4 * D * C)),
        traffic,
    )


def project_body(x, gain, valid, mixed, wo, hidden, n2, square):
    @pl.when(pl.program_id(0) == 0)
    def _():
        square[...] = jnp.zeros_like(square)

    a = sum(dot(mixed[g], wo[g]) for g in range(wo.shape[0]))
    h = x[...].astype(F32) + a
    hidden[...] = h
    n2[...] = (h * rms(h) * gain[...].astype(F32)).astype(BF)
    square[...] += row_sum(valid[...] * a * a)


def project(x, gain, valid, mixed, wo):
    T, D = x.shape
    G, C, _ = wo.shape
    tt = pick(T, 256, 128)
    tile = lambda c: pl.BlockSpec((tt, c), lambda i: (i, 0))
    out, _ = launch(
        lambda hook, *refs: project_body(*refs),
        "project",
        (T // tt,),
        (x, gain, valid, mixed, wo),
        [tile(D), whole((1, D)), tile(1), pl.BlockSpec((G, tt, C), lambda i: (0, i, 0)), whole(wo.shape)],
        [jax.ShapeDtypeStruct((T, D), F32), jax.ShapeDtypeStruct((T, D), BF), jax.ShapeDtypeStruct((1, D), F32)],
        [tile(D), tile(D), pl.BlockSpec((1, D), lambda i: (0, 0))],
        [],
        cost(2 * T * D * D, 12 * T * D),
    )
    return out


def feed_body(
    hook, n2, g, hba, hbb, upa, upb, downa, downb, feed, n2g, dua, dub, dda, ddb, ba, bb, acc_f, acc_n, act, pg, wu, wd
):
    step = pl.program_id(0)
    T, D = n2.shape
    ft = hba.shape[1]
    chunk = pick(T, 768, 384, 128)
    hook("start")

    @pl.when(step == 0)
    def _():
        acc_f[...] = jnp.zeros_like(acc_f)
        acc_n[...] = jnp.zeros_like(acc_n)

    wu[:, :ft], wu[:, ft:] = upa[...], upb[...]
    wd[:ft, :], wd[ft:, :] = downa[...], downb[...]
    hb = jnp.concatenate([hba[...], hbb[...]], axis=1).astype(F32)
    ba[...] = jnp.zeros_like(ba)
    bb[...] = jnp.zeros_like(bb)

    def one(i, _):
        s = pl.ds(pl.multiple_of(i * chunk, chunk), chunk)
        p = dot(n2[s, :], wu[...]) + hb
        ag = dot(g[s, :], wd[...], NT)
        sg = 0.5 * jnp.tanh(0.5 * p) + 0.5
        ps = p * sg
        a = ps.astype(BF)
        q = (ag * (sg + ps * (1.0 - sg))).astype(BF)
        act[s, :] = a
        pg[s, :] = q
        b = row_sum(q.astype(F32))
        ba[...] += b[:, :ft]
        bb[...] += b[:, ft:]
        acc_f[s, :] += dot(a, wd[...])
        acc_n[s, :] += dot(q, wu[...], NT)
        return 0

    lax.fori_loop(0, T // chunk, one, 0)
    hook("middle")
    u = dot(n2[...], pg[...], TN).astype(BF)
    dua[...], dub[...] = u[:, :ft], u[:, ft:]
    d = dot(act[...], g[...], TN).astype(BF)
    dda[...], ddb[...] = d[:ft], d[ft:]

    @pl.when(step == pl.num_programs(0) - 1)
    def _():
        feed[...] = acc_f[...].astype(BF)
        n2g[...] = acc_n[...].astype(BF)

    hook("end")


def feed_forward(n2, g, biases, ups, downs, traffic=None):
    T, D = n2.shape
    F = biases[0].shape[1]
    ft = pick(F, 256)
    up = pl.BlockSpec((D, ft), lambda f: (0, f))
    down = pl.BlockSpec((ft, D), lambda f: (f, 0))
    bias = pl.BlockSpec((1, ft), lambda f: (0, f))
    return launch(
        feed_body,
        "feed_forward",
        (F // ft,),
        (n2, g, *biases, *ups, *downs),
        [whole((T, D)), whole((T, D)), bias, bias, up, up, down, down],
        [jax.ShapeDtypeStruct((T, D), BF)] * 2
        + [jax.ShapeDtypeStruct((D, F), BF)] * 2
        + [jax.ShapeDtypeStruct((F, D), BF)] * 2
        + [jax.ShapeDtypeStruct((1, F), F32)] * 2,
        [whole((T, D)), whole((T, D)), up, up, down, down, bias, bias],
        [
            pltpu.VMEM((T, D), F32),
            pltpu.VMEM((T, D), F32),
            pltpu.VMEM((T, 2 * ft), BF),
            pltpu.VMEM((T, 2 * ft), BF),
            pltpu.VMEM((D, 2 * ft), BF),
            pltpu.VMEM((2 * ft, D), BF),
        ],
        cost(24 * T * D * F, 16 * T * D + 16 * D * F, 2 * T * F),
        traffic,
    )


def middle_body(n, hook, *refs):
    hook("start")
    hidden, g, gain, out_bias, valid = refs[:5]
    feeds, grads = refs[5 : 5 + n], refs[5 + n : 5 + 2 * n]
    out, low, sums = refs[5 + 2 * n :]

    @pl.when(pl.program_id(0) == 0)
    def _():
        sums[...] = jnp.zeros_like(sums)

    h, go = hidden[...], g[...].astype(F32)
    f = sum(a[...].astype(F32) for a in feeds) + out_bias[...].astype(F32)
    ng = sum(a[...].astype(F32) for a in grads)
    result = h + f
    out[...] = result.astype(BF)
    r2 = rms(h)
    wg = ng * gain[...].astype(F32)
    inner = jnp.sum(wg * h, axis=1, keepdims=True)
    low[...] = (go + wg * r2 - h * (r2 * r2 * r2 * inner / h.shape[1])).astype(BF)
    v = valid[...]
    for i, a in enumerate((ng * h * r2, go, v * f * f, v * result * result)):
        sums[i : i + 1, :] += row_sum(a)
    hook("end")


def middle(hidden, g, gain, out_bias, valid, feeds, grads, traffic=None):
    T, D = hidden.shape
    tt = pick(T, 256, 128)
    tile = lambda c: pl.BlockSpec((tt, c), lambda i: (i, 0))
    n = len(feeds)
    return launch(
        functools.partial(middle_body, n),
        "middle",
        (T // tt,),
        (hidden, g, gain, out_bias, valid, *feeds, *grads),
        [tile(D), tile(D), whole((1, D)), whole((1, D)), tile(1)] + [tile(D)] * (2 * n),
        [jax.ShapeDtypeStruct((T, D), BF), jax.ShapeDtypeStruct((T, D), BF), jax.ShapeDtypeStruct((8, D), F32)],
        [tile(D), tile(D), pl.BlockSpec((8, D), lambda i: (0, 0))],
        [],
        cost(40 * T * D, (10 + 4 * n) * T * D),
        traffic,
    )


def last_body(traffic, hook, x, gain, low, dqkv, w, out, part, summed=None):
    hook("start")

    @pl.when(pl.program_id(0) == 0)
    def _():
        part[...] = jnp.zeros_like(part)

    ng = sum(dot(dqkv[g], w[g], NT) for g in range(w.shape[0]))
    t = x[...].astype(F32)
    r1 = rms(t)
    wg = ng * gain[...].astype(F32)
    inner = jnp.sum(wg * t, axis=1, keepdims=True)
    out[...] = low[...].astype(F32) + wg * r1 - t * (r1 * r1 * r1 * inner / t.shape[1])
    part[...] += row_sum(ng * t * r1)
    if traffic is not None:
        traffic.refs["part"], traffic.refs["summed"] = part, summed
    hook("end")


def last(x, gain, low, dqkv, w, traffic=None, small=None):
    T, D = x.shape
    G, _, K = w.shape
    rows = [] if small is None else [small]
    tt = pick(T, 256, 128)
    tile = lambda c: pl.BlockSpec((tt, c), lambda i: (i, 0))
    return launch(
        functools.partial(last_body, traffic),
        "last",
        (T // tt,),
        (x, gain, low, dqkv, w),
        [tile(D), whole((1, D)), tile(D), pl.BlockSpec((G, tt, K), lambda i: (0, i, 0)), whole(w.shape)],
        [jax.ShapeDtypeStruct((n, D), F32) for n in (T, 1, *rows)],
        [tile(D), *[pl.BlockSpec((n, D), lambda i: (0, 0)) for n in (1, *rows)]],
        [],
        cost(6 * T * D * D, 8 * T * D + 6 * D * D),
        traffic,
    )


def finish_body(h, joined, up, down, q, k, v, o, up_out, down_out):
    j = joined[...].astype(F32).T
    for i, ref in enumerate((q, k, v, o)):
        ref[...] = j[i * h : (i + 1) * h]
    up_out[...] = up[...].astype(F32)
    down_out[...] = down[...].astype(F32)


def finish(joined, up, down):
    D, F = up.shape
    h = joined.shape[1] // 4
    rows = pick(D, 256)
    steps = D // rows
    tile = lambda n, c: pl.BlockSpec((n // steps, c), lambda i: (i, 0))
    ups = [tile(D, F), tile(F, D)]
    out, _ = launch(
        lambda hook, *refs: finish_body(h, *refs),
        "finish",
        (steps,),
        (joined, up, down),
        [tile(D, 4 * h), *ups],
        [jax.ShapeDtypeStruct((h, D), F32)] * 4 + [jax.ShapeDtypeStruct(a.shape, F32) for a in (up, down)],
        [pl.BlockSpec((h, rows), lambda i: (0, i))] * 4 + ups,
        [],
        cost(D * D, 6 * (4 * h * D + 2 * D * F)),
    )
    return out


def swap(a, axis, bit):
    return lax.ppermute(a, axis, [(i, i ^ bit) for i in range(lax.axis_size(axis))])


def segments(lengths):
    slots = lengths.shape[1]
    upto = lax.broadcasted_iota(jnp.int32, (1, slots, slots), 2) <= lax.broadcasted_iota(
        jnp.int32, (1, slots, slots), 1
    )
    ends = jnp.sum(jnp.where(upto, lengths[:, None, :], 0), axis=2)
    places = lax.broadcasted_iota(jnp.int32, (lengths.shape[0], L, slots), 1)
    return jnp.sum((ends[:, None, :] <= places).astype(jnp.int32), axis=2)


def merge(*dicts):
    return {k: v for d in dicts for k, v in d.items()}


def fused(x, cotangent, weights, gains, out_bias, valid, ids, mp):
    T, D = x.shape
    joined, wo, up, down, bias = weights
    h = wo.shape[0]
    hidden_units = up.shape[1]
    near, far, deep = ("dp", 1), ("dp", 2), ("dp", 4)

    J, W = Gather("j", D, 3 * h), Gather("w", h, D)
    U, V = Gather("u", D, hidden_units), Gather("v", hidden_units, D)
    both, four = (J, W), (J, W, U, V)
    steps = T // pick(T, 512, 384, 256, 128)
    t = Traffic(
        1,
        [CORE, Y, near, far],
        dict(j=joined, w=wo, u=up, v=down),
        merge(*[g.buffers("s", "q", "o", "p") for g in both], *[g.buffers("s", "q") for g in (U, V)]),
    )
    t.on(0, "start", *[g.start(s) for s in "sy" for g in both], J.wait("s"))
    t.on(0, "middle", *[g.wait("y") for g in both], *[g.start("a") for g in both])
    t.on(0, "middle", *[g.start(s) for s in "ys" for g in (U, V)])
    t.on(2, "start", *[g.wait("a") for g in both], *[g.start("b") for g in both])
    t.on(steps - 1, "end", *[g.wait("b") for g in both], *[g.start("p") for g in both])
    t.on(steps, "start", J.wait("p"))
    t.on(2 * steps - 1, "end", W.wait("s"), W.wait("p"), *[g.wait(s) for s in "ys" for g in (U, V)])
    (qkv, mixed, w, n1), got = attend(x, gains[0], *ids, h, [("j", "js"), ("jo", "jp")], t)
    wo_all = jnp.concatenate([wo, got["ws"], got["wo"], got["wp"]]).reshape(2, 2 * h, D)
    hidden, n2, att_square = project(x, gains[1], valid, mixed, wo_all)

    bias_o = swap(bias, "mp", 2)
    t = Traffic(
        2,
        [CORE, near, far],
        dict(uq=got["uq"], vq=got["vq"], u=up, v=down),
        merge(*[g.buffers("o", "p") for g in (U, V)]),
    )
    fs = hidden_units // pick(hidden_units, 256)
    t.on(0, "start", *[g.start("a") for g in (U, V)])
    t.on(2, "middle", *[g.wait("a") for g in (U, V)], *[g.start("b") for g in (U, V)])
    t.on(4, "start", *[g.wait("b") for g in (U, V)], *[g.start("p") for g in (U, V)])
    t.on(fs - 1, "end", *[g.wait("p") for g in (U, V)])
    own, far_weights = feed_forward(
        n2, cotangent, (bias, swap(bias, "mp", 1)), (up, got["us"]), (down, got["vs"]), t
    )

    a, b = (1, 2, 4), (2, 1, 4)
    U0, D0 = (
        Stream("u0", "u0a", "u0b", D, hidden_units, a, 2, joins="u1"),
        Stream("d0", "d0a", "d0b", hidden_units, D, b, 2, joins="d1"),
    )
    U1, D1 = Stream("u1", "u1a", "u1b", D, hidden_units, a, 2), Stream("d1", "d1a", "d1b", hidden_units, D, b, 2)
    half = D // 2
    att = [
        [
            Near(f"j{n}{m}", f"j{n}a", f"j{n}b", half, 4 * h, (a, b)[m], 2, m * half, None if n else f"j1{m}")
            for m in range(2)
        ]
        for n in range(2)
    ]
    first = (U0, D0)
    second = (U1, D1)
    t = Traffic(
        3,
        [CORE, near, far],
        dict(u0a=own[2], u0b=own[3], d0a=own[4], d0b=own[5]),
        merge(*[s.buffers("c", "s0", "r0", "s1", "r1") for s in first]),
    )
    t.on(0, "start", *[s.start_core for s in first])
    t.on(0, "middle", *[s.wait_core for s in first], *[s.start(0) for s in first])
    t.on(3, "start", *[s.wait(0) for s in first], *[s.start(1) for s in first])
    t.on(fs - 1, "end", *[s.wait(1) for s in first])
    other, left = feed_forward(
        n2,
        cotangent,
        (bias_o, swap(bias_o, "mp", 1)),
        (far_weights["uo"], far_weights["up"]),
        (far_weights["vo"], far_weights["vp"]),
        t,
    )
    feeds = [own, other]
    t = Traffic(
        7,
        [CORE],
        dict(u1b=other[3], d1b=other[5]),
        merge(*[s.buffers("c") for s in second]),
    )
    ls = T // pick(T, 256, 128)
    t.on(0, "start", *[s.start_core for s in second]).on(ls - 1, "end", *[s.wait_core for s in second])
    (out, low, sums), cores = middle(
        hidden, cotangent, gains[1], out_bias, valid, [f[0] for f in feeds], [f[1] for f in feeds], t
    )

    held = dict(u1a=other[2], d1a=other[4]) | cores
    early = dict(u0a=own[2], d0a=own[4]) | {k: v for k, v in left.items() if k[2] in "cr"}
    t = Traffic(
        4,
        [near, far],
        held | early,
        merge(*[s.buffers("s0", "r0", "s1", "r1") for s in second], *[s.buffers("e") for s in first]),
    )
    t.on(0, "start", *[s.start(0) for s in second])
    t.on(2 * steps - 2, "start", *[s.wait(0) for s in second], *[s.start(1) for s in second])
    t.on(2 * steps - 1, "start", *[s.keep for s in first])
    t.on(2 * steps - 1, "end", *[s.wait(1) for s in second])
    (dqkv,), arrived = attend_back(low, wo_all, qkv, *ids, t)

    t = Traffic(
        5, [Y], held | {k: v for k, v in arrived.items() if k[2] == "r"}, merge(*[s.buffers("e", "y") for s in second])
    )
    ws = D // pick(D, 256)
    t.on(0, "start", *[f for s in second for f in (s.keep, s.start_cross)])
    t.on(2 * ws - 1, "end", *[s.wait_cross for s in second])
    dw, crossed = weight_grads(n1, low, dqkv, mixed, t)

    units = jnp.zeros((1, lax.axis_size("mp") * hidden_units), F32)
    for change, part in ((0, own[6]), (1, own[7]), (2, other[6]), (3, other[7])):
        units = lax.dynamic_update_slice(units, part, (0, (mp ^ change) * hidden_units))
    count = jnp.where(jnp.arange(D) == 0, jnp.sum(valid), 0.0)[None]
    rows = jnp.concatenate([units.reshape(-1, D), sums[:4], att_square, count])
    n_rows = rows.shape[0] + 1
    tall = (n_rows + 7) // 8 * 8
    small = jnp.pad(rows, ((1, tall - n_rows), (0, 0)))

    held = dict(j0a=dw[0], j0b=dw[1], j1a=dw[2], j1b=dw[3], u1y=crossed["u1y"], d1y=crossed["d1y"], small=small)
    held |= dict(u0e=arrived["u0e"], d0e=arrived["d0e"])
    flat = [s for pair in att for s in pair]
    bits = [CORE, Y, near, far, deep]
    t = Traffic(
        6,
        bits,
        held,
        merge(*[s.buffers("s2", "r2", "f") for s in first], dict(joined=(D, 4 * h))),
        merge(
            *[s.scratch("m", "c", "s0", "r0", "s1", "r1") for s in flat],
            *[s.scratch("s2", "r2", "f") for s in att[0]],
            *[s.scratch("e", "y") for s in att[1]],
            {f"t{n}": pltpu.VMEM((tall, D), F32) for n in range(2 * len(bits) + 1)},
        ),
    )

    def load_small(t):
        return t.local("small", t.refs["small"], t.refs["t0"])

    def first_small(t):
        load_small(t).wait()
        t.refs["t0"][0:1, :] = t.refs["part"][...]

    def exchange_small(t, n):
        return t.copy(f"t{n}", t.refs[f"t{2 * n}"], t.refs[f"t{2 * n + 1}"], bits[n])

    def store_small(t):
        t.refs["summed"][...] = t.refs[f"t{2 * len(bits)}"][...]

    def start_small(n):
        return lambda t: exchange_small(t, n).start()

    def end_small(n):
        def action(t):
            exchange_small(t, n).wait()
            t.refs[f"t{2 * n + 2}"][...] = t.refs[f"t{2 * n}"][...] + t.refs[f"t{2 * n + 1}"][...]

        return action

    t.on(0, "start", *[s.start_core for s in flat], *[s.start_load for s in flat])
    t.on(0, "start", lambda t: load_small(t).start(), *[s.start(2) for s in first])
    t.on(1, "start", *[s.wait_load for s in flat], *[s.wait_core for s in flat], *[s.start(0) for s in flat])
    end = [first_small, start_small(0)]
    end += [f for s in first for f in (s.wait(2), s.total, s.start_spread(2))]
    end += [end_small(0), start_small(1)]
    end += [s.wait(0) for s in flat] + [s.start(1) for s in (*att[1], *att[0])]
    end += [end_small(1), start_small(2)]
    end += [f for s in first for f in (s.wait_spread(2), s.start_spread(1))]
    end += [f for s in att[1] for f in (s.wait(1), s.keep, s.start_cross)] + [s.wait(1) for s in att[0]]
    end += [end_small(2), start_small(3)]
    end += [s.wait_cross for s in att[1]] + [s.start(2) for s in att[0]]
    end += [f for s in first for f in (s.wait_spread(1), s.start_spread(0))]
    end += [f for s in att[0] for f in (s.wait(2), s.total, s.start_spread(2))]
    end += [end_small(3), start_small(4)]
    for j in (2, 1):
        end += [f for s in att[0] for f in (s.wait_spread(j), s.start_spread(j - 1))]
    end += [end_small(4), store_small]
    end += [f for s in att[0] for f in (s.wait_spread(0), s.start_store)]
    end += [s.wait_spread(0) for s in first] + [s.wait_store for s in att[0]]
    t.on(ls - 1, "end", *end)
    (input_gradient, _, summed), done = last(x, gains[0], low, dqkv, w, t, tall)
    return (out, input_gradient, done["joined"], done["u0f"], done["d0f"]), summed


def gathered(x, cotangent, weights, gains, out_bias, valid, ids):
    D = x.shape[1]
    joined, wo, up, down, bias = weights
    every = lambda a, d: lax.all_gather(a, "mp", axis=d, tiled=True)
    two = lambda a, d: tuple(jnp.split(every(a, d), 2, axis=d))
    sides = [jnp.concatenate(p, axis=1) for p in zip(*(two(a, 1) for a in jnp.split(joined, 3, axis=1)))]
    plain = Traffic(0, [], dict(a=sides[0], b=sides[1]), {})
    (qkv, mixed, w, n1), _ = attend(x, gains[0], *ids, sides[0].shape[1] // 3, [("a", "b")], plain)
    wo_all = every(wo, 0)[None]
    hidden, n2, att_square = project(x, gains[1], valid, mixed, wo_all)
    f, _ = feed_forward(n2, cotangent, two(bias, 1), two(up, 1), two(down, 0))
    (out, low, sums), _ = middle(hidden, cotangent, gains[1], out_bias, valid, [f[0]], [f[1]])
    (dqkv,), _ = attend_back(low, wo_all, qkv, *ids, None)
    dw, _ = weight_grads(n1, low, dqkv, mixed, None)
    (input_gradient, first_part), _ = last(x, gains[0], low, dqkv, w)

    def total(pair, d):
        part = lax.psum_scatter(jnp.concatenate(pair, axis=d), "mp", scatter_dimension=d, tiled=True)
        return lax.psum(part, "dp")

    cut = [jnp.split(a, 4, axis=1) for a in dw]
    joined_total = jnp.concatenate([total(pair, 1) for pair in zip(*cut)], axis=1)
    grads = (out, input_gradient, joined_total, total(f[2:4], 1), total(f[4:6], 0))
    units = jnp.concatenate(f[6:], axis=1).reshape(-1, D)
    count = jnp.where(jnp.arange(D) == 0, jnp.sum(valid), 0.0)[None]
    return grads, lax.psum(jnp.concatenate([first_part, units, sums[:4], att_square, count]), ("dp", "mp"))


def per_device(
    tokens,
    lengths,
    cotangent,
    query_weight,
    key_weight,
    value_weight,
    out_weight,
    up_weight,
    hidden_bias,
    down_weight,
    output_bias,
    first_gain,
    second_gain,
):
    T, D = tokens.shape
    rows = T // L
    mp = lax.axis_index("mp")
    segment_ids = segments(lax.dynamic_slice_in_dim(lengths, mp * rows, rows))
    valid = (segment_ids < SLOTS).reshape(-1, 1).astype(F32)
    ids = (segment_ids + L * lax.broadcasted_iota(jnp.int32, (rows, L), 0)).reshape(-1)
    ids = (ids[:, None], ids[None, :])
    joined = jnp.concatenate([query_weight, key_weight, value_weight], axis=1)
    bias = hidden_bias.reshape(1, -1)
    gains = (first_gain.reshape(1, -1), second_gain.reshape(1, -1))
    weights = (joined, out_weight, up_weight, down_weight, bias)
    rest = (gains, output_bias.reshape(1, -1), valid, ids)
    if lax.axis_size("mp") == 4 and lax.axis_size("dp") == 8:
        grads, small = fused(tokens, cotangent, weights, *rest, mp)
    else:
        grads, small = gathered(tokens, cotangent, weights, *rest)
    out, input_gradient, joined_total, up_total, down_total = grads
    n = hidden_bias.shape[0] * lax.axis_size("mp") // D + 1
    squares = jnp.sum(small[n + 2 : n + 6], axis=1)
    mean = lambda i: jnp.sqrt(squares[i] / (squares[3] * D))
    q, k, v, o, up_total, down_total = finish(joined_total, up_total, down_total)
    return (
        out,
        input_gradient,
        q.T,
        k.T,
        v.T,
        o,
        up_total,
        lax.dynamic_slice_in_dim(small[1:n].reshape(-1), mp * bias.shape[1], bias.shape[1]),
        down_total,
        small[n + 1],
        small[0],
        small[n],
        jnp.stack([mean(2), mean(0), mean(1)]),
    )


def solution(mesh):
    return jax.shard_map(
        per_device,
        mesh=mesh,
        in_specs=(
            P(("dp", "mp"), None),
            P("dp", None),
            P(("dp", "mp"), None),
            P(None, "mp"),
            P(None, "mp"),
            P(None, "mp"),
            P("mp", None),
            P(None, "mp"),
            P("mp"),
            P("mp", None),
            P(),
            P(),
            P(),
        ),
        out_specs=(
            P(("dp", "mp"), None),
            P(("dp", "mp"), None),
            P(None, "mp"),
            P(None, "mp"),
            P(None, "mp"),
            P("mp", None),
            P(None, "mp"),
            P("mp"),
            P("mp", None),
            P(),
            P(),
            P(),
            P(),
        ),
        check_vma=False,
    )
```

```python
import functools
import math

import jax
import jax.numpy as jnp
from jax import lax
from jax.experimental import pallas as pl
from jax.experimental.pallas import tpu as pltpu
from jax.sharding import PartitionSpec as P

HD = 80
L = 64
SLOTS = 32
LANES = 128
EPSILON = 1e-06
MASKED = -1e30
F32 = jnp.float32
BF = jnp.bfloat16
NN = (((1,), (0,)), ((), ()))
NT = (((1,), (1,)), ((), ()))
TN = (((0,), (0,)), ((), ()))
VMEM_BYTES = 60 << 20


def dot(a, b, dims=NN):
    return lax.dot_general(a, b, dims, preferred_element_type=F32)


def pick(n, *sizes):
    return next((s for s in sizes if n % s == 0), n)


def whole(shape):
    return pl.BlockSpec(shape, lambda *i: (0,) * len(shape), pipeline_mode=pl.Buffered(1))


def cost(flops, nbytes, exps=0):
    return pl.CostEstimate(flops=int(flops), bytes_accessed=int(nbytes), transcendentals=int(exps))


def row_sum(x):
    return jnp.sum(x, axis=0, keepdims=True)


def rms(x):
    return lax.rsqrt(jnp.mean(x * x, axis=1, keepdims=True) + EPSILON)


MESH = pl.DeviceIdType.MESH
CORE, Y = ("mp", 1), ("mp", 2)


def bit_of(axis, bit):
    return lax.rem(lax.axis_index(axis) // bit, 2)


def flip(axis, bit):
    return {axis: lax.axis_index(axis) + bit - 2 * bit * bit_of(axis, bit)}


class Traffic:
    def __init__(self, number, partners, arrays, buffers, scratch=None):
        self.number, self.partners = number, partners
        self.arrays, self.buffers, self.scratch = arrays, buffers, scratch or {}
        self.events, self.slots, self.refs = [], {}, {}

    def on(self, step, place, *actions):
        self.events += [(step, place, f) for f in actions]
        return self

    def run(self, step, place):
        for at, where, action in self.events:
            if where == place:
                pl.when(step == at)(functools.partial(action, self))

    def greet(self):
        sem = pltpu.get_barrier_semaphore()
        for p in self.partners:
            pl.semaphore_signal(sem, inc=1, device_id=flip(*p), device_id_type=MESH)
        pl.semaphore_wait(sem, len(self.partners))

    def copy(self, name, src, dst, to):
        i = self.slots.setdefault(name, len(self.slots))
        return pltpu.make_async_remote_copy(
            src_ref=src,
            dst_ref=dst,
            send_sem=self.sems.at[0, i],
            recv_sem=self.sems.at[1, i],
            device_id=flip(*to),
            device_id_type=MESH,
        )

    def local(self, name, src, dst):
        i = self.slots.setdefault(name, len(self.slots))
        return pltpu.make_async_copy(src, dst, self.sems.at[0, i])


COPIES = 48


def launch(body, name, grid, args, in_specs, outs, out_specs, scratch, cost_estimate, traffic=None):
    n_args, n_outs = len(args), len(outs)
    names, arrays, buffers = [], [], []
    if traffic is not None:
        names = [*traffic.arrays, *traffic.buffers]
        arrays = list(traffic.arrays.values())
        buffers = [jax.ShapeDtypeStruct(s, BF) for s in traffic.buffers.values()]
        names += [*traffic.scratch]
        scratch = [*scratch, *traffic.scratch.values(), pltpu.SemaphoreType.DMA((2, COPIES))]

    def kernel(*refs):
        hook = lambda place: None
        inputs, refs = refs[:n_args], refs[n_args:]
        moved, refs = refs[: len(arrays)], refs[len(arrays) :]
        results, refs = refs[:n_outs], refs[n_outs:]
        landing, refs = refs[: len(buffers)], refs[len(buffers) :]
        if traffic is not None:
            step = pl.program_id(0)
            for d in range(1, len(grid)):
                step = step * grid[d] + pl.program_id(d)
            traffic.sems, refs = refs[-1], refs[:-1]
            n = len(refs) - len(traffic.scratch)
            traffic.refs = dict(zip(names, [*moved, *landing, *refs[n:]]))
            refs = refs[:n]
            if traffic.partners:
                pl.when(step == 0)(traffic.greet)
            hook = lambda place: traffic.run(step, place)
        body(hook, *inputs, *results, *refs)

    anywhere = pl.BlockSpec(memory_space=pl.ANY)
    out = pl.pallas_call(
        kernel,
        grid=grid,
        in_specs=[*in_specs, *[anywhere] * len(arrays)],
        out_specs=[*out_specs, *[anywhere] * len(buffers)],
        out_shape=[*outs, *buffers],
        scratch_shapes=scratch,
        compiler_params=pltpu.CompilerParams(
            vmem_limit_bytes=VMEM_BYTES,
            **({} if traffic is None or not traffic.partners else dict(collective_id=traffic.number, has_side_effects=True)),
        ),
        cost_estimate=cost_estimate,
        name=name,
    )(*args, *arrays)
    return out[:n_outs], dict(zip(names[len(arrays) : len(arrays) + len(buffers)], out[n_outs:]))


def add_rows(sources, target, rows):
    columns = target.shape[1]
    tile = pl.BlockSpec((rows // 2 if rows // 2 % 16 == 0 else rows, columns), lambda i: (i, 0))

    def body(*refs):
        refs[-1][...] = sum(r[...].astype(F32) for r in refs[:-1]).astype(BF)

    pltpu.emit_pipeline(
        body, grid=(rows // tile.block_shape[0],), in_specs=[tile] * len(sources), out_specs=[tile]
    )(*[r.at[pl.ds(pl.multiple_of(o, 16), rows), :] for r, o in sources], target)


class Stream:
    def __init__(self, tag, mine, theirs, rows, columns, order, cut, base=0, joins=None):
        self.tag, self.mine, self.theirs, self.base = tag, mine, theirs, base
        self.rows, self.columns, self.order = rows, columns, order
        self.cut, self.joins = cut, joins

    def name(self, what):
        return self.tag + what

    def buffers(self, *what):
        size = lambda w: self.rows if w[0] in "cf" else self.rows >> self.cut if w[0] in "ey" else self.rows >> (int(w[1]) + 1)
        return {self.name(w): (size(w), self.columns) for w in what}

    def place(self, stages):
        first, n = 0, self.rows
        for bit in self.order[:stages]:
            n //= 2
            first = first + bit_of("dp", bit) * n
        return first, n

    def sources(self, t, first, arrived):
        out = [(t.refs[self.mine], first + self.base), (t.refs[self.name("c")], first)]
        for j in range(arrived):
            out.append((t.refs[self.name(f"r{j}")], first - self.place(j + 1)[0]))
        if self.joins is not None and arrived >= self.cut:
            out.append((t.refs[self.joins + "y"], first - self.place(self.cut)[0]))
        return out

    def core(self, t):
        src = t.refs[self.theirs].at[pl.ds(self.base, self.rows), :]
        return t.copy(self.name("c"), src, t.refs[self.name("c")], CORE)

    def start_core(self, t):
        self.core(t).start()

    def wait_core(self, t):
        self.core(t).wait()

    def exchange(self, t, j):
        return t.copy(self.name(f"r{j}"), t.refs[self.name(f"s{j}")], t.refs[self.name(f"r{j}")], ("dp", self.order[j]))

    def start(self, j):
        def action(t):
            first, n = self.place(j)
            n //= 2
            sent = first + (1 - bit_of("dp", self.order[j])) * n
            add_rows(self.sources(t, sent, j), t.refs[self.name(f"s{j}")], n)
            self.exchange(t, j).start()

        return action

    def wait(self, j):
        return lambda t: self.exchange(t, j).wait()

    def keep(self, t):
        first, n = self.place(self.cut)
        add_rows(self.sources(t, first, self.cut), t.refs[self.name("e")], n)

    def cross(self, t):
        return t.copy(self.name("y"), t.refs[self.name("e")], t.refs[self.name("y")], Y)

    def start_cross(self, t):
        self.cross(t).start()

    def wait_cross(self, t):
        self.cross(t).wait()

    def total(self, t):
        first, n = self.place(len(self.order))
        target = t.refs[self.name("f")].at[pl.ds(pl.multiple_of(first, 16), n), :]
        add_rows(self.sources(t, first, len(self.order)), target, n)

    def spread(self, t, j):
        first, n = self.place(j + 1)
        part = t.refs[self.name("f")].at[pl.ds(pl.multiple_of(first, 16), n), :]
        return t.copy(self.name(f"f{j}"), part, part, ("dp", self.order[j]))

    def start_spread(self, j):
        return lambda t: self.spread(t, j).start()

    def wait_spread(self, j):
        return lambda t: self.spread(t, j).wait()


def sum_rows(sources, target, rows):
    step = pick(rows, 80, 64, 32, 16)

    def one(i, _):
        part = lambda o: pl.ds(pl.multiple_of(o + i * step, 16), step)
        target[part(0), :] = sum(r[part(o), :].astype(F32) for r, o in sources).astype(BF)
        return 0

    lax.fori_loop(0, rows // step, one, 0)


class Near(Stream):
    def scratch(self, *what):
        size = lambda w: self.rows if w == "m" else self.buffers(w)[self.name(w)][0]
        return {self.name(w): pltpu.VMEM((size(w), self.columns), BF) for w in what}

    def sources(self, t, first, arrived):
        out = super().sources(t, first, arrived)
        return [(t.refs[self.name("m")], first), *out[1:]]

    def load(self, t):
        src = t.refs[self.mine].at[pl.ds(self.base, self.rows), :]
        return t.local(self.name("m"), src, t.refs[self.name("m")])

    def start_load(self, t):
        self.load(t).start()

    def wait_load(self, t):
        self.load(t).wait()

    def start(self, j):
        def action(t):
            first, n = self.place(j)
            n //= 2
            sent = first + (1 - bit_of("dp", self.order[j])) * n
            sum_rows(self.sources(t, sent, j), t.refs[self.name(f"s{j}")], n)
            self.exchange(t, j).start()

        return action

    def keep(self, t):
        first, n = self.place(self.cut)
        sum_rows(self.sources(t, first, self.cut), t.refs[self.name("e")], n)

    def total(self, t):
        first, n = self.place(len(self.order))
        target = t.refs[self.name("f")].at[pl.ds(pl.multiple_of(first, 16), n), :]
        sum_rows(self.sources(t, first, len(self.order)), target, n)

    def store(self, t):
        out = t.refs["joined"].at[pl.ds(self.base, self.rows), :]
        return t.local(self.name("o"), t.refs[self.name("f")], out)

    def start_store(self, t):
        self.store(t).start()

    def wait_store(self, t):
        self.store(t).wait()


class Gather:
    def __init__(self, tag, rows, columns):
        self.tag, self.rows, self.columns = tag, rows, columns
        self.n = rows // 4

    def buffers(self, *what):
        return {self.tag + w: (self.n if w == "q" else self.rows, self.columns) for w in what}

    def quarter(self, ref, flip_x=0, flip_z=0, first=0, rows=None):
        x, z = bit_of("dp", 1), bit_of("dp", 2)
        x, z = (1 - x if flip_x else x), (1 - z if flip_z else z)
        start = pl.multiple_of((2 * z + x) * self.n + first, 16)
        return ref.at[pl.ds(start, self.n if rows is None else rows), :]

    def copies(self, t, step):
        own, o = t.refs[self.tag], t.refs.get(self.tag + "o")
        name = self.tag + step
        if step == "s":
            return [t.copy(name, own, t.refs[name], CORE)]
        if step == "y":
            return [t.copy(name, self.quarter(own), t.refs[self.tag + "q"], Y)]
        if step == "a":
            q = t.refs[self.tag + "q"]
            return [t.copy(name + str(b), q, self.quarter(o), ("dp", b)) for b in (1, 2)]
        if step == "b":
            top = (self.n // 2 + 15) // 16 * 16
            to_x = self.quarter(o, flip_z=1, rows=top)
            to_z = self.quarter(o, flip_x=1, first=top, rows=self.n - top)
            return [t.copy(name + "1", to_x, to_x, ("dp", 1)), t.copy(name + "2", to_z, to_z, ("dp", 2))]
        return [t.copy(name, o, t.refs[self.tag + "p"], CORE)]

    def start(self, step):
        def action(t):
            for c in self.copies(t, step):
                c.start()
            if step == "a":
                add_rows([(t.refs[self.tag + "q"], 0)], self.quarter(t.refs[self.tag + "o"]), self.n)

        return action

    def wait(self, step):
        def action(t):
            for c in self.copies(t, step):
                c.wait()

        return action


def windows(C):
    out = []
    for h in range(C // HD):
        w = min(LANES * (HD * h // LANES), C - 2 * LANES)
        out.append((w, HD * h - w))
    return out


def head_masks(C):
    lane = lax.broadcasted_iota(jnp.int32, (1, 2 * LANES), 1)
    return [jnp.where((lane >= lo) & (lane < lo + HD), 1.0, 0.0).astype(BF) for _, lo in windows(C)]


def softmaxes(qs, ks, allowed):
    s = [jnp.where(allowed, dot(q, k, NT) * (1.0 / math.sqrt(HD)), MASKED) for q, k in zip(qs, ks)]
    e = [jnp.exp(x - jnp.max(x, axis=1, keepdims=True)) for x in s]
    return [x * (1.0 / jnp.sum(x, axis=1, keepdims=True)) for x in e]


def allow(idc, idr, s, B):
    causal = lax.broadcasted_iota(jnp.int32, (B, B), 1) <= lax.broadcasted_iota(
        jnp.int32, (B, B), 0
    )
    return (idc[s, :] == idr[:, s]) & causal


def put(tiles, w, val):
    for n in range(2):
        t = w // LANES + n
        part = val[:, n * LANES : (n + 1) * LANES]
        tiles[t] = part if tiles[t] is None else tiles[t] + part


def fwd_body(B, C, pairs, traffic, hook, x, gain, idc, idr, qkv, mixed, w, n1, ab, sem):
    group = pl.program_id(0)
    tt = x.shape[0]
    first = pl.program_id(1) == 0
    hook("start")
    h = C // 2
    for g, pair in enumerate(pairs):

        @pl.when(first & (group == g))
        def _():
            for side in range(2):
                c = pltpu.make_async_copy(traffic.refs[pair[side]], ab, sem)
                c.start()
                c.wait()
                a = ab[...]
                for i in range(3):
                    w[0, :, i * C + side * h : i * C + (side + 1) * h] = a[:, i * h : (i + 1) * h]

    t = x[...].astype(F32)
    normed = (t * rms(t) * gain[...].astype(F32)).astype(BF)

    @pl.when(group == 0)
    def _():
        n1[...] = normed

    qkv[0] = dot(normed, w[0]).astype(BF)
    hook("middle")
    masks = head_masks(C)
    wins = [w0 for w0, _ in windows(C)]

    def block(i, _):
        s = pl.ds(pl.multiple_of(i * B, B), B)
        ok = allow(idc, idr, s, B)
        tiles = [None] * (C // LANES)
        cut = lambda n, w0: qkv[0, s, n * C + w0 : n * C + w0 + 2 * LANES]
        for g in range(0, len(wins), 8):
            hs = range(g, min(g + 8, len(wins)))
            p = softmaxes([cut(0, wins[h]) * masks[h] for h in hs], [cut(1, wins[h]) for h in hs], ok)
            o = [dot(a.astype(BF), cut(2, wins[h]) * masks[h]) for a, h in zip(p, hs)]
            for h, a in zip(hs, o):
                put(tiles, wins[h], a)
        mixed[0, s, :] = jnp.concatenate(tiles, axis=1).astype(BF)
        return 0

    lax.fori_loop(0, tt // B, block, 0)
    hook("end")


def attend(x, gain, idc, idr, h, pairs, traffic):
    T, D = x.shape
    C, G = 2 * h, len(pairs)
    tt, B = pick(T, 512, 384, 256, 128), 128
    by_group = lambda c: pl.BlockSpec((1, tt, c), lambda g, i: (g, i, 0))
    return launch(
        functools.partial(fwd_body, B, C, pairs, traffic),
        "attend",
        (G, T // tt),
        (x, gain, idc, idr),
        [
            pl.BlockSpec((tt, D), lambda g, i: (i, 0)),
            whole((1, D)),
            pl.BlockSpec((tt, 1), lambda g, i: (i, 0)),
            pl.BlockSpec((1, tt), lambda g, i: (0, i)),
        ],
        [
            jax.ShapeDtypeStruct((G, T, 3 * C), BF),
            jax.ShapeDtypeStruct((G, T, C), BF),
            jax.ShapeDtypeStruct((G, D, 3 * C), BF),
            jax.ShapeDtypeStruct((T, D), BF),
        ],
        [
            by_group(3 * C),
            by_group(C),
            pl.BlockSpec((1, D, 3 * C), lambda g, i: (g, 0, 0)),
            pl.BlockSpec((tt, D), lambda g, i: (jnp.where(g == 0, i, T // tt - 1), 0)),
        ],
        [pltpu.VMEM((D, 3 * h), BF), pltpu.SemaphoreType.DMA],
        cost(9 * T * D * C * G, 2 * G * (T * D + 4 * C * D + 5 * T * C), G * T * B * C // HD),
        traffic,
    )


def back_body(B, C, hook, hg, wo, qkv, idc, idr, dqkv, dmix):
    tt = hg.shape[0]
    scale = 1.0 / math.sqrt(HD)
    hook("start")
    dmix[...] = dot(hg[...], wo[0], NT).astype(BF)
    masks = head_masks(C)
    wins = [w0 for w0, _ in windows(C)]

    def block(i, _):
        s = pl.ds(pl.multiple_of(i * B, B), B)
        ok = allow(idc, idr, s, B)
        dq = [None] * (C // LANES)
        dk, dv = list(dq), list(dq)
        cut = lambda n, w0: qkv[0, s, n * C + w0 : n * C + w0 + 2 * LANES]
        for g in range(0, len(wins), 8):
            hs = range(g, min(g + 8, len(wins)))
            q = [cut(0, wins[h]) * masks[h] for h in hs]
            gm = [dmix[s, wins[h] : wins[h] + 2 * LANES] * masks[h] for h in hs]
            p = softmaxes(q, [cut(1, wins[h]) for h in hs], ok)
            dp = [dot(a, cut(2, wins[h]), NT) for a, h in zip(gm, hs)]
            ds = [(a * (b - jnp.sum(a * b, axis=1, keepdims=True))).astype(BF) for a, b in zip(p, dp)]
            for h, a, b, c, d in zip(hs, p, gm, ds, q):
                put(dv, wins[h], dot(a.astype(BF), b, TN))
                put(dk, wins[h], dot(c, d, TN))
                put(dq, wins[h], dot(c, cut(1, wins[h]) * masks[h]))
        for n, tiles in enumerate((dq, dk, dv)):
            a = jnp.concatenate(tiles, axis=1)
            dqkv[0, s, n * C : (n + 1) * C] = (a if n == 2 else a * scale).astype(BF)
        return 0

    lax.fori_loop(0, tt // B, block, 0)
    hook("end")


def attend_back(hg, wo, qkv, idc, idr, traffic):
    T, D = hg.shape
    G, C, _ = wo.shape
    tt, B = pick(T, 512, 384, 256, 128), 128
    by_group = pl.BlockSpec((1, tt, 3 * C), lambda g, i: (g, i, 0))
    return launch(
        functools.partial(back_body, B, C),
        "attend_back",
        (G, T // tt),
        (hg, wo, qkv, idc, idr),
        [
            pl.BlockSpec((tt, D), lambda g, i: (i, 0)),
            pl.BlockSpec((1, C, D), lambda g, i: (g, 0, 0)),
            by_group,
            pl.BlockSpec((tt, 1), lambda g, i: (i, 0)),
            pl.BlockSpec((1, tt), lambda g, i: (0, i)),
        ],
        [jax.ShapeDtypeStruct((G, T, 3 * C), BF)],
        [by_group],
        [pltpu.VMEM((tt, C), BF)],
        cost(12 * T * D * C * G, 2 * G * (T * D + C * D + 6 * T * C), G * T * B * C // HD),
        traffic,
    )


def weight_body(C, G, hook, n1, low, dqkv, mixed, *dw):
    hook("start")
    h = C // 2
    u = dot(n1[...], dqkv[0], TN).astype(BF)
    o = dot(low[...], mixed[0], TN).astype(BF)
    for g in range(G):

        @pl.when(pl.program_id(0) == g)
        def _():
            for side in range(2):
                to = dw[2 * g + side]
                for i in range(3):
                    to[:, i * h : (i + 1) * h] = u[:, i * C + side * h : i * C + (side + 1) * h]
                to[:, 3 * h : 4 * h] = o[:, side * h : (side + 1) * h]

    hook("end")


def weight_grads(n1, low, dqkv, mixed, traffic):
    T, D = n1.shape
    G, _, C = mixed.shape
    rows = pick(D, 256)
    steps = D // rows

    def out(g):
        place = lambda n, i: (jnp.where(n == g, i, jnp.where(n < g, 0, steps - 1)), 0)
        return pl.BlockSpec((rows, 2 * C), place)

    columns = pl.BlockSpec((T, rows), lambda g, i: (0, i))
    return launch(
        functools.partial(weight_body, C, G),
        "weight_grads",
        (G, steps),
        (n1, low, dqkv, mixed),
        [
            columns,
            columns,
            pl.BlockSpec((1, T, 3 * C), lambda g, i: (g, 0, 0)),
            pl.BlockSpec((1, T, C), lambda g, i: (g, 0, 0)),
        ],
        [jax.ShapeDtypeStruct((D, 2 * C), BF)] * (2 * G),
        [out(g) for g in range(G) for _ in range(2)],
        [],
        cost(8 * T * D * C * G, 2 * G * (2 * T * D + 4 * T * C + 4 * D * C)),
        traffic,
    )


def project_body(x, gain, valid, mixed, wo, hidden, n2, square):
    @pl.when(pl.program_id(0) == 0)
    def _():
        square[...] = jnp.zeros_like(square)

    a = sum(dot(mixed[g], wo[g]) for g in range(wo.shape[0]))
    h = x[...].astype(F32) + a
    hidden[...] = h
    n2[...] = (h * rms(h) * gain[...].astype(F32)).astype(BF)
    square[...] += row_sum(valid[...] * a * a)


def project(x, gain, valid, mixed, wo):
    T, D = x.shape
    G, C, _ = wo.shape
    tt = pick(T, 256, 128)
    tile = lambda c: pl.BlockSpec((tt, c), lambda i: (i, 0))
    out, _ = launch(
        lambda hook, *refs: project_body(*refs),
        "project",
        (T // tt,),
        (x, gain, valid, mixed, wo),
        [tile(D), whole((1, D)), tile(1), pl.BlockSpec((G, tt, C), lambda i: (0, i, 0)), whole(wo.shape)],
        [jax.ShapeDtypeStruct((T, D), F32), jax.ShapeDtypeStruct((T, D), BF), jax.ShapeDtypeStruct((1, D), F32)],
        [tile(D), tile(D), pl.BlockSpec((1, D), lambda i: (0, 0))],
        [],
        cost(2 * T * D * D, 12 * T * D),
    )
    return out


def feed_body(
    hook, n2, g, hba, hbb, upa, upb, downa, downb, feed, n2g, dua, dub, dda, ddb, ba, bb, acc_f, acc_n, act, pg, wu, wd
):
    step = pl.program_id(0)
    T, D = n2.shape
    ft = hba.shape[1]
    chunk = pick(T, 768, 384, 128)
    hook("start")

    @pl.when(step == 0)
    def _():
        acc_f[...] = jnp.zeros_like(acc_f)
        acc_n[...] = jnp.zeros_like(acc_n)

    wu[:, :ft], wu[:, ft:] = upa[...], upb[...]
    wd[:ft, :], wd[ft:, :] = downa[...], downb[...]
    hb = jnp.concatenate([hba[...], hbb[...]], axis=1).astype(F32)
    ba[...] = jnp.zeros_like(ba)
    bb[...] = jnp.zeros_like(bb)

    def one(i, _):
        s = pl.ds(pl.multiple_of(i * chunk, chunk), chunk)
        p = dot(n2[s, :], wu[...]) + hb
        ag = dot(g[s, :], wd[...], NT)
        sg = 0.5 * jnp.tanh(0.5 * p) + 0.5
        ps = p * sg
        a = ps.astype(BF)
        q = (ag * (sg + ps * (1.0 - sg))).astype(BF)
        act[s, :] = a
        pg[s, :] = q
        b = row_sum(q.astype(F32))
        ba[...] += b[:, :ft]
        bb[...] += b[:, ft:]
        acc_f[s, :] += dot(a, wd[...])
        acc_n[s, :] += dot(q, wu[...], NT)
        return 0

    lax.fori_loop(0, T // chunk, one, 0)
    hook("middle")
    u = dot(n2[...], pg[...], TN).astype(BF)
    dua[...], dub[...] = u[:, :ft], u[:, ft:]
    d = dot(act[...], g[...], TN).astype(BF)
    dda[...], ddb[...] = d[:ft], d[ft:]

    @pl.when(step == pl.num_programs(0) - 1)
    def _():
        feed[...] = acc_f[...].astype(BF)
        n2g[...] = acc_n[...].astype(BF)

    hook("end")


def feed_forward(n2, g, biases, ups, downs, traffic=None):
    T, D = n2.shape
    F = biases[0].shape[1]
    ft = pick(F, 256)
    up = pl.BlockSpec((D, ft), lambda f: (0, f))
    down = pl.BlockSpec((ft, D), lambda f: (f, 0))
    bias = pl.BlockSpec((1, ft), lambda f: (0, f))
    return launch(
        feed_body,
        "feed_forward",
        (F // ft,),
        (n2, g, *biases, *ups, *downs),
        [whole((T, D)), whole((T, D)), bias, bias, up, up, down, down],
        [jax.ShapeDtypeStruct((T, D), BF)] * 2
        + [jax.ShapeDtypeStruct((D, F), BF)] * 2
        + [jax.ShapeDtypeStruct((F, D), BF)] * 2
        + [jax.ShapeDtypeStruct((1, F), F32)] * 2,
        [whole((T, D)), whole((T, D)), up, up, down, down, bias, bias],
        [
            pltpu.VMEM((T, D), F32),
            pltpu.VMEM((T, D), F32),
            pltpu.VMEM((T, 2 * ft), BF),
            pltpu.VMEM((T, 2 * ft), BF),
            pltpu.VMEM((D, 2 * ft), BF),
            pltpu.VMEM((2 * ft, D), BF),
        ],
        cost(24 * T * D * F, 16 * T * D + 16 * D * F, 2 * T * F),
        traffic,
    )


def middle_body(n, hook, *refs):
    hook("start")
    hidden, g, gain, out_bias, valid = refs[:5]
    feeds, grads = refs[5 : 5 + n], refs[5 + n : 5 + 2 * n]
    out, low, sums = refs[5 + 2 * n :]

    @pl.when(pl.program_id(0) == 0)
    def _():
        sums[...] = jnp.zeros_like(sums)

    h, go = hidden[...], g[...].astype(F32)
    f = sum(a[...].astype(F32) for a in feeds) + out_bias[...].astype(F32)
    ng = sum(a[...].astype(F32) for a in grads)
    result = h + f
    out[...] = result.astype(BF)
    r2 = rms(h)
    wg = ng * gain[...].astype(F32)
    inner = jnp.sum(wg * h, axis=1, keepdims=True)
    low[...] = (go + wg * r2 - h * (r2 * r2 * r2 * inner / h.shape[1])).astype(BF)
    v = valid[...]
    for i, a in enumerate((ng * h * r2, go, v * f * f, v * result * result)):
        sums[i : i + 1, :] += row_sum(a)
    hook("end")


def middle(hidden, g, gain, out_bias, valid, feeds, grads, traffic=None):
    T, D = hidden.shape
    tt = pick(T, 256, 128)
    tile = lambda c: pl.BlockSpec((tt, c), lambda i: (i, 0))
    n = len(feeds)
    return launch(
        functools.partial(middle_body, n),
        "middle",
        (T // tt,),
        (hidden, g, gain, out_bias, valid, *feeds, *grads),
        [tile(D), tile(D), whole((1, D)), whole((1, D)), tile(1)] + [tile(D)] * (2 * n),
        [jax.ShapeDtypeStruct((T, D), BF), jax.ShapeDtypeStruct((T, D), BF), jax.ShapeDtypeStruct((8, D), F32)],
        [tile(D), tile(D), pl.BlockSpec((8, D), lambda i: (0, 0))],
        [],
        cost(40 * T * D, (10 + 4 * n) * T * D),
        traffic,
    )


def last_body(traffic, hook, x, gain, low, dqkv, w, out, part, summed=None):
    hook("start")

    @pl.when(pl.program_id(0) == 0)
    def _():
        part[...] = jnp.zeros_like(part)

    ng = sum(dot(dqkv[g], w[g], NT) for g in range(w.shape[0]))
    t = x[...].astype(F32)
    r1 = rms(t)
    wg = ng * gain[...].astype(F32)
    inner = jnp.sum(wg * t, axis=1, keepdims=True)
    out[...] = low[...].astype(F32) + wg * r1 - t * (r1 * r1 * r1 * inner / t.shape[1])
    part[...] += row_sum(ng * t * r1)
    if traffic is not None:
        traffic.refs["part"], traffic.refs["summed"] = part, summed
    hook("end")


def last(x, gain, low, dqkv, w, traffic=None, small=None):
    T, D = x.shape
    G, _, K = w.shape
    rows = [] if small is None else [small]
    tt = pick(T, 256, 128)
    tile = lambda c: pl.BlockSpec((tt, c), lambda i: (i, 0))
    return launch(
        functools.partial(last_body, traffic),
        "last",
        (T // tt,),
        (x, gain, low, dqkv, w),
        [tile(D), whole((1, D)), tile(D), pl.BlockSpec((G, tt, K), lambda i: (0, i, 0)), whole(w.shape)],
        [jax.ShapeDtypeStruct((n, D), F32) for n in (T, 1, *rows)],
        [tile(D), *[pl.BlockSpec((n, D), lambda i: (0, 0)) for n in (1, *rows)]],
        [],
        cost(6 * T * D * D, 8 * T * D + 6 * D * D),
        traffic,
    )


def finish_body(h, joined, up, down, q, k, v, o, up_out, down_out):
    j = joined[...].astype(F32).T
    for i, ref in enumerate((q, k, v, o)):
        ref[...] = j[i * h : (i + 1) * h]
    up_out[...] = up[...].astype(F32)
    down_out[...] = down[...].astype(F32)


def finish(joined, up, down):
    D, F = up.shape
    h = joined.shape[1] // 4
    rows = pick(D, 256)
    steps = D // rows
    tile = lambda n, c: pl.BlockSpec((n // steps, c), lambda i: (i, 0))
    ups = [tile(D, F), tile(F, D)]
    out, _ = launch(
        lambda hook, *refs: finish_body(h, *refs),
        "finish",
        (steps,),
        (joined, up, down),
        [tile(D, 4 * h), *ups],
        [jax.ShapeDtypeStruct((h, D), F32)] * 4 + [jax.ShapeDtypeStruct(a.shape, F32) for a in (up, down)],
        [pl.BlockSpec((h, rows), lambda i: (0, i))] * 4 + ups,
        [],
        cost(D * D, 6 * (4 * h * D + 2 * D * F)),
    )
    return out


def swap(a, axis, bit):
    return lax.ppermute(a, axis, [(i, i ^ bit) for i in range(lax.axis_size(axis))])


def segments(lengths):
    slots = lengths.shape[1]
    upto = lax.broadcasted_iota(jnp.int32, (1, slots, slots), 2) <= lax.broadcasted_iota(
        jnp.int32, (1, slots, slots), 1
    )
    ends = jnp.sum(jnp.where(upto, lengths[:, None, :], 0), axis=2)
    places = lax.broadcasted_iota(jnp.int32, (lengths.shape[0], L, slots), 1)
    return jnp.sum((ends[:, None, :] <= places).astype(jnp.int32), axis=2)


def merge(*dicts):
    return {k: v for d in dicts for k, v in d.items()}


def fused(x, cotangent, weights, gains, out_bias, valid, ids, mp):
    T, D = x.shape
    joined, wo, up, down, bias = weights
    h = wo.shape[0]
    hidden_units = up.shape[1]
    near, far, deep = ("dp", 1), ("dp", 2), ("dp", 4)

    J, W = Gather("j", D, 3 * h), Gather("w", h, D)
    U, V = Gather("u", D, hidden_units), Gather("v", hidden_units, D)
    both, four = (J, W), (J, W, U, V)
    steps = T // pick(T, 512, 384, 256, 128)
    t = Traffic(
        1,
        [CORE, Y, near, far],
        dict(j=joined, w=wo, u=up, v=down),
        merge(*[g.buffers("s", "q", "o", "p") for g in both], *[g.buffers("s", "q") for g in (U, V)]),
    )
    t.on(0, "start", *[g.start(s) for s in "sy" for g in both], J.wait("s"))
    t.on(0, "middle", *[g.wait("y") for g in both], *[g.start("a") for g in both])
    t.on(0, "middle", *[g.start(s) for s in "ys" for g in (U, V)])
    t.on(2, "start", *[g.wait("a") for g in both], *[g.start("b") for g in both])
    t.on(steps - 1, "end", *[g.wait("b") for g in both], *[g.start("p") for g in both])
    t.on(steps, "start", J.wait("p"))
    t.on(2 * steps - 1, "end", W.wait("s"), W.wait("p"), *[g.wait(s) for s in "ys" for g in (U, V)])
    (qkv, mixed, w, n1), got = attend(x, gains[0], *ids, h, [("j", "js"), ("jo", "jp")], t)
    wo_all = jnp.concatenate([wo, got["ws"], got["wo"], got["wp"]]).reshape(2, 2 * h, D)
    hidden, n2, att_square = project(x, gains[1], valid, mixed, wo_all)

    bias_o = swap(bias, "mp", 2)
    t = Traffic(
        2,
        [CORE, near, far],
        dict(uq=got["uq"], vq=got["vq"], u=up, v=down),
        merge(*[g.buffers("o", "p") for g in (U, V)]),
    )
    fs = hidden_units // pick(hidden_units, 256)
    t.on(0, "start", *[g.start("a") for g in (U, V)])
    t.on(2, "middle", *[g.wait("a") for g in (U, V)], *[g.start("b") for g in (U, V)])
    t.on(4, "start", *[g.wait("b") for g in (U, V)], *[g.start("p") for g in (U, V)])
    t.on(fs - 1, "end", *[g.wait("p") for g in (U, V)])
    own, far_weights = feed_forward(
        n2, cotangent, (bias, swap(bias, "mp", 1)), (up, got["us"]), (down, got["vs"]), t
    )

    a, b = (1, 2, 4), (2, 1, 4)
    U0, D0 = (
        Stream("u0", "u0a", "u0b", D, hidden_units, a, 2, joins="u1"),
        Stream("d0", "d0a", "d0b", hidden_units, D, b, 2, joins="d1"),
    )
    U1, D1 = Stream("u1", "u1a", "u1b", D, hidden_units, a, 2), Stream("d1", "d1a", "d1b", hidden_units, D, b, 2)
    half = D // 2
    att = [
        [
            Near(f"j{n}{m}", f"j{n}a", f"j{n}b", half, 4 * h, (a, b)[m], 1, m * half, None if n else f"j1{m}")
            for m in range(2)
        ]
        for n in range(2)
    ]
    first = (U0, D0)
    second = (U1, D1)
    t = Traffic(
        3,
        [CORE, near, far],
        dict(u0a=own[2], u0b=own[3], d0a=own[4], d0b=own[5]),
        merge(*[s.buffers("c", "s0", "r0", "s1", "r1") for s in first]),
    )
    t.on(0, "start", *[s.start_core for s in first])
    t.on(0, "middle", *[s.wait_core for s in first], *[s.start(0) for s in first])
    t.on(3, "start", *[s.wait(0) for s in first], *[s.start(1) for s in first])
    t.on(fs - 1, "end", *[s.wait(1) for s in first])
    other, left = feed_forward(
        n2,
        cotangent,
        (bias_o, swap(bias_o, "mp", 1)),
        (far_weights["uo"], far_weights["up"]),
        (far_weights["vo"], far_weights["vp"]),
        t,
    )
    feeds = [own, other]
    t = Traffic(
        7,
        [CORE],
        dict(u1b=other[3], d1b=other[5]),
        merge(*[s.buffers("c") for s in second]),
    )
    ls = T // pick(T, 256, 128)
    t.on(0, "start", *[s.start_core for s in second]).on(ls - 1, "end", *[s.wait_core for s in second])
    (out, low, sums), cores = middle(
        hidden, cotangent, gains[1], out_bias, valid, [f[0] for f in feeds], [f[1] for f in feeds], t
    )

    held = dict(u1a=other[2], d1a=other[4]) | cores
    t = Traffic(4, [near, far], held, merge(*[s.buffers("s0", "r0", "s1", "r1") for s in second]))
    t.on(0, "start", *[s.start(0) for s in second])
    t.on(2 * steps - 2, "start", *[s.wait(0) for s in second], *[s.start(1) for s in second])
    t.on(2 * steps - 1, "end", *[s.wait(1) for s in second])
    (dqkv,), arrived = attend_back(low, wo_all, qkv, *ids, t)

    t = Traffic(
        5, [Y], held | {k: v for k, v in arrived.items() if k[2] == "r"}, merge(*[s.buffers("e", "y") for s in second])
    )
    ws = D // pick(D, 256)
    t.on(0, "start", *[f for s in second for f in (s.keep, s.start_cross)])
    t.on(2 * ws - 1, "end", *[s.wait_cross for s in second])
    dw, crossed = weight_grads(n1, low, dqkv, mixed, t)

    units = jnp.zeros((1, lax.axis_size("mp") * hidden_units), F32)
    for change, part in ((0, own[6]), (1, own[7]), (2, other[6]), (3, other[7])):
        units = lax.dynamic_update_slice(units, part, (0, (mp ^ change) * hidden_units))
    count = jnp.where(jnp.arange(D) == 0, jnp.sum(valid), 0.0)[None]
    rows = jnp.concatenate([units.reshape(-1, D), sums[:4], att_square, count])
    n_rows = rows.shape[0] + 1
    tall = (n_rows + 7) // 8 * 8
    small = jnp.pad(rows, ((1, tall - n_rows), (0, 0)))

    held = dict(j0a=dw[0], j0b=dw[1], j1a=dw[2], j1b=dw[3], u1y=crossed["u1y"], d1y=crossed["d1y"], small=small)
    held |= dict(u0a=own[2], d0a=own[4]) | {k: v for k, v in left.items() if k[2] in "cr"}
    flat = [s for pair in att for s in pair]
    bits = [CORE, Y, near, far, deep]
    t = Traffic(
        6,
        bits,
        held,
        merge(*[s.buffers("s2", "r2", "f") for s in first], dict(joined=(D, 4 * h))),
        merge(
            *[s.scratch("m", "c", "s0", "r0") for s in flat],
            *[s.scratch("s1", "r1", "s2", "r2", "f") for s in att[0]],
            *[s.scratch("e", "y") for s in att[1]],
            {f"t{n}": pltpu.VMEM((tall, D), F32) for n in range(2 * len(bits) + 1)},
        ),
    )

    def load_small(t):
        return t.local("small", t.refs["small"], t.refs["t0"])

    def first_small(t):
        load_small(t).wait()
        t.refs["t0"][0:1, :] = t.refs["part"][...]

    def exchange_small(t, n):
        return t.copy(f"t{n}", t.refs[f"t{2 * n}"], t.refs[f"t{2 * n + 1}"], bits[n])

    def store_small(t):
        t.refs["summed"][...] = t.refs[f"t{2 * len(bits)}"][...]

    def start_small(n):
        return lambda t: exchange_small(t, n).start()

    def end_small(n):
        def action(t):
            exchange_small(t, n).wait()
            t.refs[f"t{2 * n + 2}"][...] = t.refs[f"t{2 * n}"][...] + t.refs[f"t{2 * n + 1}"][...]

        return action

    t.on(0, "start", *[s.start_core for s in flat], *[s.start_load for s in flat])
    t.on(0, "start", lambda t: load_small(t).start(), *[s.start(2) for s in first])
    t.on(1, "start", *[s.wait_load for s in flat], *[s.wait_core for s in flat], *[s.start(0) for s in flat])
    end = [first_small, start_small(0)]
    end += [f for s in first for f in (s.wait(2), s.total, s.start_spread(2))]
    end += [end_small(0), start_small(1)]
    end += [f for s in att[1] for f in (s.wait(0), s.keep, s.start_cross)] + [s.wait(0) for s in att[0]]
    end += [end_small(1), start_small(2)]
    end += [f for s in first for f in (s.wait_spread(2), s.start_spread(1))]
    end += [s.wait_cross for s in att[1]] + [s.start(1) for s in att[0]]
    end += [end_small(2), start_small(3)]
    end += [f for s in att[0] for f in (s.wait(1), s.start(2))]
    end += [f for s in first for f in (s.wait_spread(1), s.start_spread(0))]
    end += [f for s in att[0] for f in (s.wait(2), s.total, s.start_spread(2))]
    end += [end_small(3), start_small(4)]
    for j in (2, 1):
        end += [f for s in att[0] for f in (s.wait_spread(j), s.start_spread(j - 1))]
    end += [end_small(4), store_small]
    end += [f for s in att[0] for f in (s.wait_spread(0), s.start_store)]
    end += [s.wait_spread(0) for s in first] + [s.wait_store for s in att[0]]
    t.on(ls - 1, "end", *end)
    (input_gradient, _, summed), done = last(x, gains[0], low, dqkv, w, t, tall)
    return (out, input_gradient, done["joined"], done["u0f"], done["d0f"]), summed


def gathered(x, cotangent, weights, gains, out_bias, valid, ids):
    D = x.shape[1]
    joined, wo, up, down, bias = weights
    every = lambda a, d: lax.all_gather(a, "mp", axis=d, tiled=True)
    two = lambda a, d: tuple(jnp.split(every(a, d), 2, axis=d))
    sides = [jnp.concatenate(p, axis=1) for p in zip(*(two(a, 1) for a in jnp.split(joined, 3, axis=1)))]
    plain = Traffic(0, [], dict(a=sides[0], b=sides[1]), {})
    (qkv, mixed, w, n1), _ = attend(x, gains[0], *ids, sides[0].shape[1] // 3, [("a", "b")], plain)
    wo_all = every(wo, 0)[None]
    hidden, n2, att_square = project(x, gains[1], valid, mixed, wo_all)
    f, _ = feed_forward(n2, cotangent, two(bias, 1), two(up, 1), two(down, 0))
    (out, low, sums), _ = middle(hidden, cotangent, gains[1], out_bias, valid, [f[0]], [f[1]])
    (dqkv,), _ = attend_back(low, wo_all, qkv, *ids, None)
    dw, _ = weight_grads(n1, low, dqkv, mixed, None)
    (input_gradient, first_part), _ = last(x, gains[0], low, dqkv, w)

    def total(pair, d):
        part = lax.psum_scatter(jnp.concatenate(pair, axis=d), "mp", scatter_dimension=d, tiled=True)
        return lax.psum(part, "dp")

    cut = [jnp.split(a, 4, axis=1) for a in dw]
    joined_total = jnp.concatenate([total(pair, 1) for pair in zip(*cut)], axis=1)
    grads = (out, input_gradient, joined_total, total(f[2:4], 1), total(f[4:6], 0))
    units = jnp.concatenate(f[6:], axis=1).reshape(-1, D)
    count = jnp.where(jnp.arange(D) == 0, jnp.sum(valid), 0.0)[None]
    return grads, lax.psum(jnp.concatenate([first_part, units, sums[:4], att_square, count]), ("dp", "mp"))


def per_device(
    tokens,
    lengths,
    cotangent,
    query_weight,
    key_weight,
    value_weight,
    out_weight,
    up_weight,
    hidden_bias,
    down_weight,
    output_bias,
    first_gain,
    second_gain,
):
    T, D = tokens.shape
    rows = T // L
    mp = lax.axis_index("mp")
    segment_ids = segments(lax.dynamic_slice_in_dim(lengths, mp * rows, rows))
    valid = (segment_ids < SLOTS).reshape(-1, 1).astype(F32)
    ids = (segment_ids + L * lax.broadcasted_iota(jnp.int32, (rows, L), 0)).reshape(-1)
    ids = (ids[:, None], ids[None, :])
    joined = jnp.concatenate([query_weight, key_weight, value_weight], axis=1)
    bias = hidden_bias.reshape(1, -1)
    gains = (first_gain.reshape(1, -1), second_gain.reshape(1, -1))
    weights = (joined, out_weight, up_weight, down_weight, bias)
    rest = (gains, output_bias.reshape(1, -1), valid, ids)
    if lax.axis_size("mp") == 4 and lax.axis_size("dp") == 8:
        grads, small = fused(tokens, cotangent, weights, *rest, mp)
    else:
        grads, small = gathered(tokens, cotangent, weights, *rest)
    out, input_gradient, joined_total, up_total, down_total = grads
    n = hidden_bias.shape[0] * lax.axis_size("mp") // D + 1
    squares = jnp.sum(small[n + 2 : n + 6], axis=1)
    mean = lambda i: jnp.sqrt(squares[i] / (squares[3] * D))
    q, k, v, o, up_total, down_total = finish(joined_total, up_total, down_total)
    return (
        out,
        input_gradient,
        q.T,
        k.T,
        v.T,
        o,
        up_total,
        lax.dynamic_slice_in_dim(small[1:n].reshape(-1), mp * bias.shape[1], bias.shape[1]),
        down_total,
        small[n + 1],
        small[0],
        small[n],
        jnp.stack([mean(2), mean(0), mean(1)]),
    )


def solution(mesh):
    return jax.shard_map(
        per_device,
        mesh=mesh,
        in_specs=(
            P(("dp", "mp"), None),
            P("dp", None),
            P(("dp", "mp"), None),
            P(None, "mp"),
            P(None, "mp"),
            P(None, "mp"),
            P("mp", None),
            P(None, "mp"),
            P("mp"),
            P("mp", None),
            P(),
            P(),
            P(),
        ),
        out_specs=(
            P(("dp", "mp"), None),
            P(("dp", "mp"), None),
            P(None, "mp"),
            P(None, "mp"),
            P(None, "mp"),
            P("mp", None),
            P(None, "mp"),
            P("mp"),
            P("mp", None),
            P(),
            P(),
            P(),
            P(),
        ),
        check_vma=False,
    )
```
